32 devices in a mesh: wide: 16 (over z, x, core), narrow: 2 (over y).
Axes of the slice: x: 2, y: 2, z: 4, core: 2. Of those that a mesh axis runs over, the one named last changes fastest.
Arguments:
- tokens: bfloat16 [128, 196, 768], P('wide'), may hold values from -6 to 6
- merge_map: int32 [128, 196], P('wide'), may hold values from 0 to 195, as said below
- counts: int32 [128], P('wide'), may hold values from 60 to 196, as said below
- ln_gain: float32 [2, 768], replicated, may hold values from 0.1 to 1.9
- w_qkv: bfloat16 [2, 3, 768, 768], P(None, None, None, 'narrow'), may hold values from -0.21875 to 0.21875
- qk_gain: float32 [2, 2, 64], replicated, may hold values from 0.1 to 1.9
- w_out: bfloat16 [2, 768, 768], P(None, 'narrow'), may hold values from -0.625 to 0.625
- w_up: bfloat16 [2, 768, 3072], P(None, None, 'narrow'), may hold values from -0.21875 to 0.21875
- b_up: bfloat16 [2, 3072], P(None, 'narrow'), may hold values from -3 to 3
- w_down: bfloat16 [2, 3072, 768], P(None, 'narrow'), may hold values from -0.109375 to 0.109375
- b_down: float32 [2, 768], replicated, may hold values from -2 to 2
- cotangent: bfloat16 [128, 196, 768], P('wide'), may hold values from -6 to 6
Outputs:
- first_out: float32 [128, 196, 768], P('wide')
- second_out: float32 [128, 196, 768], P('wide')
- grad_tokens: float32 [128, 196, 768], P('wide')
- grad_ln_gain: float32 [2, 768], replicated
- grad_qkv: float32 [2, 3, 768, 768], P(None, None, None, 'narrow')
- grad_qk_gain: float32 [2, 2, 64], replicated
- grad_out: float32 [2, 768, 768], P(None, 'narrow')
- grad_up: float32 [2, 768, 3072], P(None, None, 'narrow')
- grad_b_up: float32 [2, 3072], P(None, 'narrow')
- grad_down: float32 [2, 3072, 768], P(None, 'narrow')
- grad_b_down: float32 [2, 768], replicated
The draws below stay inside these ranges and needn't reach their ends.
Inputs may be any that keep to these rules, and one draw needn't show every extreme that they name: `counts`: each image's live tokens fill its first slots; at least one image has 196 live tokens and at least one has 60. merge_map[i, p] names the live token of image i (below counts[i]) into which patch p was merged; every live token of an image is named by at least one patch.
All inputs are finite; a program needn't handle non-finite values.
Results may differ from the reference program's by a relative error of at most 0.022.
Values may be sent and summed in bfloat16 or wider, within the bound.
No kernel may reach another device: no remote copies, remote signals or barrier semaphores. Data moves between devices by JAX's collectives and lax.ppermute only.
A program may use at most 320 MiB of HBM per device.

```python
import jax
import jax.numpy as jnp
from jax import lax

D = 768
HEADS = 12
HD = 64
FF = 3072
LAYERS = 2
SLOTS = 196
LIVE_MIN = 60
IMG_DEV = 8
IMAGES = 128
N_WIDE = 16
N_NARROW = 2


def live_counts(key):
    drawn = jax.random.randint(jax.random.fold_in(key, 11), (IMAGES,), LIVE_MIN, SLOTS + 1)
    chosen = jax.random.permutation(jax.random.fold_in(key, 12), IMAGES)
    drawn = drawn.at[chosen[0]].set(SLOTS)
    return drawn.at[chosen[1]].set(LIVE_MIN).astype(jnp.int32)


def draw_counts(key, part):
    return live_counts(key)


def draw_merge_map(key, part):
    counts = live_counts(key)
    key = jax.random.fold_in(key, 5)
    slot_ids = jnp.arange(SLOTS, dtype=jnp.int32)
    spread_ids = jax.random.randint(jax.random.fold_in(key, 1), (IMAGES, SLOTS), 0, 1048576)
    target = jnp.where(slot_ids[None, :] < counts[:, None], slot_ids[None, :], spread_ids % counts[:, None])
    image_keys = jax.random.split(jax.random.fold_in(key, 2), IMAGES)

    def shuffle(piece_key):
        return jax.random.permutation(piece_key, SLOTS)
    orders = jax.vmap(shuffle)(image_keys)
    return jnp.take_along_axis(target, orders, axis=1).astype(jnp.int32)


def levels(stream_key, dims, shards, least, high):
    level, own = 1.0, jax.random.fold_in(stream_key, 6)
    for axis_at, shards_of in shards:
        draws = jnp.exp(jax.random.uniform(jax.random.fold_in(own, axis_at), (shards_of,), jnp.float32, least / len(shards), high / len(shards)))
        level = level * jnp.repeat(draws, dims[axis_at] // shards_of).reshape([-1 if axis == axis_at else 1 for axis in range(len(dims))])
    return level


def gaussian(own_key, dims, deviation, reach, cuts=(), kind=jnp.bfloat16):
    array = jax.random.normal(own_key, dims, jnp.float32) * deviation
    if len(cuts) > 0:
        array = levels(own_key, dims, cuts, -0.22, 0.18) * array
    return jnp.clip(array, min=-reach, max=reach).astype(kind)


def setup_inputs(seed: int = 0) -> dict:
    key_of = jax.random.split(jax.random.key(seed), 13)
    tokens = gaussian(key_of[0], (IMAGES, SLOTS, D), 1.0, 6.0, ((0, 16),))
    merge_map = draw_merge_map(jax.random.fold_in(key_of[12], 71), 0)
    counts = draw_counts(jax.random.fold_in(key_of[12], 71), 0)
    ln_gain = jnp.clip(1.0 + 0.18 * jax.random.normal(key_of[3], (LAYERS, D), jnp.float32), 0.1, 1.9)
    w_qkv = gaussian(key_of[4], (LAYERS, 3, D, HEADS * HD), D ** -0.5, 0.21875, ((3, 2),))
    qk_gain = jnp.clip(1.0 + 0.18 * jax.random.normal(key_of[5], (LAYERS, 2, HD), jnp.float32), 0.1, 1.9)
    w_out = gaussian(key_of[6], (LAYERS, HEADS * HD, D), (HEADS * HD // 8) ** -0.5, 0.625, ((1, 2),))
    w_up = gaussian(key_of[7], (LAYERS, D, FF), D ** -0.5, 0.21875, ((2, 2),))
    b_up = gaussian(key_of[8], (LAYERS, FF), 0.5, 3.0, ((1, 2),))
    w_down = gaussian(key_of[9], (LAYERS, FF, D), FF ** -0.5, 0.109375, ((1, 2),))
    b_down = gaussian(key_of[10], (LAYERS, D), 0.3, 2.0, (), jnp.float32)
    cotangent = gaussian(key_of[11], (IMAGES, SLOTS, D), 1.0, 6.0, ((0, 16),))
    return {"tokens": tokens, "merge_map": merge_map, "counts": counts, "ln_gain": ln_gain, "w_qkv": w_qkv, "qk_gain": qk_gain, "w_out": w_out, "w_up": w_up, "b_up": b_up, "w_down": w_down, "b_down": b_down, "cotangent": cotangent}


@jax.custom_vjp
def low(v):
    return lax.optimization_barrier(v.astype(jnp.bfloat16)).astype(jnp.float32)

@jax.custom_vjp
def low_back(v):
    return v

def low_keep(v):
    return (low(v), None)

def low_pass(kept, grad):
    return (grad,)

def back_keep(v):
    return (v, None)

def back_low(kept, grad):
    return (low(grad),)
low.defvjp(low_keep, low_pass)
low_back.defvjp(back_keep, back_low)
exact_precision = lax.Precision.HIGHEST

def group_order(weight, dim_index):
    dims_full = weight.shape
    length = dims_full[dim_index]
    split = weight.reshape(dims_full[:dim_index] + (2, N_NARROW // 2, length // N_NARROW) + dims_full[dim_index + 1:])
    return jnp.swapaxes(split, dim_index, dim_index + 1).reshape(dims_full)

def norm_rows(inputs, gain_row):
    centre = lax.optimization_barrier(jnp.mean(inputs, axis=-1, keepdims=True))
    centered = inputs - centre
    inverse = lax.rsqrt(lax.optimization_barrier(jnp.mean(centered * centered, axis=-1, keepdims=True)) + 1e-06)
    return centered * inverse * gain_row

def attention_images(normed_low, bias_rows, qkv_heads, qk_gains):
    projected = jnp.einsum('bsd,kdhe->kbhse', normed_low, qkv_heads, precision=exact_precision)
    queries = low(norm_rows(low_back(projected[0]), qk_gains[0]))
    keys_normed = low(norm_rows(low_back(projected[1]), qk_gains[1]))
    values_low = low(low_back(projected[2]))
    scores = low_back(jnp.einsum('bhse,bhte->bhst', queries, keys_normed, precision=exact_precision))
    logits = scores * HD ** (-0.5) + bias_rows[:, None, None, :]
    softened = jax.nn.softmax(logits, axis=-1)
    mixed = jnp.einsum('bhst,bhte->bhse', low(softened), values_low, precision=exact_precision)
    return low(low_back(mixed))

def attention_all(normed_low, bias_rows, qkv_heads, qk_gains):
    blocks = normed_low.reshape(N_WIDE, IMG_DEV, SLOTS, D)
    bias_blocks = bias_rows.reshape(N_WIDE, IMG_DEV, SLOTS)

    def one_block(carried, pieces):
        return (carried, attention_images(pieces[0], pieces[1], qkv_heads, qk_gains))
    ignored, mixed_low = lax.scan(jax.checkpoint(one_block), None, (blocks, bias_blocks))
    return mixed_low.reshape(IMAGES, HEADS, SLOTS, HD)

def one_layer(current, row_weight, bias_rows, weights):
    gain_row, qkv_weight, qk_gains, out_weight, up_weight, up_bias, down_weight, down_bias = weights
    normed_low = low(norm_rows(current, gain_row))
    qkv_heads = group_order(qkv_weight, 2).reshape(3, D, HEADS, HD)
    mixed_low = attention_all(normed_low, bias_rows, qkv_heads, qk_gains)
    out_heads = group_order(out_weight, 0).reshape(HEADS, HD, D)
    attended = low_back(jnp.einsum('bhse,hed->bsd', mixed_low, out_heads, precision=exact_precision))
    pre_act = low_back(jnp.einsum('bsd,df->bsf', normed_low, group_order(up_weight, 1), precision=exact_precision) + group_order(up_bias, 0))
    hidden = low(jax.nn.gelu(pre_act))
    fed_out = low_back(jnp.einsum('bsf,fd->bsd', hidden, group_order(down_weight, 0), precision=exact_precision))
    return row_weight * (current + attended + fed_out + down_bias)

def reference(tokens, merge_map, counts, ln_gain, w_qkv, qk_gain, w_out, w_up, b_up, w_down, b_down, cotangent):
    slot_ids = jnp.arange(SLOTS, dtype=jnp.int32)
    live_rows = slot_ids[None, :] < counts[:, None]
    row_weight = jnp.where(live_rows, 1.0, 0.0).astype(jnp.float32)[:, :, None]
    merged_sizes = lax.optimization_barrier(jnp.sum(jnp.where(merge_map[:, :, None] == slot_ids[None, None, :], 1.0, 0.0), axis=1)).astype(jnp.float32)
    bias_rows = jnp.where(live_rows, jnp.log(jnp.where(live_rows, merged_sizes, 1.0)), -1e+30).astype(jnp.float32)
    params = tuple((element.astype(jnp.float32) for element in (ln_gain, w_qkv, qk_gain, w_out, w_up, b_up, w_down, b_down)))

    def forward(inputs, weights):
        current = inputs
        outputs = []
        for layer_at in range(LAYERS):
            current = one_layer(current, row_weight, bias_rows, tuple((element[layer_at] for element in weights)))
            outputs.append(current)
        return (outputs[0], outputs[-1])
    (first_out, second), pullback = jax.vjp(forward, tokens.astype(jnp.float32), params)
    grad_tokens, gradients = pullback((jnp.zeros_like(first_out), cotangent.astype(jnp.float32)))
    return (first_out, second, grad_tokens, gradients[0], gradients[1], gradients[2], gradients[3], gradients[4], gradients[5], gradients[6], gradients[7])
```

```python
import functools

import jax
import jax.numpy as jnp
from jax import lax
from jax.experimental import pallas as pl
from jax.experimental.pallas import tpu as pltpu
from jax.sharding import PartitionSpec as P


def shifted_2(value, axis, by):
    length = lax.axis_size(axis)
    pairs = [(i, i + by) for i in range(length) if 0 <= i + by < length]
    return lax.ppermute(value, axis, pairs)


def norm_rows(inputs, gain_row):
    centre = jnp.mean(inputs, axis=-1, keepdims=True)
    centered = inputs - centre
    inverse = lax.rsqrt(jnp.mean(centered * centered, axis=-1, keepdims=True) + 1e-06)
    normal = centered * inverse
    return (normal, inverse, normal * gain_row)


def norm_back(upstream, normal, inverse, gain_row):
    scaled = upstream * gain_row
    return inverse * (
        scaled
        - jnp.mean(scaled, axis=-1, keepdims=True)
        - normal * jnp.mean(scaled * normal, axis=-1, keepdims=True)
    )


def attend(normed_low, key_bias, qkv_full, out_full, qk_gains):
    head_dim = qk_gains.shape[-1]
    head_count = qkv_full.shape[-1] // head_dim
    qkv_heads = qkv_full.reshape(3, qkv_full.shape[1], head_count, head_dim)
    projected = jnp.einsum(
        "bsd,kdhe->kbhse", normed_low, qkv_heads, preferred_element_type=jnp.float32
    )
    q_normal, q_inverse, queries = norm_rows(projected[0], qk_gains[0])
    k_normal, k_inverse, keys_normed = norm_rows(projected[1], qk_gains[1])
    queries_low = queries.astype(jnp.bfloat16)
    keys_low = keys_normed.astype(jnp.bfloat16)
    values_low = projected[2].astype(jnp.bfloat16)
    score_scale = head_dim ** (-0.5)
    scores = jnp.einsum(
        "bhse,bhte->bhst", queries_low, keys_low, preferred_element_type=jnp.float32
    )
    logits = scores * score_scale + key_bias[:, None, None, :]
    shifted = jnp.exp(logits - jnp.max(logits, axis=-1, keepdims=True))
    softened = shifted / jnp.sum(shifted, axis=-1, keepdims=True)
    soft_low = softened.astype(jnp.bfloat16)
    mixed_low = jnp.einsum(
        "bhst,bhte->bhse", soft_low, values_low, preferred_element_type=jnp.float32
    ).astype(jnp.bfloat16)
    out_heads = out_full.reshape(head_count, head_dim, out_full.shape[-1])
    branch = jnp.einsum("bhse,hed->bsd", mixed_low, out_heads, preferred_element_type=jnp.float32)
    kept_parts = (
        q_normal,
        q_inverse,
        k_normal,
        k_inverse,
        queries_low,
        keys_low,
        values_low,
        softened,
        soft_low,
        mixed_low,
        qkv_heads,
        out_heads,
        score_scale,
    )
    return (branch, kept_parts)


def attend_back(normed_low, key_bias, qkv_full, out_full, qk_gains, grad_low):
    branch, kept_parts = attend(normed_low, key_bias, qkv_full, out_full, qk_gains)
    (
        q_normal,
        q_inverse,
        k_normal,
        k_inverse,
        queries_low,
        keys_low,
        values_low,
        softened,
        soft_low,
        mixed_low,
        qkv_heads,
        out_heads,
        score_scale,
    ) = kept_parts
    d_mixed = jnp.einsum(
        "bsd,hed->bhse", grad_low, out_heads, preferred_element_type=jnp.float32
    ).astype(jnp.bfloat16)
    g_out = jnp.einsum(
        "bhse,bsd->hed", mixed_low, grad_low, preferred_element_type=jnp.float32
    ).reshape(out_full.shape)
    d_soft = jnp.einsum("bhse,bhte->bhst", d_mixed, values_low, preferred_element_type=jnp.float32)
    row_dot = jnp.sum(softened * d_soft, axis=-1, keepdims=True)
    d_scores = (softened * (d_soft - row_dot) * score_scale).astype(jnp.bfloat16)
    d_queries = jnp.einsum(
        "bhst,bhte->bhse", d_scores, keys_low, preferred_element_type=jnp.float32
    )
    d_keys = jnp.einsum(
        "bhst,bhse->bhte", d_scores, queries_low, preferred_element_type=jnp.float32
    )
    d_values = jnp.einsum("bhst,bhse->bhte", soft_low, d_mixed, preferred_element_type=jnp.float32)
    g_gains = jnp.stack(
        [jnp.sum(d_queries * q_normal, axis=(0, 1, 2)), jnp.sum(d_keys * k_normal, axis=(0, 1, 2))]
    )
    d_projected = jnp.stack(
        [
            norm_back(d_queries, q_normal, q_inverse, qk_gains[0]),
            norm_back(d_keys, k_normal, k_inverse, qk_gains[1]),
            d_values,
        ]
    ).astype(jnp.bfloat16)
    g_qkv = jnp.einsum(
        "bsd,kbhse->kdhe", normed_low, d_projected, preferred_element_type=jnp.float32
    ).reshape(qkv_full.shape)
    d_normed = jnp.einsum(
        "kbhse,kdhe->bsd", d_projected, qkv_heads, preferred_element_type=jnp.float32
    )
    return (d_normed, g_qkv, g_out, g_gains)


def expand(normed_low, up_full, bias_full, down_full):
    pre_act = jnp.einsum(
        "bsd,df->bsf", normed_low, up_full, preferred_element_type=jnp.float32
    ) + bias_full.astype(jnp.float32)
    hidden, gelu_back = jax.vjp(jax.nn.gelu, pre_act)
    hidden_low = hidden.astype(jnp.bfloat16)
    branch = jnp.einsum("bsf,fd->bsd", hidden_low, down_full, preferred_element_type=jnp.float32)
    return (branch, hidden_low, gelu_back)


def expand_back(normed_low, up_full, bias_full, down_full, grad_low):
    branch, hidden_low, gelu_back = expand(normed_low, up_full, bias_full, down_full)
    d_hidden = jnp.einsum("bsd,fd->bsf", grad_low, down_full, preferred_element_type=jnp.float32)
    d_pre = gelu_back(d_hidden)[0].astype(jnp.bfloat16)
    g_bias = jnp.sum(d_pre, axis=(0, 1), dtype=jnp.float32)
    g_up = jnp.einsum("bsd,bsf->df", normed_low, d_pre, preferred_element_type=jnp.float32)
    g_down = jnp.einsum("bsf,bsd->fd", hidden_low, grad_low, preferred_element_type=jnp.float32)
    d_normed = jnp.einsum("bsf,df->bsd", d_pre, up_full, preferred_element_type=jnp.float32)
    return (d_normed, g_up, g_bias, g_down)


def body(
    tokens, merge_map, counts, ln_gain, w_qkv, qk_gain, w_out, w_up, b_up, w_down, b_down, cotangent
):
    pair_gap = lax.axis_size("narrow") // 2
    on_attention = lax.axis_index("narrow") < pair_gap
    layers = ln_gain.shape[0]
    col_half = w_qkv.shape[-1]
    unit_half = w_up.shape[-1]
    model_dim = tokens.shape[-1]
    slot_ids = jnp.arange(tokens.shape[1], dtype=jnp.int32)
    live_rows = slot_ids[None, :] < counts[:, None]
    row_weight = jnp.where(live_rows, 1.0, 0.0).astype(jnp.float32)[:, :, None]
    merged_sizes = jnp.sum(
        jnp.where(merge_map[:, :, None] == slot_ids[None, None, :], 1.0, 0.0), axis=1
    ).astype(jnp.float32)
    key_bias = jnp.where(live_rows, jnp.log(jnp.where(live_rows, merged_sizes, 1.0)), -1e30)
    attn_far = shifted_2((w_qkv, w_out), "narrow", -pair_gap)
    mlp_far = shifted_2((w_up, b_up, w_down), "narrow", pair_gap)

    def attention_weights(layer_at):
        qkv_full = jnp.concatenate([w_qkv[layer_at], attn_far[0][layer_at]], axis=-1)
        out_full = jnp.concatenate([w_out[layer_at], attn_far[1][layer_at]], axis=0)
        return (qkv_full, out_full)

    def feed_weights(layer_at):
        up_full = jnp.concatenate([mlp_far[0][layer_at], w_up[layer_at]], axis=-1)
        bias_full = jnp.concatenate([mlp_far[1][layer_at], b_up[layer_at]], axis=-1)
        down_full = jnp.concatenate([mlp_far[2][layer_at], w_down[layer_at]], axis=0)
        return (up_full, bias_full, down_full)

    current = tokens.astype(jnp.float32)
    layer_inputs = []
    outputs = []
    for layer_at in range(layers):
        normal, inverse, normed = norm_rows(current, ln_gain[layer_at])
        normed_low = normed.astype(jnp.bfloat16)

        def attention_forward():
            qkv_full, out_full = attention_weights(layer_at)
            return attend(normed_low, key_bias, qkv_full, out_full, qk_gain[layer_at])[0]

        def feed_forward():
            up_full, bias_full, down_full = feed_weights(layer_at)
            return expand(normed_low, up_full, bias_full, down_full)[0]

        partial_value = lax.cond(on_attention, attention_forward, feed_forward)
        layer_inputs.append(current)
        branch_total = lax.psum(partial_value, "narrow")
        current = row_weight * (current + branch_total + b_down[layer_at])
        outputs.append(current)
    grad_rows = cotangent.astype(jnp.float32)
    collected = []
    for layer_at in reversed(range(layers)):
        normal, inverse, normed = norm_rows(layer_inputs[layer_at], ln_gain[layer_at])
        normed_low = normed.astype(jnp.bfloat16)
        masked_grad = row_weight * grad_rows
        grad_low = masked_grad.astype(jnp.bfloat16)

        def attention_side():
            qkv_full, out_full = attention_weights(layer_at)
            d_normed, g_qkv, g_out, g_gains = attend_back(
                normed_low, key_bias, qkv_full, out_full, qk_gain[layer_at], grad_low
            )
            return (
                d_normed,
                g_gains,
                g_qkv,
                g_out,
                jnp.zeros((model_dim, 2 * unit_half), jnp.float32),
                jnp.zeros((2 * unit_half,), jnp.float32),
                jnp.zeros((2 * unit_half, model_dim), jnp.float32),
            )

        def feed_side():
            up_full, bias_full, down_full = feed_weights(layer_at)
            d_normed, g_up, g_bias, g_down = expand_back(
                normed_low, up_full, bias_full, down_full, grad_low
            )
            return (
                d_normed,
                jnp.zeros(qk_gain[layer_at].shape, jnp.float32),
                jnp.zeros((3, model_dim, 2 * col_half), jnp.float32),
                jnp.zeros((2 * col_half, model_dim), jnp.float32),
                g_up,
                g_bias,
                g_down,
            )

        returned = lax.cond(on_attention, attention_side, feed_side)
        d_normed, g_gains = (
            lax.psum(returned[0].astype(jnp.bfloat16), "narrow").astype(jnp.float32),
            lax.psum(returned[1].astype(jnp.bfloat16), "narrow").astype(jnp.float32),
        )
        g_ln = jnp.sum(d_normed * normal, axis=(0, 1))
        grad_rows = masked_grad + norm_back(d_normed, normal, inverse, ln_gain[layer_at])
        qkv_far, out_far = (
            shifted_2(returned[2][..., col_half:].astype(jnp.bfloat16), "narrow", pair_gap).astype(
                jnp.float32
            ),
            shifted_2(returned[3][col_half:].astype(jnp.bfloat16), "narrow", pair_gap).astype(
                jnp.float32
            ),
        )
        up_far, bias_far, down_far = (
            shifted_2(returned[4][:, :unit_half].astype(jnp.bfloat16), "narrow", -pair_gap).astype(
                jnp.float32
            ),
            shifted_2(returned[5][:unit_half].astype(jnp.bfloat16), "narrow", -pair_gap).astype(
                jnp.float32
            ),
            shifted_2(returned[6][:unit_half].astype(jnp.bfloat16), "narrow", -pair_gap).astype(
                jnp.float32
            ),
        )
        own_qkv = jnp.where(on_attention, returned[2][..., :col_half], qkv_far)
        own_out = jnp.where(on_attention, returned[3][:col_half], out_far)
        own_up = jnp.where(on_attention, up_far, returned[4][:, unit_half:])
        own_bias = jnp.where(on_attention, bias_far, returned[5][unit_half:])
        own_down = jnp.where(on_attention, down_far, returned[6][unit_half:])
        g_bdown = jnp.sum(masked_grad, axis=(0, 1))
        shards = (own_qkv, own_out, own_up, own_bias, own_down, g_ln, g_gains, g_bdown)
        collected.append(shards)
    collected = collected[::-1]
    stacked = tuple(
        (jnp.stack([element[position] for element in collected]) for position in range(8))
    )
    stacked = (
        lax.psum(stacked[0].astype(jnp.bfloat16), "wide").astype(jnp.float32),
        lax.psum(stacked[1].astype(jnp.bfloat16), "wide").astype(jnp.float32),
        lax.psum(stacked[2].astype(jnp.bfloat16), "wide").astype(jnp.float32),
        lax.psum(stacked[3].astype(jnp.bfloat16), "wide").astype(jnp.float32),
        lax.psum(stacked[4].astype(jnp.bfloat16), "wide").astype(jnp.float32),
        lax.psum(stacked[5].astype(jnp.bfloat16), "wide").astype(jnp.float32),
        lax.psum(stacked[6].astype(jnp.bfloat16), "wide").astype(jnp.float32),
        lax.psum(stacked[7].astype(jnp.bfloat16), "wide").astype(jnp.float32),
    )
    return (
        outputs[0],
        outputs[-1],
        grad_rows,
        stacked[5],
        stacked[0],
        stacked[6],
        stacked[1],
        stacked[2],
        stacked[3],
        stacked[4],
        stacked[7],
    )


EPS = 1e-06
F32 = jnp.float32
BF16 = jnp.bfloat16
GELU_IN = 0.7978845608028654
GELU_CUBE = 0.044715


def padded_to(length, step):
    return -(-length // step) * step


def dot(a, b):
    return jnp.dot(a, b, preferred_element_type=F32)


def dot_nt(a, b):
    return lax.dot_general(a, b, (((1,), (1,)), ((), ())), preferred_element_type=F32)


def normal_rows(x):
    centered = x - jnp.mean(x, axis=-1, keepdims=True)
    inverse = lax.rsqrt(jnp.mean(centered * centered, axis=-1, keepdims=True) + EPS)
    return centered * inverse, inverse


def back_rows(upstream, normal, inverse, gain):
    scaled = upstream * gain
    return inverse * (
        scaled
        - jnp.mean(scaled, axis=-1, keepdims=True)
        - normal * jnp.mean(scaled * normal, axis=-1, keepdims=True)
    )


def live_of(count, rows):
    return lax.broadcasted_iota(jnp.int32, (rows, 1), 0) < count


def padded_rows(source, wide_rows, live):
    slots = source.shape[0]
    edge = slots // 8 * 8
    wide_rows[edge:, :] = jnp.zeros((wide_rows.shape[0] - edge, wide_rows.shape[1]), F32)
    wide_rows[:slots, :] = source[...].astype(F32)
    return jnp.where(live, wide_rows[...], 0.0)


def head_norm(x):
    centered = x - jnp.mean(x, axis=0, keepdims=True)
    inverse = lax.rsqrt(jnp.mean(centered * centered, axis=0, keepdims=True) + EPS)
    return centered * inverse, inverse


def head_back(upstream, normal, inverse, gain):
    scaled = upstream * gain
    return inverse * (
        scaled
        - jnp.mean(scaled, axis=0, keepdims=True)
        - normal * jnp.mean(scaled * normal, axis=0, keepdims=True)
    )


def key_sizes(patch_ref, rows):
    slot = lax.broadcasted_iota(jnp.int32, (rows, patch_ref.shape[-1]), 0)
    named = jnp.where(patch_ref[0] == slot, 1.0, 0.0)
    return jnp.sum(named, axis=-1, keepdims=True)


def scores_of(proj, head, inner, gains, soft):
    head_dim = gains.shape[0] // 2
    at = head * head_dim
    q_normal, q_inverse = head_norm(proj[at : at + head_dim, :])
    k_normal, k_inverse = head_norm(proj[inner + at : inner + at + head_dim, :])
    queries = (q_normal * gains[:head_dim, :]).astype(BF16).astype(F32) * head_dim ** (-0.5)
    queries = queries.astype(BF16)
    keys = (k_normal * gains[head_dim:, :]).astype(BF16)
    values = proj[2 * inner + at : 2 * inner + at + head_dim, :].astype(BF16)
    return q_normal, q_inverse, k_normal, k_inverse, queries, keys, values


def soften(queries, keys, sizes, soft, rows):
    scores = dot(keys.T[:rows], queries)
    raised = jnp.exp(scores) * sizes
    soft[:rows, :] = raised.astype(BF16)
    return raised, 1.0 / jnp.sum(raised, axis=0, keepdims=True)


def forward_kernel(first, rows, counts, tok, patch, gain, w_qkv, gains, w_out, w_up, b_up, w_down,
                   out, wide_rows, normed, proj, soft, mixed):
    step = pl.program_id(0)
    inner = w_out.shape[0]
    head_dim = gains.shape[0] // 2

    @pl.when(step == 0)
    def _():
        normed[...] = jnp.zeros(normed.shape, BF16)
        soft[...] = jnp.zeros(soft.shape, BF16)

    live = live_of(counts[first + step], rows)
    x = padded_rows(tok.at[0], wide_rows, live)
    normed[:rows, :] = (normal_rows(x)[0] * gain[...]).astype(BF16)
    for part in range(3):
        proj[part * inner : (part + 1) * inner, :] = dot_nt(w_qkv[part], normed[...])
    sizes = key_sizes(patch, rows)
    for head in range(inner // head_dim):
        at = head * head_dim
        _, _, _, _, queries, keys, values = scores_of(proj, head, inner, gains, soft)
        raised, over = soften(queries, keys, sizes, soft.at[head], rows)
        mixed[at : at + head_dim, :] = (dot(values, soft[head]) * over).astype(BF16)
    total = dot(mixed[...].T[:rows], w_out[...])
    units = w_up.shape[1]
    tile = units // 3
    for at in range(0, units, tile):
        pre = dot(normed[:rows, :], w_up[:, at : at + tile]) + b_up[:, at : at + tile]
        hidden = 0.5 * pre * (1.0 + jnp.tanh(GELU_IN * (pre + GELU_CUBE * pre * pre * pre)))
        total = total + dot(hidden.astype(BF16), w_down[at : at + tile, :])
    out[...] = total.astype(BF16)


def feed_kernel(top, first, rows, per_step, counts, *refs):
    refs = list(refs)
    tok, own, far, cot = refs[:4]
    refs = refs[4:]
    if not top:
        own_grad, far_grad, gain_top = refs[:3]
        refs = refs[3:]
    gain, b_prev, w_up, b_up, w_down = refs[:5]
    refs = refs[5:]
    if top:
        x_out, fed = refs[:2]
        refs = refs[2:]
    else:
        g_out = refs[0]
        refs = refs[1:]
    normed, low, d_feed, hidden_out, d_pre_out, sum_up, sum_down, wide_rows = refs
    step = pl.program_id(0)
    slots = tok.shape[1]

    @pl.when(step == 0)
    def _():
        sum_up[...] = jnp.zeros(sum_up.shape, F32)
        sum_down[...] = jnp.zeros(sum_down.shape, F32)

    for j in range(per_step):
        block = slice(j * rows, (j + 1) * rows)
        live = live_of(counts[first + step * per_step + j], rows)
        x0 = padded_rows(tok.at[j], wide_rows, live)
        branch = own[block, :].astype(F32) + far[block, :].astype(F32)
        x1 = jnp.where(live, x0 + branch + b_prev[...], 0.0)
        grad = padded_rows(cot.at[j], wide_rows, live)
        if top:
            x = x1
            x_out[j] = x1[:slots]
        else:
            x = x0
            normal, inverse = normal_rows(x1)
            d_normed = own_grad[block, :].astype(F32) + far_grad[block, :].astype(F32)
            grad = grad + back_rows(d_normed, normal, inverse, gain_top[...])
            g_out[block, :] = grad
        normed[block, :] = (normal_rows(x)[0] * gain[...]).astype(BF16)
        low[block, :] = grad.astype(BF16)
        sum_down[...] += jnp.sum(grad, axis=0, keepdims=True)
    units = w_up.shape[1]
    tile = units // 3
    d_total = jnp.zeros((per_step * rows, tok.shape[2]), F32)
    total = jnp.zeros((per_step * rows, tok.shape[2]), F32)
    for at in range(0, units, tile):
        part = slice(at, at + tile)
        pre = dot(normed[...], w_up[:, part]) + b_up[:, part]
        square = pre * pre
        bent = jnp.tanh(pre * (GELU_IN + (GELU_IN * GELU_CUBE) * square))
        half = 0.5 + 0.5 * bent
        hidden = (pre * half).astype(BF16)
        slope = half + (0.5 * pre) * (1.0 - bent * bent) * (GELU_IN + (3 * GELU_IN * GELU_CUBE) * square)
        d_pre = (dot_nt(low[...], w_down[part, :]) * slope).astype(BF16)
        hidden_out[:, part] = hidden
        d_pre_out[:, part] = d_pre
        sum_up[:, part] += jnp.sum(d_pre.astype(F32), axis=0, keepdims=True)
        d_total = d_total + dot_nt(d_pre, w_up[:, part])
        if top:
            total = total + dot(hidden, w_down[part, :])
    d_feed[...] = d_total.astype(BF16)
    if top:
        fed[...] = total.astype(BF16)


def heads_kernel(top, rows, patch, normed_in, low_in, d_feed, *refs):
    refs = list(refs)
    if top:
        fed = refs[0]
        refs = refs[1:]
    w_qkv, gains, w_out = refs[:3]
    refs = refs[3:]
    if top:
        out = refs[0]
        refs = refs[1:]
    d_normed, mixed_out, d_q, d_k, d_v, sum_gain, sum_row = refs[:7]
    normed, low, proj, d_mixed, soft, d_soft, mixed, d_proj = refs[7:]
    step = pl.program_id(0)
    inner = w_out.shape[0]
    head_dim = gains.shape[0] // 2

    @pl.when(step == 0)
    def _():
        normed[...] = jnp.zeros(normed.shape, BF16)
        low[...] = jnp.zeros(low.shape, BF16)
        soft[...] = jnp.zeros(soft.shape, BF16)
        d_soft[...] = jnp.zeros(d_soft.shape, BF16)
        sum_gain[...] = jnp.zeros(sum_gain.shape, F32)
        sum_row[...] = jnp.zeros(sum_row.shape, F32)

    normed[:rows, :] = normed_in[...]
    low[:rows, :] = low_in[...]
    for part in range(3):
        proj[part * inner : (part + 1) * inner, :] = dot_nt(w_qkv[part], normed[...])
    d_mixed[...] = dot_nt(w_out[...], low[...]).astype(BF16)
    sizes = key_sizes(patch, rows)
    q_gain, k_gain = gains[:head_dim, :], gains[head_dim:, :]
    for head in range(inner // head_dim):
        at = head * head_dim
        here = slice(at, at + head_dim)
        q_normal, q_inverse, k_normal, k_inverse, queries, keys, values = scores_of(proj, head, inner, gains, soft)
        raised, over = soften(queries, keys, sizes, soft.at[head], rows)
        mixed_here = dot(values, soft[head]) * over
        mixed[here, :] = mixed_here.astype(BF16)
        d_mixed_here = d_mixed[here, :].astype(F32)
        row_dot = jnp.sum(d_mixed_here * mixed_here, axis=0, keepdims=True) * over
        scaled = (d_mixed_here * over).astype(BF16)
        slope = dot(values.T[:rows], scaled)
        d_soft[head, :rows, :] = (raised * (slope - row_dot)).astype(BF16)
        d_queries = dot(keys, d_soft[head]) * head_dim ** (-0.5)
        d_keys = dot_nt(queries, d_soft[head])
        sum_gain[:head_dim, :] += d_queries * q_normal
        sum_gain[head_dim:, :] += d_keys * k_normal
        d_proj[here, :] = head_back(d_queries, q_normal, q_inverse, q_gain).astype(BF16)
        d_proj[inner + at : inner + at + head_dim, :] = head_back(d_keys, k_normal, k_inverse, k_gain).astype(BF16)
        d_proj[2 * inner + at : 2 * inner + at + head_dim, :] = dot_nt(scaled, soft[head]).astype(BF16)
    mixed_rows = mixed[...].T[:rows]
    mixed_out[...] = mixed_rows
    if top:
        out[...] = (fed[...].astype(F32) + dot(mixed_rows, w_out[...])).astype(BF16)
    total = d_feed[...].astype(F32)
    for part, target in enumerate((d_q, d_k, d_v)):
        d_rows = d_proj[part * inner : (part + 1) * inner, :].T[:rows]
        target[...] = d_rows
        total = total + dot(d_rows, w_qkv[part])
    d_normed[...] = total.astype(BF16)
    sum_row[...] += jnp.sum(total * normed_in[...].astype(F32), axis=0, keepdims=True)


def second_kernel(rows, counts, tok, own, far, own_next, far_next, b_first, b_next, out, wide_rows):
    slots = tok.shape[1]
    live = live_of(counts[pl.program_id(0)], rows)
    x0 = padded_rows(tok.at[0], wide_rows, live)
    x1 = jnp.where(live, x0 + (own[...].astype(F32) + far[...].astype(F32)) + b_first[...], 0.0)
    branch = own_next[...].astype(F32) + far_next[...].astype(F32)
    out[0] = jnp.where(live, x1 + branch + b_next[...], 0.0)[:slots]


def tokens_kernel(rows, counts, tok, grad, own, far, gain, out, wide_rows):
    slots = tok.shape[1]
    live = live_of(counts[pl.program_id(0)], rows)
    normal, inverse = normal_rows(padded_rows(tok.at[0], wide_rows, live))
    d_normed = own[...].astype(F32) + far[...].astype(F32)
    out[0] = (grad[...] + back_rows(d_normed, normal, inverse, gain[...]))[:slots]


def whole_spec(array):
    return pl.BlockSpec(array.shape, lambda i, *_: (0,) * array.ndim)


def rows_spec(rows, columns, first=0):
    return pl.BlockSpec((rows, columns), lambda i, *_: (first + i, 0))


def image_spec(images, slots, columns, first=0):
    return pl.BlockSpec((images, slots, columns), lambda i, *_: (first + i, 0, 0))


def params(mib):
    return pltpu.CompilerParams(dimension_semantics=("arbitrary",), vmem_limit_bytes=mib * 1024 * 1024)


def cost(flops, moved):
    return pl.CostEstimate(flops=flops, bytes_accessed=moved, transcendentals=0)


def split_body(tokens, merge_map, counts, ln_gain, w_qkv, qk_gain, w_out, w_up, b_up, w_down, b_down, cotangent):
    images, slots, dim = tokens.shape
    layers, inner = w_out.shape[:2]
    units = w_up.shape[2]
    head_dim = qk_gain.shape[-1]
    heads = inner // head_dim
    rows, lanes = padded_to(slots, 16), padded_to(slots, 128)
    n_narrow = lax.axis_size("narrow")
    all_rows = images * rows

    def others(value):
        if n_narrow == 2:
            return lax.ppermute(value, "narrow", [(0, 1), (1, 0)])
        wide_value = value.astype(F32)
        return (lax.psum(wide_value, "narrow") - wide_value).astype(BF16)

    patches = jnp.pad(merge_map, ((0, 0), (0, lanes - slots)), constant_values=-1)[:, None, :]
    turned = jnp.swapaxes(w_qkv, 2, 3)
    gains = qk_gain.reshape(layers, 2 * head_dim, 1)
    bias_up = b_up.astype(F32)[:, None, :]
    ln = ln_gain[:, None, :]
    bias_down = b_down[:, None, :]
    row_array = jax.ShapeDtypeStruct((all_rows, dim), BF16)
    unit_array = jax.ShapeDtypeStruct((all_rows, units), BF16)
    head_array = jax.ShapeDtypeStruct((all_rows, inner), BF16)
    image_array = jax.ShapeDtypeStruct((images, slots, dim), F32)
    head_flops = 2 * all_rows * dim * inner * 4 + 4 * all_rows * rows * inner
    feed_flops = 2 * all_rows * dim * units * 2
    layer_bytes = 2 * (4 * dim * inner + 2 * dim * units)

    def call(kernel, operands, specs, shapes, out_specs, scratch, grid, flops, moved, mib, prefetch=1):
        return pl.pallas_call(
            kernel,
            grid_spec=pltpu.PrefetchScalarGridSpec(
                num_scalar_prefetch=prefetch,
                grid=(grid,),
                in_specs=specs,
                out_specs=out_specs,
                scratch_shapes=scratch,
            ),
            out_shape=shapes,
            compiler_params=params(mib),
            cost_estimate=cost(flops, moved),
        )(*operands)

    wide_rows = pltpu.VMEM((rows, dim), F32)
    head_scratch = [
        pltpu.VMEM((lanes, dim), BF16),
        pltpu.VMEM((3 * inner, lanes), F32),
        pltpu.VMEM((heads, lanes, lanes), BF16),
        pltpu.VMEM((inner, lanes), BF16),
    ]
    tok_spec = image_spec(1, slots, dim)
    patch_spec = image_spec(1, 1, lanes)
    row_spec = rows_spec(rows, dim)

    def forward(layer):
        weights = (ln[layer], turned[layer], gains[layer], w_out[layer], w_up[layer], bias_up[layer], w_down[layer])
        return call(
            functools.partial(forward_kernel, 0, rows),
            (counts, tokens, patches) + weights,
            [tok_spec, patch_spec] + [whole_spec(w) for w in weights],
            row_array,
            row_spec,
            [wide_rows] + head_scratch,
            images,
            head_flops + feed_flops,
            layer_bytes,
            40,
        )

    def feed_back(layer, top, pieces):
        per_step = 2
        weights = (ln[layer], bias_down[0], w_up[layer], bias_up[layer], w_down[layer])
        if not top:
            weights = (ln[layer + 1],) + weights
        block = per_step * rows
        extra = [image_array, row_array] if top else [jax.ShapeDtypeStruct((all_rows, dim), F32)]
        extra_specs = [image_spec(per_step, slots, dim), rows_spec(block, dim)] if top else [rows_spec(block, dim)]
        outs = extra + [
            row_array,
            row_array,
            row_array,
            unit_array,
            unit_array,
            jax.ShapeDtypeStruct((1, units), F32),
            jax.ShapeDtypeStruct((1, dim), F32),
        ]
        out_specs = extra_specs + [
            rows_spec(block, dim),
            rows_spec(block, dim),
            rows_spec(block, dim),
            rows_spec(block, units),
            rows_spec(block, units),
            whole_spec(outs[-2]),
            whole_spec(outs[-1]),
        ]
        operands = (tokens, pieces[0], pieces[1], cotangent) + tuple(pieces[2:])
        image_block = image_spec(per_step, slots, dim)
        specs = [image_block, rows_spec(block, dim), rows_spec(block, dim), image_block]
        specs += [rows_spec(block, dim)] * len(pieces[2:])
        return call(
            functools.partial(feed_kernel, top, 0, rows, per_step),
            (counts,) + operands + weights,
            specs + [whole_spec(w) for w in weights],
            outs,
            out_specs,
            [wide_rows],
            images // per_step,
            2 * feed_flops,
            layer_bytes * 2 + 12 * all_rows * dim * 2,
            56,
        )

    def heads_back(layer, top, normed, low, d_feed, fed):
        weights = (turned[layer], gains[layer], w_out[layer])
        streams = (normed, low, d_feed) + ((fed,) if top else ())
        outs = ([row_array] if top else []) + [
            row_array,
            head_array,
            head_array,
            head_array,
            head_array,
            jax.ShapeDtypeStruct((2 * head_dim, lanes), F32),
            jax.ShapeDtypeStruct((1, dim), F32),
        ]
        out_specs = ([row_spec] if top else []) + [
            row_spec,
            rows_spec(rows, inner),
            rows_spec(rows, inner),
            rows_spec(rows, inner),
            rows_spec(rows, inner),
            whole_spec(outs[-2]),
            whole_spec(outs[-1]),
        ]
        return call(
            functools.partial(heads_kernel, top, rows),
            (patches,) + streams + weights,
            [patch_spec] + [row_spec] * len(streams) + [whole_spec(w) for w in weights],
            outs,
            out_specs,
            [head_scratch[0]] * 2
            + [head_scratch[1], head_scratch[3], head_scratch[2], head_scratch[2], head_scratch[3]]
            + [pltpu.VMEM((3 * inner, lanes), BF16)],
            images,
            3 * head_flops,
            layer_bytes * 2,
            40,
            prefetch=0,
        )

    def weight_grad(left, right):
        return lax.dot_general(left, right, (((0,), (0,)), ((), ())), preferred_element_type=F32).astype(BF16)

    own = forward(0)
    far = others(own)
    first_out, fed, normed, low, d_feed, hidden, d_pre, s_up1, s_down1 = feed_back(1, True, (own, far))
    up1, down1 = lax.psum((weight_grad(normed, d_pre), weight_grad(hidden, low)), "wide")
    own_next, own_grad, mixed, d_q, d_k, d_v, s_gain1, s_row1 = heads_back(1, True, normed, low, d_feed, fed)
    far_grad = others(own_grad)
    far_next = others(own_next)
    qkv1 = [weight_grad(normed, part) for part in (d_q, d_k, d_v)]
    qkv1, out1 = lax.psum((qkv1, weight_grad(mixed, low)), "wide")
    g_first, normed, low, d_feed, hidden, d_pre, s_up0, s_down0 = feed_back(
        0, False, (own, far, own_grad, far_grad)
    )
    up0, down0 = lax.psum((weight_grad(normed, d_pre), weight_grad(hidden, low)), "wide")
    own_grad, mixed, d_q, d_k, d_v, s_gain0, s_row0 = heads_back(0, False, normed, low, d_feed, None)
    far_grad = others(own_grad)
    qkv0 = [weight_grad(normed, part) for part in (d_q, d_k, d_v)]
    qkv0, out0 = lax.psum((qkv0, weight_grad(mixed, low)), "wide")
    second_out = call(
        functools.partial(second_kernel, rows),
        (counts, tokens, own, far, own_next, far_next, bias_down[0], bias_down[1]),
        [tok_spec] + [row_spec] * 4 + [whole_spec(bias_down[0])] * 2,
        image_array,
        tok_spec,
        [wide_rows],
        images,
        10 * all_rows * dim,
        12 * all_rows * dim,
        16,
    )
    grad_tokens = call(
        functools.partial(tokens_kernel, rows),
        (counts, tokens, g_first, own_grad, far_grad, ln[0]),
        [tok_spec] + [row_spec] * 3 + [whole_spec(ln[0])],
        image_array,
        tok_spec,
        [wide_rows],
        images,
        10 * all_rows * dim,
        12 * all_rows * dim,
        16,
    )
    here = lax.axis_index("narrow")
    up_sums = jnp.concatenate([s_up0, s_up1])
    placed = jnp.where(jnp.arange(n_narrow)[None, :, None] == here, up_sums[:, None, :], 0.0)
    small = jnp.concatenate(
        [
            jnp.concatenate([s_row0, s_row1]) / ln_gain,
            jnp.sum(jnp.stack([s_gain0, s_gain1]), axis=-1),
            jnp.concatenate([s_down0, s_down1]) / n_narrow,
            placed.reshape(layers, n_narrow * units),
        ],
        axis=1,
    )
    small = lax.psum(small, ("wide", "narrow"))
    g_ln = small[:, :dim]
    g_gain = small[:, dim : dim + 2 * head_dim].reshape(qk_gain.shape)
    g_b_down = small[:, dim + 2 * head_dim : 2 * dim + 2 * head_dim]
    g_b_up = small[:, 2 * dim + 2 * head_dim :].reshape(layers, n_narrow, units)
    g_b_up = lax.dynamic_index_in_dim(g_b_up, here, axis=1, keepdims=False)

    def both(lower, upper):
        return jnp.stack([lower, upper]).astype(F32)

    return (
        first_out,
        second_out,
        grad_tokens,
        g_ln,
        jnp.stack([jnp.stack(qkv0), jnp.stack(qkv1)]).astype(F32),
        g_gain,
        both(out0, out1),
        both(up0, up1),
        g_b_up,
        both(down0, down1),
        g_b_down,
    )


def pick_body(*arrays):
    if arrays[4].shape[-1] % arrays[5].shape[-1] == 0:
        return split_body(*arrays)
    return body(*arrays)


def solution(mesh):
    placed = (
        P("wide", None, None),
        P("wide", None),
        P("wide"),
        P(),
        P(None, None, None, "narrow"),
        P(),
        P(None, "narrow", None),
        P(None, None, "narrow"),
        P(None, "narrow"),
        P(None, "narrow", None),
        P(),
        P("wide", None, None),
    )
    return jax.shard_map(
        pick_body,
        mesh=mesh,
        in_specs=placed,
        out_specs=(
            P("wide", None, None),
            P("wide", None, None),
            P("wide", None, None),
            P(),
            P(None, None, None, "narrow"),
            P(),
            P(None, "narrow", None),
            P(None, None, "narrow"),
            P(None, "narrow"),
            P(None, "narrow", None),
            P(),
        ),
        check_vma=False,
    )
```

```python
import functools

import jax
import jax.numpy as jnp
from jax import lax
from jax.experimental import pallas as pl
from jax.experimental.pallas import tpu as pltpu
from jax.sharding import PartitionSpec as P


def shifted_2(value, axis, by):
    length = lax.axis_size(axis)
    pairs = [(i, i + by) for i in range(length) if 0 <= i + by < length]
    return lax.ppermute(value, axis, pairs)


def norm_rows(inputs, gain_row):
    centre = jnp.mean(inputs, axis=-1, keepdims=True)
    centered = inputs - centre
    inverse = lax.rsqrt(jnp.mean(centered * centered, axis=-1, keepdims=True) + 1e-06)
    normal = centered * inverse
    return (normal, inverse, normal * gain_row)


def norm_back(upstream, normal, inverse, gain_row):
    scaled = upstream * gain_row
    return inverse * (
        scaled
        - jnp.mean(scaled, axis=-1, keepdims=True)
        - normal * jnp.mean(scaled * normal, axis=-1, keepdims=True)
    )


def attend(normed_low, key_bias, qkv_full, out_full, qk_gains):
    head_dim = qk_gains.shape[-1]
    head_count = qkv_full.shape[-1] // head_dim
    qkv_heads = qkv_full.reshape(3, qkv_full.shape[1], head_count, head_dim)
    projected = jnp.einsum(
        "bsd,kdhe->kbhse", normed_low, qkv_heads, preferred_element_type=jnp.float32
    )
    q_normal, q_inverse, queries = norm_rows(projected[0], qk_gains[0])
    k_normal, k_inverse, keys_normed = norm_rows(projected[1], qk_gains[1])
    queries_low = queries.astype(jnp.bfloat16)
    keys_low = keys_normed.astype(jnp.bfloat16)
    values_low = projected[2].astype(jnp.bfloat16)
    score_scale = head_dim ** (-0.5)
    scores = jnp.einsum(
        "bhse,bhte->bhst", queries_low, keys_low, preferred_element_type=jnp.float32
    )
    logits = scores * score_scale + key_bias[:, None, None, :]
    shifted = jnp.exp(logits - jnp.max(logits, axis=-1, keepdims=True))
    softened = shifted / jnp.sum(shifted, axis=-1, keepdims=True)
    soft_low = softened.astype(jnp.bfloat16)
    mixed_low = jnp.einsum(
        "bhst,bhte->bhse", soft_low, values_low, preferred_element_type=jnp.float32
    ).astype(jnp.bfloat16)
    out_heads = out_full.reshape(head_count, head_dim, out_full.shape[-1])
    branch = jnp.einsum("bhse,hed->bsd", mixed_low, out_heads, preferred_element_type=jnp.float32)
    kept_parts = (
        q_normal,
        q_inverse,
        k_normal,
        k_inverse,
        queries_low,
        keys_low,
        values_low,
        softened,
        soft_low,
        mixed_low,
        qkv_heads,
        out_heads,
        score_scale,
    )
    return (branch, kept_parts)


def attend_back(normed_low, key_bias, qkv_full, out_full, qk_gains, grad_low):
    branch, kept_parts = attend(normed_low, key_bias, qkv_full, out_full, qk_gains)
    (
        q_normal,
        q_inverse,
        k_normal,
        k_inverse,
        queries_low,
        keys_low,
        values_low,
        softened,
        soft_low,
        mixed_low,
        qkv_heads,
        out_heads,
        score_scale,
    ) = kept_parts
    d_mixed = jnp.einsum(
        "bsd,hed->bhse", grad_low, out_heads, preferred_element_type=jnp.float32
    ).astype(jnp.bfloat16)
    g_out = jnp.einsum(
        "bhse,bsd->hed", mixed_low, grad_low, preferred_element_type=jnp.float32
    ).reshape(out_full.shape)
    d_soft = jnp.einsum("bhse,bhte->bhst", d_mixed, values_low, preferred_element_type=jnp.float32)
    row_dot = jnp.sum(softened * d_soft, axis=-1, keepdims=True)
    d_scores = (softened * (d_soft - row_dot) * score_scale).astype(jnp.bfloat16)
    d_queries = jnp.einsum(
        "bhst,bhte->bhse", d_scores, keys_low, preferred_element_type=jnp.float32
    )
    d_keys = jnp.einsum(
        "bhst,bhse->bhte", d_scores, queries_low, preferred_element_type=jnp.float32
    )
    d_values = jnp.einsum("bhst,bhse->bhte", soft_low, d_mixed, preferred_element_type=jnp.float32)
    g_gains = jnp.stack(
        [jnp.sum(d_queries * q_normal, axis=(0, 1, 2)), jnp.sum(d_keys * k_normal, axis=(0, 1, 2))]
    )
    d_projected = jnp.stack(
        [
            norm_back(d_queries, q_normal, q_inverse, qk_gains[0]),
            norm_back(d_keys, k_normal, k_inverse, qk_gains[1]),
            d_values,
        ]
    ).astype(jnp.bfloat16)
    g_qkv = jnp.einsum(
        "bsd,kbhse->kdhe", normed_low, d_projected, preferred_element_type=jnp.float32
    ).reshape(qkv_full.shape)
    d_normed = jnp.einsum(
        "kbhse,kdhe->bsd", d_projected, qkv_heads, preferred_element_type=jnp.float32
    )
    return (d_normed, g_qkv, g_out, g_gains)


def expand(normed_low, up_full, bias_full, down_full):
    pre_act = jnp.einsum(
        "bsd,df->bsf", normed_low, up_full, preferred_element_type=jnp.float32
    ) + bias_full.astype(jnp.float32)
    hidden, gelu_back = jax.vjp(jax.nn.gelu, pre_act)
    hidden_low = hidden.astype(jnp.bfloat16)
    branch = jnp.einsum("bsf,fd->bsd", hidden_low, down_full, preferred_element_type=jnp.float32)
    return (branch, hidden_low, gelu_back)


def expand_back(normed_low, up_full, bias_full, down_full, grad_low):
    branch, hidden_low, gelu_back = expand(normed_low, up_full, bias_full, down_full)
    d_hidden = jnp.einsum("bsd,fd->bsf", grad_low, down_full, preferred_element_type=jnp.float32)
    d_pre = gelu_back(d_hidden)[0].astype(jnp.bfloat16)
    g_bias = jnp.sum(d_pre, axis=(0, 1), dtype=jnp.float32)
    g_up = jnp.einsum("bsd,bsf->df", normed_low, d_pre, preferred_element_type=jnp.float32)
    g_down = jnp.einsum("bsf,bsd->fd", hidden_low, grad_low, preferred_element_type=jnp.float32)
    d_normed = jnp.einsum("bsf,df->bsd", d_pre, up_full, preferred_element_type=jnp.float32)
    return (d_normed, g_up, g_bias, g_down)


def body(
    tokens, merge_map, counts, ln_gain, w_qkv, qk_gain, w_out, w_up, b_up, w_down, b_down, cotangent
):
    pair_gap = lax.axis_size("narrow") // 2
    on_attention = lax.axis_index("narrow") < pair_gap
    layers = ln_gain.shape[0]
    col_half = w_qkv.shape[-1]
    unit_half = w_up.shape[-1]
    model_dim = tokens.shape[-1]
    slot_ids = jnp.arange(tokens.shape[1], dtype=jnp.int32)
    live_rows = slot_ids[None, :] < counts[:, None]
    row_weight = jnp.where(live_rows, 1.0, 0.0).astype(jnp.float32)[:, :, None]
    merged_sizes = jnp.sum(
        jnp.where(merge_map[:, :, None] == slot_ids[None, None, :], 1.0, 0.0), axis=1
    ).astype(jnp.float32)
    key_bias = jnp.where(live_rows, jnp.log(jnp.where(live_rows, merged_sizes, 1.0)), -1e30)
    attn_far = shifted_2((w_qkv, w_out), "narrow", -pair_gap)
    mlp_far = shifted_2((w_up, b_up, w_down), "narrow", pair_gap)

    def attention_weights(layer_at):
        qkv_full = jnp.concatenate([w_qkv[layer_at], attn_far[0][layer_at]], axis=-1)
        out_full = jnp.concatenate([w_out[layer_at], attn_far[1][layer_at]], axis=0)
        return (qkv_full, out_full)

    def feed_weights(layer_at):
        up_full = jnp.concatenate([mlp_far[0][layer_at], w_up[layer_at]], axis=-1)
        bias_full = jnp.concatenate([mlp_far[1][layer_at], b_up[layer_at]], axis=-1)
        down_full = jnp.concatenate([mlp_far[2][layer_at], w_down[layer_at]], axis=0)
        return (up_full, bias_full, down_full)

    current = tokens.astype(jnp.float32)
    layer_inputs = []
    outputs = []
    for layer_at in range(layers):
        normal, inverse, normed = norm_rows(current, ln_gain[layer_at])
        normed_low = normed.astype(jnp.bfloat16)

        def attention_forward():
            qkv_full, out_full = attention_weights(layer_at)
            return attend(normed_low, key_bias, qkv_full, out_full, qk_gain[layer_at])[0]

        def feed_forward():
            up_full, bias_full, down_full = feed_weights(layer_at)
            return expand(normed_low, up_full, bias_full, down_full)[0]

        partial_value = lax.cond(on_attention, attention_forward, feed_forward)
        layer_inputs.append(current)
        branch_total = lax.psum(partial_value, "narrow")
        current = row_weight * (current + branch_total + b_down[layer_at])
        outputs.append(current)
    grad_rows = cotangent.astype(jnp.float32)
    collected = []
    for layer_at in reversed(range(layers)):
        normal, inverse, normed = norm_rows(layer_inputs[layer_at], ln_gain[layer_at])
        normed_low = normed.astype(jnp.bfloat16)
        masked_grad = row_weight * grad_rows
        grad_low = masked_grad.astype(jnp.bfloat16)

        def attention_side():
            qkv_full, out_full = attention_weights(layer_at)
            d_normed, g_qkv, g_out, g_gains = attend_back(
                normed_low, key_bias, qkv_full, out_full, qk_gain[layer_at], grad_low
            )
            return (
                d_normed,
                g_gains,
                g_qkv,
                g_out,
                jnp.zeros((model_dim, 2 * unit_half), jnp.float32),
                jnp.zeros((2 * unit_half,), jnp.float32),
                jnp.zeros((2 * unit_half, model_dim), jnp.float32),
            )

        def feed_side():
            up_full, bias_full, down_full = feed_weights(layer_at)
            d_normed, g_up, g_bias, g_down = expand_back(
                normed_low, up_full, bias_full, down_full, grad_low
            )
            return (
                d_normed,
                jnp.zeros(qk_gain[layer_at].shape, jnp.float32),
                jnp.zeros((3, model_dim, 2 * col_half), jnp.float32),
                jnp.zeros((2 * col_half, model_dim), jnp.float32),
                g_up,
                g_bias,
                g_down,
            )

        returned = lax.cond(on_attention, attention_side, feed_side)
        d_normed, g_gains = (
            lax.psum(returned[0].astype(jnp.bfloat16), "narrow").astype(jnp.float32),
            lax.psum(returned[1].astype(jnp.bfloat16), "narrow").astype(jnp.float32),
        )
        g_ln = jnp.sum(d_normed * normal, axis=(0, 1))
        grad_rows = masked_grad + norm_back(d_normed, normal, inverse, ln_gain[layer_at])
        qkv_far, out_far = (
            shifted_2(returned[2][..., col_half:].astype(jnp.bfloat16), "narrow", pair_gap).astype(
                jnp.float32
            ),
            shifted_2(returned[3][col_half:].astype(jnp.bfloat16), "narrow", pair_gap).astype(
                jnp.float32
            ),
        )
        up_far, bias_far, down_far = (
            shifted_2(returned[4][:, :unit_half].astype(jnp.bfloat16), "narrow", -pair_gap).astype(
                jnp.float32
            ),
            shifted_2(returned[5][:unit_half].astype(jnp.bfloat16), "narrow", -pair_gap).astype(
                jnp.float32
            ),
            shifted_2(returned[6][:unit_half].astype(jnp.bfloat16), "narrow", -pair_gap).astype(
                jnp.float32
            ),
        )
        own_qkv = jnp.where(on_attention, returned[2][..., :col_half], qkv_far)
        own_out = jnp.where(on_attention, returned[3][:col_half], out_far)
        own_up = jnp.where(on_attention, up_far, returned[4][:, unit_half:])
        own_bias = jnp.where(on_attention, bias_far, returned[5][unit_half:])
        own_down = jnp.where(on_attention, down_far, returned[6][unit_half:])
        g_bdown = jnp.sum(masked_grad, axis=(0, 1))
        shards = (own_qkv, own_out, own_up, own_bias, own_down, g_ln, g_gains, g_bdown)
        collected.append(shards)
    collected = collected[::-1]
    stacked = tuple(
        (jnp.stack([element[position] for element in collected]) for position in range(8))
    )
    stacked = (
        lax.psum(stacked[0].astype(jnp.bfloat16), "wide").astype(jnp.float32),
        lax.psum(stacked[1].astype(jnp.bfloat16), "wide").astype(jnp.float32),
        lax.psum(stacked[2].astype(jnp.bfloat16), "wide").astype(jnp.float32),
        lax.psum(stacked[3].astype(jnp.bfloat16), "wide").astype(jnp.float32),
        lax.psum(stacked[4].astype(jnp.bfloat16), "wide").astype(jnp.float32),
        lax.psum(stacked[5].astype(jnp.bfloat16), "wide").astype(jnp.float32),
        lax.psum(stacked[6].astype(jnp.bfloat16), "wide").astype(jnp.float32),
        lax.psum(stacked[7].astype(jnp.bfloat16), "wide").astype(jnp.float32),
    )
    return (
        outputs[0],
        outputs[-1],
        grad_rows,
        stacked[5],
        stacked[0],
        stacked[6],
        stacked[1],
        stacked[2],
        stacked[3],
        stacked[4],
        stacked[7],
    )


EPS = 1e-06
F32 = jnp.float32
BF16 = jnp.bfloat16
COST_SCALE = 3
AG_AFTER = 1
VMEM_BYTES = 60 * 1024 * 1024
GELU_IN = 0.7978845608028654
GELU_CUBE = 0.044715


def padded_to(length, step):
    return -(-length // step) * step


def dot(a, b):
    return jnp.dot(a, b, preferred_element_type=F32)


def dot_nt(a, b):
    return lax.dot_general(a, b, (((1,), (1,)), ((), ())), preferred_element_type=F32)


def normal_rows(x):
    centered = x - jnp.mean(x, axis=-1, keepdims=True)
    inverse = lax.rsqrt(jnp.mean(centered * centered, axis=-1, keepdims=True) + EPS)
    return centered * inverse, inverse


def back_rows(upstream, normal, inverse, gain):
    scaled = upstream * gain
    return inverse * (
        scaled
        - jnp.mean(scaled, axis=-1, keepdims=True)
        - normal * jnp.mean(scaled * normal, axis=-1, keepdims=True)
    )


def live_of(count, rows):
    return lax.broadcasted_iota(jnp.int32, (rows, 1), 0) < count


def fill_rows(source, wide_rows):
    slots = source.shape[0]
    edge = slots // 8 * 8
    wide_rows[edge:, :] = jnp.zeros((wide_rows.shape[0] - edge, wide_rows.shape[1]), F32)
    wide_rows[:slots, :] = source[...].astype(F32)


def head_norm(x):
    centered = x - jnp.mean(x, axis=1, keepdims=True)
    inverse = lax.rsqrt(jnp.mean(centered * centered, axis=1, keepdims=True) + EPS)
    return centered * inverse, inverse


def head_back(upstream, normal, inverse, gain):
    scaled = upstream * gain
    return inverse * (
        scaled
        - jnp.mean(scaled, axis=1, keepdims=True)
        - normal * jnp.mean(scaled * normal, axis=1, keepdims=True)
    )


def key_sizes(patch_ref, image, rows):
    slots = patch_ref.shape[1]
    slot = lax.broadcasted_iota(jnp.int32, (rows, slots), 0)
    named = jnp.where(patch_ref[pl.ds(image, 1), :] == slot, 1.0, 0.0)
    return jnp.sum(named, axis=-1, keepdims=True)


def head_gains(qk_gain, layer):
    both = qk_gain[layer]
    return [jnp.broadcast_to(both[at : at + 1, :], (8, both.shape[1])).T[:, :1] for at in range(2)]


def project(turned, normed, gains, proj, lows):
    inner, head_dim = proj.shape[0] // 3, gains[0].shape[0]
    heads, lanes = inner // head_dim, proj.shape[1]
    proj[...] = dot_nt(turned, normed)
    inverses = []
    for part in range(2):
        here = slice(part * inner, (part + 1) * inner)
        normal, inverse = head_norm(proj[here, :].reshape(heads, head_dim, lanes))
        inverses.append(inverse)
        proj[here, :] = normal.reshape(inner, lanes)
        low = (normal * gains[part][None]).astype(BF16)
        if part == 0:
            low = (low.astype(F32) * head_dim ** (-0.5)).astype(BF16)
        lows[here, :] = low.reshape(inner, lanes)
    lows[2 * inner :, :] = proj[2 * inner :, :].astype(BF16)
    return inverses


def soften(lows, sizes, scores, soft):
    heads, rows, strip = scores.shape[0], scores.shape[1], 16
    inner = lows.shape[0] // 3
    head_dim = inner // heads
    for head in range(heads):
        at = head * head_dim
        keys = lows[inner + at : inner + at + head_dim, :]
        scores[head] = dot(keys.T[:rows], lows[at : at + head_dim, :])
    over = []
    for head in range(heads):
        total = jnp.zeros((8, scores.shape[2]), F32)
        for at in range(0, rows, strip):
            raised = jnp.exp(scores[head, at : at + strip, :]) * sizes[at : at + strip, :]
            scores[head, at : at + strip, :] = raised
            soft[head, at : at + strip, :] = raised.astype(BF16)
            total = total + (raised[:8] + raised[8:])
        over.append(1.0 / jnp.sum(total, axis=0, keepdims=True))
    return over


def forward_kernel(layer, first, rows, turn, counts, *refs):
    tok, patch, gain, w_qkv, qk_gain, w_out, w_up, b_up, w_down, out = refs[:10]
    if turn:
        turned = refs[10]
        refs = refs[11:]
    else:
        turned = w_qkv
        refs = refs[10:]
    wide_rows, normed, proj, lows, scores, soft, mixed, pre_rows, hidden = refs
    step = pl.program_id(0)
    inner = w_out.shape[1]

    @pl.when(step == 0)
    def _():
        normed[...] = jnp.zeros(normed.shape, BF16)
        soft[...] = jnp.zeros(soft.shape, BF16)
        if turn:
            for part in range(3):
                turned[0, part] = w_qkv[0, part].T

    fill_rows(tok.at[0], wide_rows.at[0])
    strip = 16
    for at in range(0, rows, strip):
        x = jnp.where(live_of(counts[first + step] - at, strip), wide_rows[0, at : at + strip, :], 0.0)
        normed[at : at + strip, :] = (normal_rows(x)[0] * gain[layer : layer + 1, :]).astype(BF16)
    gains = head_gains(qk_gain, layer)
    head_dim = gains[0].shape[0]
    project(turned[0].reshape(3 * inner, turned.shape[3]), normed[...], gains, proj, lows)
    over = soften(lows, key_sizes(patch, first + step, rows), scores, soft)
    for head in range(inner // head_dim):
        at = head * head_dim
        values = lows[2 * inner + at : 2 * inner + at + head_dim, :]
        mixed[at : at + head_dim, :] = (dot(values, soft[head]) * over[head]).astype(BF16)
    bias = b_up[...].astype(F32)[layer : layer + 1, :]
    units = w_up.shape[2]
    tile = units // 3
    for slot, at in enumerate(range(0, units, tile)):
        pre_rows[slot % 2] = dot(normed[:rows, :], w_up[0, :, at : at + tile])
        for row in range(0, rows, strip):
            pre = pre_rows[slot % 2, row : row + strip, :] + bias[:, at : at + tile]
            bent = jnp.tanh(pre * (GELU_IN + (GELU_IN * GELU_CUBE) * (pre * pre)))
            hidden[row : row + strip, at : at + tile] = (pre * (0.5 + 0.5 * bent)).astype(BF16)
    out[...] = (dot(mixed[...].T[:rows], w_out[0]) + dot(hidden[...], w_down[0])).astype(BF16)


def feed_kernel(layer, top, first, rows, per_step, counts, *refs):
    refs = list(refs)
    tok, own, far, cot = refs[:4]
    refs = refs[4:]
    if not top:
        own_grad, far_grad = refs[:2]
        refs = refs[2:]
    gain, b_prev, w_up, b_up, w_down = refs[:5]
    refs = refs[5:]
    extra = refs[0]
    refs = refs[1:]
    normed, low, d_feed, hidden_out, d_pre_out, sum_up, sum_down, normed_t, low_t, wide_rows, pre_rows, d_rows = refs
    step = pl.program_id(0)

    @pl.when(step == 0)
    def _():
        sum_up[...] = jnp.zeros(sum_up.shape, F32)
        sum_down[...] = jnp.zeros(sum_down.shape, F32)

    strip = 16
    for j in range(per_step):
        count = counts[first + step * per_step + j]
        fill_rows(tok.at[j], wide_rows.at[0])
        fill_rows(cot.at[j], wide_rows.at[1])
        total = jnp.zeros((8, tok.shape[2]), F32)
        for at in range(0, rows, strip):
            block = slice(j * rows + at, j * rows + at + strip)
            live = live_of(count - at, strip)
            x0 = jnp.where(live, wide_rows[0, at : at + strip, :], 0.0)
            branch = own[block, :].astype(F32) + far[block, :].astype(F32)
            x1 = jnp.where(live, x0 + branch + b_prev[:1, :], 0.0)
            grad = jnp.where(live, wide_rows[1, at : at + strip, :], 0.0)
            if top:
                x = x1
            else:
                x = x0
                normal, inverse = normal_rows(x1)
                d_normed = own_grad[block, :].astype(F32) + far_grad[block, :].astype(F32)
                grad = grad + back_rows(d_normed, normal, inverse, gain[layer + 1 : layer + 2, :])
                extra[block, :] = grad
            normed[block, :] = (normal_rows(x)[0] * gain[layer : layer + 1, :]).astype(BF16)
            low[block, :] = grad.astype(BF16)
            total = total + (grad[:8] + grad[8:])
        sum_down[...] += jnp.sum(total, axis=0, keepdims=True)
    normed_t[0] = normed[...].T
    low_t[0] = low[...].T
    bias = b_up[...].astype(F32)[layer : layer + 1, :]
    units = w_up.shape[2]
    tile = units // 3
    for slot, at in enumerate(range(0, units, tile)):
        part = slice(at, at + tile)
        pre_rows[slot % 2] = dot(normed[...], w_up[0, :, part])
        d_rows[slot % 2] = dot_nt(low[...], w_down[0, part, :])
        total = jnp.zeros((8, tile), F32)
        for row in range(0, per_step * rows, strip):
            block = slice(row, row + strip)
            pre = pre_rows[slot % 2, block, :] + bias[:, part]
            square = pre * pre
            bent = jnp.tanh(pre * (GELU_IN + (GELU_IN * GELU_CUBE) * square))
            half = 0.5 + 0.5 * bent
            hidden_out[block, part] = (pre * half).astype(BF16)
            steep = GELU_IN + (3 * GELU_IN * GELU_CUBE) * square
            slope = half + (0.5 * pre) * ((1.0 - bent * bent) * steep)
            d_pre = (d_rows[slot % 2, block, :] * slope).astype(BF16)
            d_pre_out[block, part] = d_pre
            d_pre = d_pre.astype(F32)
            total = total + (d_pre[:8] + d_pre[8:])
        sum_up[:, part] += jnp.sum(total, axis=0, keepdims=True)
    d_feed[...] = dot_nt(d_pre_out[...], w_up[0]).astype(BF16)
    if top:
        extra[...] = dot(hidden_out[...], w_down[0]).astype(BF16)


def heads_kernel(layer, top, first, rows, patch, normed_in, low_in, d_feed, *refs):
    refs = list(refs)
    if top:
        fed = refs[0]
        refs = refs[1:]
    w_qkv, qk_gain, w_out = refs[:3]
    refs = refs[3:]
    if top:
        out = refs[0]
        refs = refs[1:]
    d_normed, rights, sum_gain, sum_row = refs[:4]
    normed, low, proj, lows, d_mixed, scores, slopes, soft, d_soft, mixed, d_heads, d_proj, row_dots, total = refs[4:]
    step = pl.program_id(0)
    inner = w_out.shape[1]
    gains = head_gains(qk_gain, layer)
    head_dim = gains[0].shape[0]

    @pl.when(step == 0)
    def _():
        normed[...] = jnp.zeros(normed.shape, BF16)
        low[...] = jnp.zeros(low.shape, BF16)
        soft[...] = jnp.zeros(soft.shape, BF16)
        d_soft[...] = jnp.zeros(d_soft.shape, BF16)
        sum_gain[...] = jnp.zeros(sum_gain.shape, F32)
        sum_row[...] = jnp.zeros(sum_row.shape, F32)

    normed[:rows, :] = normed_in[...]
    low[:rows, :] = low_in[...]
    turned = w_qkv[0].reshape(3 * inner, w_qkv.shape[3])
    heads, lanes = inner // head_dim, proj.shape[1]
    inverses = project(turned, normed[...], gains, proj, lows)
    d_mixed[...] = dot_nt(w_out[0], low[...]).astype(BF16)
    over = soften(lows, key_sizes(patch, first + step, rows), scores, soft)
    for head in range(heads):
        here = slice(head * head_dim, (head + 1) * head_dim)
        mixed_here = dot(lows[2 * inner + here.start : 2 * inner + here.stop, :], soft[head]) * over[head]
        mixed[here, :] = mixed_here.astype(BF16)
        d_mixed_here = d_mixed[here, :].astype(F32)
        row_dots[head : head + 1, :] = jnp.sum(d_mixed_here * mixed_here, axis=0, keepdims=True) * over[head]
        d_mixed[here, :] = (d_mixed_here * over[head]).astype(BF16)
    for head in range(heads):
        here = slice(head * head_dim, (head + 1) * head_dim)
        values = lows[2 * inner + here.start : 2 * inner + here.stop, :]
        slopes[head] = dot(values.T[:rows], d_mixed[here, :])
    for head in range(heads):
        for row in range(0, rows, 16):
            block = slice(row, row + 16)
            slope = slopes[head, block, :] - row_dots[head : head + 1, :]
            d_soft[head, block, :] = (scores[head, block, :] * slope).astype(BF16)
    for head in range(heads):
        here = slice(head * head_dim, (head + 1) * head_dim)
        keys = slice(inner + here.start, inner + here.stop)
        values = slice(2 * inner + here.start, 2 * inner + here.stop)
        d_heads[here, :] = dot(lows[keys, :], d_soft[head]) * head_dim ** (-0.5)
        d_heads[keys, :] = dot_nt(lows[here, :], d_soft[head])
        d_proj[values, :] = dot_nt(d_mixed[here, :], soft[head]).astype(BF16)
    for part in range(2):
        here = slice(part * inner, (part + 1) * inner)
        normal = proj[here, :].reshape(heads, head_dim, lanes)
        upstream = d_heads[here, :].reshape(heads, head_dim, lanes)
        sum_gain[part * head_dim : (part + 1) * head_dim, :] += jnp.sum(upstream * normal, axis=0)
        back = head_back(upstream, normal, inverses[part], gains[part][None])
        d_proj[here, :] = back.reshape(inner, lanes).astype(BF16)
    mixed_rows = mixed[...].T[:rows]
    rights[:, 3 * inner :] = mixed_rows
    if top:
        out[...] = (fed[...].astype(F32) + dot(mixed_rows, w_out[0])).astype(BF16)
    for part in range(3):
        rights[:, part * inner : (part + 1) * inner] = d_proj[part * inner : (part + 1) * inner, :].T[:rows]
    total[...] = dot(rights[:, : 3 * inner], turned)
    row_sum = jnp.zeros((8, total.shape[1]), F32)
    for row in range(0, rows, 16):
        block = slice(row, row + 16)
        d_here = total[block, :] + d_feed[block, :].astype(F32)
        d_normed[block, :] = d_here.astype(BF16)
        d_here = d_here * normed_in[block, :].astype(F32)
        row_sum = row_sum + (d_here[:8] + d_here[8:])
    sum_row[...] += jnp.sum(row_sum, axis=0, keepdims=True)


def live_slots(counts, shape):
    slot = lax.broadcasted_iota(jnp.int32, shape, 0) + pl.program_id(0) * shape[0]
    image = lax.broadcasted_iota(jnp.int32, shape, 1)
    count = jnp.zeros(shape, jnp.int32)
    for at in range(shape[1]):
        count = jnp.where(image == at, counts[at], count)
    return slot < count


def chunk_sums(refs, sums):
    image = 0
    for own, far in refs:
        for at in range(own.shape[0]):
            sums[:, image, :] = own[at].astype(F32) + far[at].astype(F32)
            image += 1


def output_kernel(layer, chunks, counts, before, *refs):
    pairs = [(refs[2 * at], refs[2 * at + 1]) for at in range(chunks)]
    bias, out, sums = refs[2 * chunks :]
    live = live_slots(counts, out.shape[:2] + (1,))
    chunk_sums(pairs, sums)
    for at in range(0, out.shape[0], 2):
        part = slice(at, at + 2)
        total = before[part].astype(F32) + sums[part] + bias[layer : layer + 1, :]
        out[part] = jnp.where(live[part], total, 0.0)


def tokens_kernel(chunks, counts, tok, *refs):
    pairs = [(refs[2 * at], refs[2 * at + 1]) for at in range(chunks)]
    grads = refs[2 * chunks : -4]
    gain, out, sums, turned = refs[-4:]
    live = live_slots(counts, out.shape[:2] + (1,))
    chunk_sums(pairs, sums)
    image = 0
    for grad in grads:
        for at in range(grad.shape[0]):
            turned[:, image, :] = grad[at]
            image += 1
    for at in range(0, out.shape[0], 2):
        part = slice(at, at + 2)
        normal, inverse = normal_rows(jnp.where(live[part], tok[part].astype(F32), 0.0))
        total = turned[part] + back_rows(sums[part], normal, inverse, gain[:1, :])
        out[part] = jnp.where(live[part], total, 0.0)


def weight_tile(lefts, rights):
    total, first, at = None, 0, 0
    for left in lefts:
        for block in range(left.shape[0]):
            rows = left.shape[2]
            if first == rights[at].shape[0]:
                first, at = 0, at + 1
            term = dot(left[block], rights[at][first : first + rows, :])
            total = term if total is None else total + term
            first += rows
    return total.astype(BF16)


def store_tile(bit, tile, both, kept, sent, columns=slice(None)):
    if sent is None:
        kept[:, columns] = tile
        return
    both[:, :, : tile.shape[1]] = tile.reshape(2, -1, tile.shape[1])
    kept[:, columns] = both[bit, :, : tile.shape[1]]
    sent[:, columns] = both[1 - bit, :, : tile.shape[1]]


def feed_weight_kernel(counts, *refs):
    normed_t, low_t, d_pre, hidden = [refs[first:last] for first, last in counts]
    out = refs[-1]
    half = pl.num_programs(0) // 2

    @pl.when(pl.program_id(0) < half)
    def _():
        out[...] = weight_tile(normed_t, d_pre)

    @pl.when(pl.program_id(0) >= half)
    def _():
        out[...] = weight_tile(low_t, hidden)


def heads_weight_kernel(counts, bits, *refs):
    normed_t, low_t, rights, gain, *sums = [refs[first:last] for first, last in counts]
    if sums:
        kept, sent, both, lined = refs[-4:]
    else:
        kept, sent, both = refs[-1], None, None
    inner = rights[0].shape[1]
    for part in range(4):

        @pl.when(pl.program_id(0) == part)
        def _(part=part):
            lefts = low_t if part == 3 else normed_t
            columns = slice(part * inner, (part + 1) * inner)
            store_tile(bits[0], weight_tile(lefts, rights), both, kept, sent, columns)

    if not sums:
        return

    @pl.when(pl.program_id(0) == 0)
    def _():
        lined[...] = jnp.zeros(lined.shape, F32)
        row = 0
        for layer in range(len(sums) // 4):
            s_row, s_gain, s_down, s_up = [
                functools.reduce(lambda a, b: a + b, [one[...] for one in group])
                for group in sums[4 * layer : 4 * layer + 4]
            ]
            s_row = s_row / gain[0][layer : layer + 1, :]
            s_gain = jnp.sum(s_gain.T, axis=0, keepdims=True)
            for values in (s_row, s_gain, s_down, s_up):
                for at in range(0, values.shape[1], 128):
                    lined[row : row + 1, :] = values[:, at : at + 128]
                    row += 1
        none = jnp.zeros((kept.shape[0], 128), BF16)
        kept[:, 4 * inner :] = none
        sent[:, 4 * inner :] = none
        small = lined[...].astype(BF16)

        @pl.when(bits[0] == 0)
        def _():
            kept[: lined.shape[0], 4 * inner :] = small

        @pl.when(bits[0] == 1)
        def _():
            sent[: lined.shape[0], 4 * inner :] = small


def halve_kernel(bits, kept, got, *refs):
    total = (kept[...].astype(F32) + got[...].astype(F32)).astype(BF16)
    if len(refs) == 1:
        refs[0][...] = total
        return
    left, sent, both = refs
    both[...] = total.reshape(both.shape)
    left[...] = both[bits[0]]
    sent[...] = both[1 - bits[0]]


def join_kernel(bits, own, got, out):
    out[bits[0]] = own[...]
    out[1 - bits[0]] = got[...]


def feed_unpack_kernel(bits, own, got, *refs):
    up, down = refs[-2:]
    units = up.shape[2]

    def place(pack):
        up[0] = pack[:, :units].astype(F32)
        down[0] = pack[:, units : 2 * units].astype(F32).T

    pl.when(pl.program_id(0) == 0)(lambda: place(own))
    pl.when(pl.program_id(0) == 1)(lambda: place(got))


def heads_unpack_kernel(bits, own, got, *refs):
    qkv, out = refs[-2:]
    inner = qkv.shape[3]

    def place(pack):
        for at in range(3):
            qkv[0, at] = pack[:, at * inner : (at + 1) * inner].astype(F32)
        out[0] = pack[:, 3 * inner : 4 * inner].astype(F32).T

    pl.when(pl.program_id(0) == 0)(lambda: place(own))
    pl.when(pl.program_id(0) == 1)(lambda: place(got))


def spans(groups):
    ends = []
    for group in groups:
        first = ends[-1][1] if ends else 0
        ends.append((first, first + len(group)))
    return tuple(ends)


def whole_spec(array):
    return pl.BlockSpec(array.shape, lambda i, *_: (0,) * array.ndim)


def layer_spec(array, layer):
    if layer is None:
        return whole_spec(array)
    return pl.BlockSpec((1,) + array.shape[1:], lambda i, *_: (layer,) + (0,) * (array.ndim - 1))


def rows_spec(rows, columns, first=0):
    return pl.BlockSpec((rows, columns), lambda i, *_: (first + i, 0))


def image_spec(images, slots, columns, first=0):
    return pl.BlockSpec((images, slots, columns), lambda i, *_: (first + i, 0, 0))


def slots_spec(images, slots, columns):
    return pl.BlockSpec((images, slots, columns), lambda i, *_: (0, i, 0))


def call(kernel, operands, specs, shapes, out_specs, scratch, grid, flops, moved, prefetch=1, aliases=None):
    return pl.pallas_call(
        kernel,
        grid_spec=pltpu.PrefetchScalarGridSpec(
            num_scalar_prefetch=prefetch,
            grid=(grid,),
            in_specs=specs,
            out_specs=out_specs,
            scratch_shapes=scratch,
        ),
        out_shape=shapes,
        compiler_params=pltpu.CompilerParams(
            dimension_semantics=("arbitrary",), vmem_limit_bytes=VMEM_BYTES
        ),
        cost_estimate=pl.CostEstimate(flops=flops // COST_SCALE, bytes_accessed=moved // COST_SCALE, transcendentals=0),
        input_output_aliases=aliases or {},
    )(*operands)


def bit_steps(axis):
    size = lax.axis_size(axis)
    bits = size.bit_length() - 1
    here = lax.axis_index(axis)
    steps = []
    for step in range(bits):

        def bit_of(place, step=step):
            if bits < 3 or step not in (1, 2):
                return 1 << step
            return 1 << (step if place % 2 == 0 else 3 - step)
        pairs = [(place, place ^ bit_of(place)) for place in range(size)]
        bit = (here >> step) & 1
        if bits >= 3 and step in (1, 2):
            bit = jnp.where(here % 2 == 0, bit, (here >> (3 - step)) & 1)
        steps.append((pairs, bit))
    return steps


def tie(value, *others):
    return lax.optimization_barrier((value,) + others)[0]


def column_tiles(width):
    return 3 if width % 3 == 0 and width >= 3072 else 1


def halve(bit, kept, got, last):
    rows, width = kept.shape
    tiles = column_tiles(width)
    tile = width // tiles
    out_rows = rows if last else rows // 2
    spec = pl.BlockSpec((out_rows, tile), lambda i, *_: (0, i))
    whole = pl.BlockSpec((rows, tile), lambda i, *_: (0, i))
    count = 1 if last else 2
    return call(
        halve_kernel,
        (bit, kept, got),
        [whole] * 2,
        [jax.ShapeDtypeStruct((out_rows, width), BF16)] * count,
        [spec] * count,
        [] if last else [pltpu.VMEM((2, out_rows, tile), BF16)],
        tiles,
        rows * width,
        6 * rows * width,
    )


def join(bit, own, got):
    rows, width = own.shape
    tiles = column_tiles(width)
    tile = width // tiles
    spec = pl.BlockSpec((rows, tile), lambda i, *_: (0, i))
    out = call(
        join_kernel,
        (bit, own, got),
        [spec] * 2,
        jax.ShapeDtypeStruct((2, rows, width), BF16),
        pl.BlockSpec((2, rows, tile), lambda i, *_: (0, 0, i)),
        [],
        tiles,
        rows * width,
        8 * rows * width,
    )
    return out.reshape(2 * rows, width)


class HalvingSum:
    def __init__(self, kept, sent, axis):
        self.axis, self.value = axis, kept
        steps = bit_steps(axis)
        self.bits = [jnp.reshape(bit, (1,)).astype(jnp.int32) for _, bit in steps]
        self.pairs = [pairs for pairs, _ in steps]
        self.todo = [(True, at) for at in range(len(steps))] + [(False, at) for at in reversed(range(len(steps)))]
        self.begin(sent)

    def begin(self, sent):
        self.sent = sent
        self.got = lax.ppermute(sent, self.axis, self.pairs[self.todo[0][1]])

    def step(self, *after):
        if len(self.todo) == 1:
            return
        halving, at = self.todo.pop(0)
        got = tie(self.got, *after) if after else self.got
        if halving:
            last = at + 1 == len(self.bits)
            made = halve(self.bits[0 if last else at + 1], self.value, got, last)
            self.value = made[0]
            self.begin(made[-1])
        else:
            self.value = join(self.bits[at], self.value, got)
            self.begin(self.value)

    def halves(self, *after):
        while len(self.todo) > 1:
            self.step()
        return self.bits[0], self.value, tie(self.got, *after) if after else self.got


def split_body(tokens, merge_map, counts, ln_gain, w_qkv, qk_gain, w_out, w_up, b_up, w_down, b_down, cotangent):
    images, slots, dim = tokens.shape
    layers, inner = w_out.shape[:2]
    units = w_up.shape[2]
    head_dim = qk_gain.shape[-1]
    heads = inner // head_dim
    rows, lanes = padded_to(slots, 16), padded_to(slots, 128)
    n_narrow = lax.axis_size("narrow")
    size = images // 2
    firsts = (0, size)
    pair = 2 if size % 2 == 0 else 1
    chunk_rows = size * rows
    core_bit = jnp.reshape(lax.axis_index("wide") & 1, (1,)).astype(jnp.int32)
    small_rows = layers * (2 * dim + 2 * head_dim + units) // 128

    def others(value):
        if n_narrow == 2:
            return lax.ppermute(value, "narrow", [(0, 1), (1, 0)])
        wide_value = value.astype(F32)
        return (lax.psum(wide_value, "narrow") - wide_value).astype(BF16)

    row_array = jax.ShapeDtypeStruct((chunk_rows, dim), BF16)
    unit_array = jax.ShapeDtypeStruct((chunk_rows, units), BF16)
    head_flops = 2 * chunk_rows * dim * inner * 4 + 4 * chunk_rows * rows * inner
    feed_flops = 2 * chunk_rows * dim * units * 2
    layer_bytes = 2 * (4 * dim * inner + 2 * dim * units)
    lane_rows = pltpu.VMEM((lanes, dim), BF16)
    proj_rows = pltpu.VMEM((3 * inner, lanes), F32)
    low_rows = pltpu.VMEM((3 * inner, lanes), BF16)
    score_rows = pltpu.VMEM((heads, rows, lanes), F32)
    soft_rows = pltpu.VMEM((heads, lanes, lanes), BF16)
    head_rows = pltpu.VMEM((inner, lanes), BF16)
    row_spec = rows_spec(rows, dim)

    def forward(layer, first, qkv, qkv_layer, turn):
        weights = [
            (merge_map, None),
            (ln_gain, None),
            (qkv, qkv_layer),
            (qk_gain, None),
            (w_out, layer),
            (w_up, layer),
            (b_up, None),
            (w_down, layer),
        ]
        turned = jax.ShapeDtypeStruct((1, 3, inner, dim), BF16)
        return call(
            functools.partial(forward_kernel, layer, first, rows, turn),
            (counts, tokens) + tuple(w for w, _ in weights),
            [image_spec(1, slots, dim, first)] + [layer_spec(w, at) for w, at in weights],
            [row_array] + [turned] * turn,
            [row_spec] + [whole_spec(turned)] * turn,
            [
                pltpu.VMEM((1, rows, dim), F32),
                lane_rows,
                proj_rows,
                low_rows,
                score_rows,
                soft_rows,
                head_rows,
                pltpu.VMEM((2, rows, units // 3), F32),
                pltpu.VMEM((rows, units), BF16),
            ],
            size,
            2 * (head_flops + feed_flops),
            layer_bytes,
        )

    def feed_back(layer, top, first, pieces):
        weights = [(ln_gain, None), (b_down, None), (w_up, layer), (b_up, None), (w_down, layer)]
        outs = [
            row_array if top else jax.ShapeDtypeStruct((chunk_rows, dim), F32),
            row_array,
            row_array,
            row_array,
            unit_array,
            unit_array,
            jax.ShapeDtypeStruct((1, units), F32),
            jax.ShapeDtypeStruct((1, dim), F32),
        ] + [jax.ShapeDtypeStruct((size // pair, dim, pair * rows), BF16)] * 2
        block = rows_spec(pair * rows, dim)
        out_specs = [block] * 4 + [rows_spec(pair * rows, units)] * 2 + [whole_spec(outs[6]), whole_spec(outs[7])]
        out_specs += [image_spec(1, dim, pair * rows)] * 2
        operands = (tokens, pieces[0], pieces[1], cotangent) + tuple(pieces[2:])
        image_block = image_spec(pair, slots, dim, first // pair)
        specs = [image_block, block, block, image_block] + [block] * len(pieces[2:])
        return call(
            functools.partial(feed_kernel, layer, top, first, rows, pair),
            (counts,) + operands + tuple(w for w, _ in weights),
            specs + [layer_spec(w, at) for w, at in weights],
            outs,
            out_specs,
            [pltpu.VMEM((2, rows, dim), F32)] + [pltpu.VMEM((2, pair * rows, units // 3), F32)] * 2,
            size // pair,
            3 * feed_flops,
            layer_bytes + 12 * chunk_rows * dim * 2,
        )

    def heads_back(layer, top, first, turned, normed, low, d_feed, fed, begin=0, count=size):
        weights = [(turned, 0), (qk_gain, None), (w_out, layer)]
        streams = (normed, low, d_feed) + ((fed,) if top else ())
        row_array = jax.ShapeDtypeStruct((count * rows, dim), BF16)
        outs = ([row_array] if top else []) + [
            row_array,
            jax.ShapeDtypeStruct((count * rows, 4 * inner), BF16),
            jax.ShapeDtypeStruct((2 * head_dim, lanes), F32),
            jax.ShapeDtypeStruct((1, dim), F32),
        ]
        out_specs = ([row_spec] if top else []) + [
            row_spec,
            rows_spec(rows, 4 * inner),
            whole_spec(outs[-2]),
            whole_spec(outs[-1]),
        ]
        return call(
            functools.partial(heads_kernel, layer, top, first + begin, rows),
            (merge_map,) + streams + tuple(w for w, _ in weights),
            [whole_spec(merge_map)] + [rows_spec(rows, dim, begin)] * len(streams) + [layer_spec(w, at) for w, at in weights],
            outs,
            out_specs,
            [lane_rows] * 2
            + [proj_rows, low_rows, head_rows, score_rows, score_rows, soft_rows, soft_rows, head_rows]
            + [pltpu.VMEM((2 * inner, lanes), F32), low_rows, pltpu.VMEM((padded_to(heads, 8), lanes), F32), pltpu.VMEM((rows, dim), F32)],
            count,
            6 * head_flops,
            layer_bytes,
            prefetch=0,
        )

    def feed_grads(fed, before=()):
        groups = [[one[at] for one in fed] for at in (8, 9, 5, 4)]
        tile = units // 3
        tiles = units // tile
        flat = [array for group in groups for array in group]
        specs = [whole_spec(one) for one in groups[0] + groups[1]]
        specs += [pl.BlockSpec((chunk_rows, tile), lambda i: (0, jnp.minimum(i, tiles - 1)))] * len(fed)
        specs += [pl.BlockSpec((chunk_rows, tile), lambda i: (0, jnp.maximum(i - tiles, 0)))] * len(fed)
        return call(
            functools.partial(feed_weight_kernel, spans(groups)),
            (*flat, *before),
            specs + [pl.BlockSpec(memory_space=pl.ANY)] * len(before),
            jax.ShapeDtypeStruct((dim, before[0].shape[1] if before else 2 * units), BF16),
            pl.BlockSpec((dim, tile), lambda i: (0, i)),
            [],
            2 * tiles,
            2 * images * rows * dim * units * 2,
            2 * images * rows * (dim + units) * 2,
            prefetch=0,
            aliases={len(flat): 0} if before else None,
        )

    def heads_grads(fed, made, sums=(), wider=0):
        columns = 4 * inner + (128 if sums else 0)
        groups = [[one[at] for one in fed] for at in (8, 9)] + [[one[1] for one in made], [ln_gain]] + list(sums)
        flat = [array for group in groups for array in group]
        specs = [whole_spec(one) for one in groups[0] + groups[1]]
        specs += [pl.BlockSpec((one.shape[0], inner), lambda i, *_: (0, i)) for one in groups[2]]
        specs += [whole_spec(one) for group in groups[3:] for one in group]
        width = columns + wider
        halved = 2 if sums else 1
        return call(
            functools.partial(heads_weight_kernel, spans(groups)),
            (core_bit, *flat),
            specs,
            [jax.ShapeDtypeStruct((dim // halved, width), BF16)] * halved,
            [pl.BlockSpec((dim // halved, columns), lambda i, *_: (0, width // columns - 1))] * halved,
            [pltpu.VMEM((2, dim // 2, inner), BF16), pltpu.VMEM((padded_to(small_rows, 16), 128), F32)] if sums else [],
            4,
            2 * images * rows * dim * inner * 4,
            2 * images * rows * (dim + inner) * 4,
        )

    def unpack(kernel, halves, width, place, shapes, blocks, places, before):
        return call(
            kernel,
            (*halves, *before),
            [pl.BlockSpec((dim // 2, width), lambda i, *_: (0, place))]
            + [pl.BlockSpec((dim // 2, width), lambda i, *_: (halves[2].shape[0] // (dim // 2) - 1, place))]
            + [pl.BlockSpec(memory_space=pl.ANY)] * len(before),
            [jax.ShapeDtypeStruct(shape, F32) for shape in shapes],
            [pl.BlockSpec(block, place_of) for block, place_of in zip(blocks, places)],
            [],
            2,
            dim * width,
            6 * dim * width,
            aliases={at + 3: at for at in range(len(before))},
        )

    def row_half(i, bits):
        return lax.rem(i + bits[0], 2)

    def feed_unpack(halves, layer, before=()):
        return unpack(
            feed_unpack_kernel,
            halves,
            2 * units,
            0,
            ((layers, dim, units), (layers, units, dim)),
            ((1, dim // 2, units), (1, units, dim // 2)),
            (lambda i, bits: (layer, row_half(i, bits), 0), lambda i, bits: (layer, 0, row_half(i, bits))),
            before,
        )

    def heads_unpack(halves, layer, place=0, before=()):
        return unpack(
            heads_unpack_kernel,
            halves,
            halves[1].shape[1] - place * 4 * inner,
            place,
            ((layers, 3, dim, inner), (layers, inner, dim)),
            ((1, 3, dim // 2, inner), (1, inner, dim // 2)),
            (lambda i, bits: (layer, 0, row_half(i, bits), 0), lambda i, bits: (layer, 0, row_half(i, bits))),
            before,
        )

    tokens_slots = jnp.swapaxes(tokens, 0, 1)
    step_slots = 16
    slot_spec = pl.BlockSpec((step_slots, images, dim), lambda i, *_: (i, 0, 0))
    slot_array = jax.ShapeDtypeStruct((slots, images, dim), F32)
    chunk_spec = slots_spec(size, step_slots, dim)
    turned_rows = pltpu.VMEM((step_slots, images, dim), F32)

    def by_image(value):
        return value.reshape(value.shape[0] // rows, rows, dim)

    def paired(ours, theirs):
        return [by_image(one) for two in zip(ours, theirs) for one in two]

    def layer_output(before, ours, theirs, layer):
        return call(
            functools.partial(output_kernel, layer, len(firsts)),
            (counts, before, *paired(ours, theirs), b_down),
            [slot_spec] + [chunk_spec] * (2 * len(firsts)) + [whole_spec(b_down)],
            slot_array,
            slot_spec,
            [turned_rows],
            -(-slots // step_slots),
            10 * images * rows * dim,
            12 * images * rows * dim,
        )

    own_a, turned0 = forward(0, 0, w_qkv, 0, True)
    far_a = others(own_a)
    (own_b,) = forward(0, size, turned0, 0, False)
    far_b = others(own_b)
    turned1 = jnp.swapaxes(tie(w_qkv, own_b)[1:], 2, 3)
    cotangent = tie(cotangent, own_b)
    fed1_a = feed_back(1, True, 0, (own_a, tie(far_a, own_b, turned1)))
    fed1_b = feed_back(1, True, size, (own_b, tie(far_b, fed1_a[0])))
    fed1 = (fed1_a, fed1_b)
    pack_feed1 = feed_grads(fed1)
    part_feed1 = lax.psum_scatter(pack_feed1, "wide", scatter_dimension=0, tiled=True)
    made1_a = heads_back(1, True, 0, turned1, tie(fed1_a[1], pack_feed1), *fed1_a[2:4], fed1_a[0])
    far_grad_a = others(made1_a[1])
    made1_b = heads_back(1, True, size, turned1, tie(fed1_b[1], made1_a[0]), *fed1_b[2:4], fed1_b[0])
    far_grad_b = others(made1_b[1])
    made1 = (made1_a[1:], made1_b[1:])
    (pack_rest,) = heads_grads(fed1, made1, (), 2 * units)
    fed0_a = feed_back(0, False, 0, (own_a, far_a, made1_a[1], tie(far_grad_a, pack_rest)))
    pack_feed1 = lax.all_gather(tie(part_feed1, fed0_a[0], far_grad_b), "wide", axis=0, tiled=True)
    first_out = layer_output(tie(tokens_slots, fed0_a[0]), (own_a, own_b), (far_a, far_b), 0)
    fed0_b = feed_back(0, False, size, (own_b, far_b, made1_b[1], tie(far_grad_b, first_out)))
    fed0 = (fed0_a, fed0_b)
    far_next_a = others(tie(made1_a[0], first_out))
    far_next_b = others(tie(made1_b[0], first_out))
    pack_rest = feed_grads(fed0, (pack_rest,))
    made0, far_last = [], []
    for at in range(2):
        source = fed0[at]
        ready = (pack_rest,) + tuple(one[0] for one in made0)
        made0.append(heads_back(0, False, at * size, turned0, tie(source[1], *ready), *source[2:4], None))
        far_last.append(others(made0[-1][0]))
        if at == 0:
            pack_rest = tie(pack_rest, made0[0][0], far_next_a, far_next_b, pack_feed1)
    part_rest = lax.psum_scatter(pack_rest, "wide", scatter_dimension=0, tiled=True)
    sums = []
    for fed, made in ((fed0, made0), (fed1, made1)):
        sums += [[one[3] for one in made], [one[2] for one in made], [one[7] for one in fed], [one[6] for one in fed]]
    heads0 = HalvingSum(*heads_grads(fed0, made0, sums), "wide")
    heads0.step()
    second_out = layer_output(tie(first_out, heads0.sent), (made1_a[0], made1_b[0]), (far_next_a, far_next_b), 1)
    heads0.step(second_out)
    heads0.step(far_last[0], far_last[1])
    pack_rest = lax.all_gather(tie(part_rest, heads0.sent), "wide", axis=0, tiled=True)
    grad_tokens = call(
        functools.partial(tokens_kernel, len(made0)),
        (
            counts,
            tie(tokens_slots, heads0.sent),
            *paired([one[0] for one in made0], far_last),
            by_image(fed0_a[0]),
            by_image(fed0_b[0]),
            ln_gain,
        ),
        [slot_spec] + [chunk_spec] * (3 * len(made0)) + [whole_spec(ln_gain)],
        slot_array,
        slot_spec,
        [turned_rows] * 2,
        -(-slots // step_slots),
        10 * images * rows * dim,
        12 * images * rows * dim,
    )
    heads0.step(grad_tokens)
    none = jnp.zeros((1,), jnp.int32)
    feed_outs = feed_unpack((none,) + (tie(pack_feed1, heads0.sent),) * 2, 1)
    heads0.step(feed_outs[0])
    while len(heads0.todo) > 1:
        heads0.step()
    rest = (none,) + (tie(pack_rest, heads0.sent),) * 2
    up, down = feed_unpack(rest, 0, feed_outs)
    heads_outs = heads_unpack(rest, 1, 2)
    halves0 = heads0.halves(heads_outs[0], up)
    small = jnp.where(halves0[0][0] == 0, *[half[:small_rows, 4 * inner :] for half in halves0[1:]])
    small = small.astype(F32).reshape(layers, -1)
    narrow_part = small[:, : dim + 2 * head_dim]
    if n_narrow == 2:
        narrow_part = narrow_part + lax.ppermute(narrow_part, "narrow", [(0, 1), (1, 0)])
    else:
        narrow_part = lax.psum(narrow_part, "narrow")
    g_b_down = small[:, dim + 2 * head_dim : 2 * dim + 2 * head_dim]
    g_b_up = small[:, 2 * dim + 2 * head_dim :]
    qkv, out = heads_unpack((halves0[0], tie(halves0[1], g_b_up), halves0[2]), 0, 0, heads_outs)
    return (
        jnp.swapaxes(first_out, 0, 1),
        jnp.swapaxes(second_out, 0, 1),
        jnp.swapaxes(grad_tokens, 0, 1),
        narrow_part[:, :dim],
        qkv,
        narrow_part[:, dim:].reshape(qk_gain.shape),
        out,
        up,
        g_b_up,
        down,
        g_b_down,
    )


def pick_body(*arrays):
    images, dim, inner, units = arrays[0].shape[0], arrays[0].shape[2], arrays[4].shape[-1], arrays[7].shape[-1]
    whole_heads = inner % arrays[5].shape[-1] == 0
    if whole_heads and images % 4 == 0 and units % inner == 0 and dim % 256 == 0 and inner % 128 == 0:
        return split_body(*arrays)
    return body(*arrays)


def solution(mesh):
    placed = (
        P("wide", None, None),
        P("wide", None),
        P("wide"),
        P(),
        P(None, None, None, "narrow"),
        P(),
        P(None, "narrow", None),
        P(None, None, "narrow"),
        P(None, "narrow"),
        P(None, "narrow", None),
        P(),
        P("wide", None, None),
    )
    return jax.shard_map(
        pick_body,
        mesh=mesh,
        in_specs=placed,
        out_specs=(
            P("wide", None, None),
            P("wide", None, None),
            P("wide", None, None),
            P(),
            P(None, None, None, "narrow"),
            P(),
            P(None, "narrow", None),
            P(None, None, "narrow"),
            P(None, "narrow"),
            P(None, "narrow", None),
            P(),
        ),
        check_vma=False,
    )
```

```python
import functools

import jax
import jax.numpy as jnp
from jax import lax
from jax.experimental import pallas as pl
from jax.experimental.pallas import tpu as pltpu
from jax.sharding import PartitionSpec as P


def shifted_2(value, axis, by):
    length = lax.axis_size(axis)
    pairs = [(i, i + by) for i in range(length) if 0 <= i + by < length]
    return lax.ppermute(value, axis, pairs)


def norm_rows(inputs, gain_row):
    centre = jnp.mean(inputs, axis=-1, keepdims=True)
    centered = inputs - centre
    inverse = lax.rsqrt(jnp.mean(centered * centered, axis=-1, keepdims=True) + 1e-06)
    normal = centered * inverse
    return (normal, inverse, normal * gain_row)


def norm_back(upstream, normal, inverse, gain_row):
    scaled = upstream * gain_row
    return inverse * (
        scaled
        - jnp.mean(scaled, axis=-1, keepdims=True)
        - normal * jnp.mean(scaled * normal, axis=-1, keepdims=True)
    )


def attend(normed_low, key_bias, qkv_full, out_full, qk_gains):
    head_dim = qk_gains.shape[-1]
    head_count = qkv_full.shape[-1] // head_dim
    qkv_heads = qkv_full.reshape(3, qkv_full.shape[1], head_count, head_dim)
    projected = jnp.einsum(
        "bsd,kdhe->kbhse", normed_low, qkv_heads, preferred_element_type=jnp.float32
    )
    q_normal, q_inverse, queries = norm_rows(projected[0], qk_gains[0])
    k_normal, k_inverse, keys_normed = norm_rows(projected[1], qk_gains[1])
    queries_low = queries.astype(jnp.bfloat16)
    keys_low = keys_normed.astype(jnp.bfloat16)
    values_low = projected[2].astype(jnp.bfloat16)
    score_scale = head_dim ** (-0.5)
    scores = jnp.einsum(
        "bhse,bhte->bhst", queries_low, keys_low, preferred_element_type=jnp.float32
    )
    logits = scores * score_scale + key_bias[:, None, None, :]
    shifted = jnp.exp(logits - jnp.max(logits, axis=-1, keepdims=True))
    softened = shifted / jnp.sum(shifted, axis=-1, keepdims=True)
    soft_low = softened.astype(jnp.bfloat16)
    mixed_low = jnp.einsum(
        "bhst,bhte->bhse", soft_low, values_low, preferred_element_type=jnp.float32
    ).astype(jnp.bfloat16)
    out_heads = out_full.reshape(head_count, head_dim, out_full.shape[-1])
    branch = jnp.einsum("bhse,hed->bsd", mixed_low, out_heads, preferred_element_type=jnp.float32)
    kept_parts = (
        q_normal,
        q_inverse,
        k_normal,
        k_inverse,
        queries_low,
        keys_low,
        values_low,
        softened,
        soft_low,
        mixed_low,
        qkv_heads,
        out_heads,
        score_scale,
    )
    return (branch, kept_parts)


def attend_back(normed_low, key_bias, qkv_full, out_full, qk_gains, grad_low):
    branch, kept_parts = attend(normed_low, key_bias, qkv_full, out_full, qk_gains)
    (
        q_normal,
        q_inverse,
        k_normal,
        k_inverse,
        queries_low,
        keys_low,
        values_low,
        softened,
        soft_low,
        mixed_low,
        qkv_heads,
        out_heads,
        score_scale,
    ) = kept_parts
    d_mixed = jnp.einsum(
        "bsd,hed->bhse", grad_low, out_heads, preferred_element_type=jnp.float32
    ).astype(jnp.bfloat16)
    g_out = jnp.einsum(
        "bhse,bsd->hed", mixed_low, grad_low, preferred_element_type=jnp.float32
    ).reshape(out_full.shape)
    d_soft = jnp.einsum("bhse,bhte->bhst", d_mixed, values_low, preferred_element_type=jnp.float32)
    row_dot = jnp.sum(softened * d_soft, axis=-1, keepdims=True)
    d_scores = (softened * (d_soft - row_dot) * score_scale).astype(jnp.bfloat16)
    d_queries = jnp.einsum(
        "bhst,bhte->bhse", d_scores, keys_low, preferred_element_type=jnp.float32
    )
    d_keys = jnp.einsum(
        "bhst,bhse->bhte", d_scores, queries_low, preferred_element_type=jnp.float32
    )
    d_values = jnp.einsum("bhst,bhse->bhte", soft_low, d_mixed, preferred_element_type=jnp.float32)
    g_gains = jnp.stack(
        [jnp.sum(d_queries * q_normal, axis=(0, 1, 2)), jnp.sum(d_keys * k_normal, axis=(0, 1, 2))]
    )
    d_projected = jnp.stack(
        [
            norm_back(d_queries, q_normal, q_inverse, qk_gains[0]),
            norm_back(d_keys, k_normal, k_inverse, qk_gains[1]),
            d_values,
        ]
    ).astype(jnp.bfloat16)
    g_qkv = jnp.einsum(
        "bsd,kbhse->kdhe", normed_low, d_projected, preferred_element_type=jnp.float32
    ).reshape(qkv_full.shape)
    d_normed = jnp.einsum(
        "kbhse,kdhe->bsd", d_projected, qkv_heads, preferred_element_type=jnp.float32
    )
    return (d_normed, g_qkv, g_out, g_gains)


def expand(normed_low, up_full, bias_full, down_full):
    pre_act = jnp.einsum(
        "bsd,df->bsf", normed_low, up_full, preferred_element_type=jnp.float32
    ) + bias_full.astype(jnp.float32)
    hidden, gelu_back = jax.vjp(jax.nn.gelu, pre_act)
    hidden_low = hidden.astype(jnp.bfloat16)
    branch = jnp.einsum("bsf,fd->bsd", hidden_low, down_full, preferred_element_type=jnp.float32)
    return (branch, hidden_low, gelu_back)


def expand_back(normed_low, up_full, bias_full, down_full, grad_low):
    branch, hidden_low, gelu_back = expand(normed_low, up_full, bias_full, down_full)
    d_hidden = jnp.einsum("bsd,fd->bsf", grad_low, down_full, preferred_element_type=jnp.float32)
    d_pre = gelu_back(d_hidden)[0].astype(jnp.bfloat16)
    g_bias = jnp.sum(d_pre, axis=(0, 1), dtype=jnp.float32)
    g_up = jnp.einsum("bsd,bsf->df", normed_low, d_pre, preferred_element_type=jnp.float32)
    g_down = jnp.einsum("bsf,bsd->fd", hidden_low, grad_low, preferred_element_type=jnp.float32)
    d_normed = jnp.einsum("bsf,df->bsd", d_pre, up_full, preferred_element_type=jnp.float32)
    return (d_normed, g_up, g_bias, g_down)


def body(
    tokens, merge_map, counts, ln_gain, w_qkv, qk_gain, w_out, w_up, b_up, w_down, b_down, cotangent
):
    pair_gap = lax.axis_size("narrow") // 2
    on_attention = lax.axis_index("narrow") < pair_gap
    layers = ln_gain.shape[0]
    col_half = w_qkv.shape[-1]
    unit_half = w_up.shape[-1]
    model_dim = tokens.shape[-1]
    slot_ids = jnp.arange(tokens.shape[1], dtype=jnp.int32)
    live_rows = slot_ids[None, :] < counts[:, None]
    row_weight = jnp.where(live_rows, 1.0, 0.0).astype(jnp.float32)[:, :, None]
    merged_sizes = jnp.sum(
        jnp.where(merge_map[:, :, None] == slot_ids[None, None, :], 1.0, 0.0), axis=1
    ).astype(jnp.float32)
    key_bias = jnp.where(live_rows, jnp.log(jnp.where(live_rows, merged_sizes, 1.0)), -1e30)
    attn_far = shifted_2((w_qkv, w_out), "narrow", -pair_gap)
    mlp_far = shifted_2((w_up, b_up, w_down), "narrow", pair_gap)

    def attention_weights(layer_at):
        qkv_full = jnp.concatenate([w_qkv[layer_at], attn_far[0][layer_at]], axis=-1)
        out_full = jnp.concatenate([w_out[layer_at], attn_far[1][layer_at]], axis=0)
        return (qkv_full, out_full)

    def feed_weights(layer_at):
        up_full = jnp.concatenate([mlp_far[0][layer_at], w_up[layer_at]], axis=-1)
        bias_full = jnp.concatenate([mlp_far[1][layer_at], b_up[layer_at]], axis=-1)
        down_full = jnp.concatenate([mlp_far[2][layer_at], w_down[layer_at]], axis=0)
        return (up_full, bias_full, down_full)

    current = tokens.astype(jnp.float32)
    layer_inputs = []
    outputs = []
    for layer_at in range(layers):
        normal, inverse, normed = norm_rows(current, ln_gain[layer_at])
        normed_low = normed.astype(jnp.bfloat16)

        def attention_forward():
            qkv_full, out_full = attention_weights(layer_at)
            return attend(normed_low, key_bias, qkv_full, out_full, qk_gain[layer_at])[0]

        def feed_forward():
            up_full, bias_full, down_full = feed_weights(layer_at)
            return expand(normed_low, up_full, bias_full, down_full)[0]

        partial_value = lax.cond(on_attention, attention_forward, feed_forward)
        layer_inputs.append(current)
        branch_total = lax.psum(partial_value, "narrow")
        current = row_weight * (current + branch_total + b_down[layer_at])
        outputs.append(current)
    grad_rows = cotangent.astype(jnp.float32)
    collected = []
    for layer_at in reversed(range(layers)):
        normal, inverse, normed = norm_rows(layer_inputs[layer_at], ln_gain[layer_at])
        normed_low = normed.astype(jnp.bfloat16)
        masked_grad = row_weight * grad_rows
        grad_low = masked_grad.astype(jnp.bfloat16)

        def attention_side():
            qkv_full, out_full = attention_weights(layer_at)
            d_normed, g_qkv, g_out, g_gains = attend_back(
                normed_low, key_bias, qkv_full, out_full, qk_gain[layer_at], grad_low
            )
            return (
                d_normed,
                g_gains,
                g_qkv,
                g_out,
                jnp.zeros((model_dim, 2 * unit_half), jnp.float32),
                jnp.zeros((2 * unit_half,), jnp.float32),
                jnp.zeros((2 * unit_half, model_dim), jnp.float32),
            )

        def feed_side():
            up_full, bias_full, down_full = feed_weights(layer_at)
            d_normed, g_up, g_bias, g_down = expand_back(
                normed_low, up_full, bias_full, down_full, grad_low
            )
            return (
                d_normed,
                jnp.zeros(qk_gain[layer_at].shape, jnp.float32),
                jnp.zeros((3, model_dim, 2 * col_half), jnp.float32),
                jnp.zeros((2 * col_half, model_dim), jnp.float32),
                g_up,
                g_bias,
                g_down,
            )

        returned = lax.cond(on_attention, attention_side, feed_side)
        d_normed, g_gains = (
            lax.psum(returned[0].astype(jnp.bfloat16), "narrow").astype(jnp.float32),
            lax.psum(returned[1].astype(jnp.bfloat16), "narrow").astype(jnp.float32),
        )
        g_ln = jnp.sum(d_normed * normal, axis=(0, 1))
        grad_rows = masked_grad + norm_back(d_normed, normal, inverse, ln_gain[layer_at])
        qkv_far, out_far = (
            shifted_2(returned[2][..., col_half:].astype(jnp.bfloat16), "narrow", pair_gap).astype(
                jnp.float32
            ),
            shifted_2(returned[3][col_half:].astype(jnp.bfloat16), "narrow", pair_gap).astype(
                jnp.float32
            ),
        )
        up_far, bias_far, down_far = (
            shifted_2(returned[4][:, :unit_half].astype(jnp.bfloat16), "narrow", -pair_gap).astype(
                jnp.float32
            ),
            shifted_2(returned[5][:unit_half].astype(jnp.bfloat16), "narrow", -pair_gap).astype(
                jnp.float32
            ),
            shifted_2(returned[6][:unit_half].astype(jnp.bfloat16), "narrow", -pair_gap).astype(
                jnp.float32
            ),
        )
        own_qkv = jnp.where(on_attention, returned[2][..., :col_half], qkv_far)
        own_out = jnp.where(on_attention, returned[3][:col_half], out_far)
        own_up = jnp.where(on_attention, up_far, returned[4][:, unit_half:])
        own_bias = jnp.where(on_attention, bias_far, returned[5][unit_half:])
        own_down = jnp.where(on_attention, down_far, returned[6][unit_half:])
        g_bdown = jnp.sum(masked_grad, axis=(0, 1))
        shards = (own_qkv, own_out, own_up, own_bias, own_down, g_ln, g_gains, g_bdown)
        collected.append(shards)
    collected = collected[::-1]
    stacked = tuple(
        (jnp.stack([element[position] for element in collected]) for position in range(8))
    )
    stacked = (
        lax.psum(stacked[0].astype(jnp.bfloat16), "wide").astype(jnp.float32),
        lax.psum(stacked[1].astype(jnp.bfloat16), "wide").astype(jnp.float32),
        lax.psum(stacked[2].astype(jnp.bfloat16), "wide").astype(jnp.float32),
        lax.psum(stacked[3].astype(jnp.bfloat16), "wide").astype(jnp.float32),
        lax.psum(stacked[4].astype(jnp.bfloat16), "wide").astype(jnp.float32),
        lax.psum(stacked[5].astype(jnp.bfloat16), "wide").astype(jnp.float32),
        lax.psum(stacked[6].astype(jnp.bfloat16), "wide").astype(jnp.float32),
        lax.psum(stacked[7].astype(jnp.bfloat16), "wide").astype(jnp.float32),
    )
    return (
        outputs[0],
        outputs[-1],
        grad_rows,
        stacked[5],
        stacked[0],
        stacked[6],
        stacked[1],
        stacked[2],
        stacked[3],
        stacked[4],
        stacked[7],
    )


EPS = 1e-06
F32 = jnp.float32
BF16 = jnp.bfloat16
COST_SCALE = 3
AG_AFTER = 1
VMEM_BYTES = 60 * 1024 * 1024
GELU_IN = 0.7978845608028654
GELU_CUBE = 0.044715


def padded_to(length, step):
    return -(-length // step) * step


def dot(a, b):
    return jnp.dot(a, b, preferred_element_type=F32)


def dot_nt(a, b):
    return lax.dot_general(a, b, (((1,), (1,)), ((), ())), preferred_element_type=F32)


def normal_rows(x):
    centered = x - jnp.mean(x, axis=-1, keepdims=True)
    inverse = lax.rsqrt(jnp.mean(centered * centered, axis=-1, keepdims=True) + EPS)
    return centered * inverse, inverse


def back_rows(upstream, normal, inverse, gain):
    scaled = upstream * gain
    return inverse * (
        scaled
        - jnp.mean(scaled, axis=-1, keepdims=True)
        - normal * jnp.mean(scaled * normal, axis=-1, keepdims=True)
    )


def live_of(count, rows):
    return lax.broadcasted_iota(jnp.int32, (rows, 1), 0) < count


def fill_rows(source, wide_rows):
    slots = source.shape[0]
    edge = slots // 8 * 8
    wide_rows[edge:, :] = jnp.zeros((wide_rows.shape[0] - edge, wide_rows.shape[1]), F32)
    wide_rows[:slots, :] = source[...].astype(F32)


def head_norm(x):
    centered = x - jnp.mean(x, axis=1, keepdims=True)
    inverse = lax.rsqrt(jnp.mean(centered * centered, axis=1, keepdims=True) + EPS)
    return centered * inverse, inverse


def head_back(upstream, normal, inverse, gain):
    scaled = upstream * gain
    return inverse * (
        scaled
        - jnp.mean(scaled, axis=1, keepdims=True)
        - normal * jnp.mean(scaled * normal, axis=1, keepdims=True)
    )


def key_sizes(patch_ref, image, rows):
    slots = patch_ref.shape[1]
    slot = lax.broadcasted_iota(jnp.int32, (rows, slots), 0)
    named = jnp.where(patch_ref[pl.ds(image, 1), :] == slot, 1.0, 0.0)
    return jnp.sum(named, axis=-1, keepdims=True)


def head_gains(qk_gain, layer):
    both = qk_gain[layer]
    return [jnp.broadcast_to(both[at : at + 1, :], (8, both.shape[1])).T[:, :1] for at in range(2)]


def project(turned, normed, gains, proj, lows):
    inner, head_dim = proj.shape[0] // 3, gains[0].shape[0]
    heads, lanes = inner // head_dim, proj.shape[1]
    proj[...] = dot_nt(turned, normed)
    inverses = []
    for part in range(2):
        here = slice(part * inner, (part + 1) * inner)
        normal, inverse = head_norm(proj[here, :].reshape(heads, head_dim, lanes))
        inverses.append(inverse)
        proj[here, :] = normal.reshape(inner, lanes)
        low = (normal * gains[part][None]).astype(BF16)
        if part == 0:
            low = (low.astype(F32) * head_dim ** (-0.5)).astype(BF16)
        lows[here, :] = low.reshape(inner, lanes)
    lows[2 * inner :, :] = proj[2 * inner :, :].astype(BF16)
    return inverses


def soften(lows, sizes, scores, soft):
    heads, rows, strip = scores.shape[0], scores.shape[1], 16
    inner = lows.shape[0] // 3
    head_dim = inner // heads
    for head in range(heads):
        at = head * head_dim
        keys = lows[inner + at : inner + at + head_dim, :]
        scores[head] = dot(keys.T[:rows], lows[at : at + head_dim, :])
    over = []
    for head in range(heads):
        total = jnp.zeros((8, scores.shape[2]), F32)
        for at in range(0, rows, strip):
            raised = jnp.exp(scores[head, at : at + strip, :]) * sizes[at : at + strip, :]
            scores[head, at : at + strip, :] = raised
            soft[head, at : at + strip, :] = raised.astype(BF16)
            total = total + (raised[:8] + raised[8:])
        over.append(1.0 / jnp.sum(total, axis=0, keepdims=True))
    return over


def forward_kernel(layer, first, rows, turn, counts, *refs):
    tok, patch, gain, w_qkv, qk_gain, w_out, w_up, b_up, w_down, out = refs[:10]
    if turn:
        turned = refs[10]
        refs = refs[11:]
    else:
        turned = w_qkv
        refs = refs[10:]
    wide_rows, normed, proj, lows, scores, soft, mixed, pre_rows, hidden = refs
    step = pl.program_id(0)
    inner = w_out.shape[1]

    @pl.when(step == 0)
    def _():
        normed[...] = jnp.zeros(normed.shape, BF16)
        soft[...] = jnp.zeros(soft.shape, BF16)
        if turn:
            for at in range(w_qkv.shape[0]):
                for part in range(3):
                    turned[at, part] = w_qkv[at, part].T

    fill_rows(tok.at[0], wide_rows.at[0])
    strip = 16
    for at in range(0, rows, strip):
        x = jnp.where(live_of(counts[first + step] - at, strip), wide_rows[0, at : at + strip, :], 0.0)
        normed[at : at + strip, :] = (normal_rows(x)[0] * gain[layer : layer + 1, :]).astype(BF16)
    gains = head_gains(qk_gain, layer)
    head_dim = gains[0].shape[0]
    project(turned[0].reshape(3 * inner, turned.shape[3]), normed[...], gains, proj, lows)
    over = soften(lows, key_sizes(patch, first + step, rows), scores, soft)
    for head in range(inner // head_dim):
        at = head * head_dim
        values = lows[2 * inner + at : 2 * inner + at + head_dim, :]
        mixed[at : at + head_dim, :] = (dot(values, soft[head]) * over[head]).astype(BF16)
    bias = b_up[...].astype(F32)[layer : layer + 1, :]
    units = w_up.shape[2]
    tile = units // 3
    for slot, at in enumerate(range(0, units, tile)):
        pre_rows[slot % 2] = dot(normed[:rows, :], w_up[0, :, at : at + tile])
        for row in range(0, rows, strip):
            pre = pre_rows[slot % 2, row : row + strip, :] + bias[:, at : at + tile]
            bent = jnp.tanh(pre * (GELU_IN + (GELU_IN * GELU_CUBE) * (pre * pre)))
            hidden[row : row + strip, at : at + tile] = (pre * (0.5 + 0.5 * bent)).astype(BF16)
    out[...] = (dot(mixed[...].T[:rows], w_out[0]) + dot(hidden[...], w_down[0])).astype(BF16)


def feed_kernel(layer, top, first, rows, per_step, tok_images, counts, *refs):
    refs = list(refs)
    tok, cot = refs[:2]
    steps = (tok_images + per_step - 1) // per_step
    own_pieces, far_pieces = refs[2 : 2 + steps], refs[2 + steps : 2 + 2 * steps]
    refs = refs[2 + 2 * steps :]
    if not top:
        own_grad, far_grad = refs[:2]
        refs = refs[2:]
    gain, b_prev, w_up, b_up, w_down = refs[:5]
    refs = refs[5:]
    extra = refs[0]
    refs = refs[1:]
    normed, low, d_feed, hidden_out, d_pre_out, sum_up, sum_down, normed_t, low_t, wide_rows, pre_rows, d_rows, own, far = refs
    step = pl.program_id(0)
    for at in range(steps):

        @pl.when(step == at)
        def _(at=at):
            own[...] = own_pieces[at][...]
            far[...] = far_pieces[at][...]


    @pl.when(step == 0)
    def _():
        sum_up[...] = jnp.zeros(sum_up.shape, F32)
        sum_down[...] = jnp.zeros(sum_down.shape, F32)

    strip = 16
    for j in range(per_step):
        count = counts[first + step * per_step + j]
        fill_rows(tok.at[j], wide_rows.at[0])
        fill_rows(cot.at[j], wide_rows.at[1])
        total = jnp.zeros((8, tok.shape[2]), F32)
        for at in range(0, rows, strip):
            block = slice(j * rows + at, j * rows + at + strip)
            live = live_of(count - at, strip)
            x0 = jnp.where(live, wide_rows[0, at : at + strip, :], 0.0)
            branch = own[block, :].astype(F32) + far[block, :].astype(F32)
            x1 = jnp.where(live, x0 + branch + b_prev[:1, :], 0.0)
            grad = jnp.where(live, wide_rows[1, at : at + strip, :], 0.0)
            if top:
                x = x1
            else:
                x = x0
                normal, inverse = normal_rows(x1)
                d_normed = own_grad[block, :].astype(F32) + far_grad[block, :].astype(F32)
                grad = grad + back_rows(d_normed, normal, inverse, gain[layer + 1 : layer + 2, :])
                extra[block, :] = grad
            normed[block, :] = (normal_rows(x)[0] * gain[layer : layer + 1, :]).astype(BF16)
            low[block, :] = grad.astype(BF16)
            total = total + (grad[:8] + grad[8:])
        sum_down[...] += jnp.sum(total, axis=0, keepdims=True)
    normed_t[0] = normed[...].T
    low_t[0] = low[...].T
    bias = b_up[...].astype(F32)[layer : layer + 1, :]
    units = w_up.shape[2]
    tile = units // 3
    for slot, at in enumerate(range(0, units, tile)):
        part = slice(at, at + tile)
        pre_rows[slot % 2] = dot(normed[...], w_up[0, :, part])
        d_rows[slot % 2] = dot_nt(low[...], w_down[0, part, :])
        total = jnp.zeros((8, tile), F32)
        for row in range(0, per_step * rows, strip):
            block = slice(row, row + strip)
            pre = pre_rows[slot % 2, block, :] + bias[:, part]
            square = pre * pre
            bent = jnp.tanh(pre * (GELU_IN + (GELU_IN * GELU_CUBE) * square))
            half = 0.5 + 0.5 * bent
            hidden_out[block, part] = (pre * half).astype(BF16)
            steep = GELU_IN + (3 * GELU_IN * GELU_CUBE) * square
            slope = half + (0.5 * pre) * ((1.0 - bent * bent) * steep)
            d_pre = (d_rows[slot % 2, block, :] * slope).astype(BF16)
            d_pre_out[block, part] = d_pre
            d_pre = d_pre.astype(F32)
            total = total + (d_pre[:8] + d_pre[8:])
        sum_up[:, part] += jnp.sum(total, axis=0, keepdims=True)
    d_feed[...] = dot_nt(d_pre_out[...], w_up[0]).astype(BF16)
    if top:
        extra[...] = dot(hidden_out[...], w_down[0]).astype(BF16)


def heads_kernel(layer, top, first, rows, patch, normed_in, low_in, d_feed, *refs):
    refs = list(refs)
    if top:
        fed = refs[0]
        refs = refs[1:]
    w_qkv, qk_gain, w_out = refs[:3]
    refs = refs[3:]
    if top:
        out = refs[0]
        refs = refs[1:]
    d_normed, rights, sum_gain, sum_row = refs[:4]
    normed, low, proj, lows, d_mixed, scores, slopes, soft, d_soft, mixed, d_heads, d_proj, row_dots, total = refs[4:]
    step = pl.program_id(0)
    inner = w_out.shape[1]
    gains = head_gains(qk_gain, layer)
    head_dim = gains[0].shape[0]

    @pl.when(step == 0)
    def _():
        normed[...] = jnp.zeros(normed.shape, BF16)
        low[...] = jnp.zeros(low.shape, BF16)
        soft[...] = jnp.zeros(soft.shape, BF16)
        d_soft[...] = jnp.zeros(d_soft.shape, BF16)
        sum_gain[...] = jnp.zeros(sum_gain.shape, F32)
        sum_row[...] = jnp.zeros(sum_row.shape, F32)

    normed[:rows, :] = normed_in[...]
    low[:rows, :] = low_in[...]
    turned = w_qkv[0].reshape(3 * inner, w_qkv.shape[3])
    heads, lanes = inner // head_dim, proj.shape[1]
    inverses = project(turned, normed[...], gains, proj, lows)
    d_mixed[...] = dot_nt(w_out[0], low[...]).astype(BF16)
    over = soften(lows, key_sizes(patch, first + step, rows), scores, soft)
    for head in range(heads):
        here = slice(head * head_dim, (head + 1) * head_dim)
        mixed_here = dot(lows[2 * inner + here.start : 2 * inner + here.stop, :], soft[head]) * over[head]
        mixed[here, :] = mixed_here.astype(BF16)
        d_mixed_here = d_mixed[here, :].astype(F32)
        row_dots[head : head + 1, :] = jnp.sum(d_mixed_here * mixed_here, axis=0, keepdims=True) * over[head]
        d_mixed[here, :] = (d_mixed_here * over[head]).astype(BF16)
    for head in range(heads):
        here = slice(head * head_dim, (head + 1) * head_dim)
        values = lows[2 * inner + here.start : 2 * inner + here.stop, :]
        slopes[head] = dot(values.T[:rows], d_mixed[here, :])
    for head in range(heads):
        for row in range(0, rows, 16):
            block = slice(row, row + 16)
            slope = slopes[head, block, :] - row_dots[head : head + 1, :]
            d_soft[head, block, :] = (scores[head, block, :] * slope).astype(BF16)
    for head in range(heads):
        here = slice(head * head_dim, (head + 1) * head_dim)
        keys = slice(inner + here.start, inner + here.stop)
        values = slice(2 * inner + here.start, 2 * inner + here.stop)
        d_heads[here, :] = dot(lows[keys, :], d_soft[head]) * head_dim ** (-0.5)
        d_heads[keys, :] = dot_nt(lows[here, :], d_soft[head])
        d_proj[values, :] = dot_nt(d_mixed[here, :], soft[head]).astype(BF16)
    for part in range(2):
        here = slice(part * inner, (part + 1) * inner)
        normal = proj[here, :].reshape(heads, head_dim, lanes)
        upstream = d_heads[here, :].reshape(heads, head_dim, lanes)
        sum_gain[part * head_dim : (part + 1) * head_dim, :] += jnp.sum(upstream * normal, axis=0)
        back = head_back(upstream, normal, inverses[part], gains[part][None])
        d_proj[here, :] = back.reshape(inner, lanes).astype(BF16)
    mixed_rows = mixed[...].T[:rows]
    rights[:, 3 * inner :] = mixed_rows
    if top:
        out[...] = (fed[...].astype(F32) + dot(mixed_rows, w_out[0])).astype(BF16)
    for part in range(3):
        rights[:, part * inner : (part + 1) * inner] = d_proj[part * inner : (part + 1) * inner, :].T[:rows]
    total[...] = dot(rights[:, : 3 * inner], turned)
    row_sum = jnp.zeros((8, total.shape[1]), F32)
    for row in range(0, rows, 16):
        block = slice(row, row + 16)
        d_here = total[block, :] + d_feed[block, :].astype(F32)
        d_normed[block, :] = d_here.astype(BF16)
        d_here = d_here * normed_in[block, :].astype(F32)
        row_sum = row_sum + (d_here[:8] + d_here[8:])
    sum_row[...] += jnp.sum(row_sum, axis=0, keepdims=True)


def live_slots(counts, shape):
    slot = lax.broadcasted_iota(jnp.int32, shape, 0) + pl.program_id(0) * shape[0]
    image = lax.broadcasted_iota(jnp.int32, shape, 1)
    count = jnp.zeros(shape, jnp.int32)
    for at in range(shape[1]):
        count = jnp.where(image == at, counts[at], count)
    return slot < count


def chunk_sums(refs, sums):
    image = 0
    for own, far in refs:
        for at in range(own.shape[0]):
            sums[:, image, :] = own[at].astype(F32) + far[at].astype(F32)
            image += 1


def output_kernel(layer, chunks, counts, before, *refs):
    pairs = [(refs[2 * at], refs[2 * at + 1]) for at in range(chunks)]
    bias, out, sums = refs[2 * chunks :]
    live = live_slots(counts, out.shape[:2] + (1,))
    chunk_sums(pairs, sums)
    for at in range(0, out.shape[0], 2):
        part = slice(at, at + 2)
        total = before[part].astype(F32) + sums[part] + bias[layer : layer + 1, :]
        out[part] = jnp.where(live[part], total, 0.0)


def tokens_kernel(chunks, counts, tok, *refs):
    pairs = [(refs[2 * at], refs[2 * at + 1]) for at in range(chunks)]
    grads = refs[2 * chunks : -4]
    gain, out, sums, turned = refs[-4:]
    live = live_slots(counts, out.shape[:2] + (1,))
    chunk_sums(pairs, sums)
    image = 0
    for grad in grads:
        for at in range(grad.shape[0]):
            turned[:, image, :] = grad[at]
            image += 1
    for at in range(0, out.shape[0], 2):
        part = slice(at, at + 2)
        normal, inverse = normal_rows(jnp.where(live[part], tok[part].astype(F32), 0.0))
        total = turned[part] + back_rows(sums[part], normal, inverse, gain[:1, :])
        out[part] = jnp.where(live[part], total, 0.0)


def weight_tile(lefts, rights):
    total, first, at = None, 0, 0
    for left in lefts:
        for block in range(left.shape[0]):
            rows = left.shape[2]
            if first == rights[at].shape[0]:
                first, at = 0, at + 1
            term = dot(left[block], rights[at][first : first + rows, :])
            total = term if total is None else total + term
            first += rows
    return total.astype(BF16)


def store_tile(bit, tile, both, kept, sent, columns=slice(None)):
    if sent is None:
        kept[:, columns] = tile
        return
    both[:, :, : tile.shape[1]] = tile.reshape(2, -1, tile.shape[1])
    kept[:, columns] = both[bit, :, : tile.shape[1]]
    sent[:, columns] = both[1 - bit, :, : tile.shape[1]]


def feed_weight_kernel(counts, *refs):
    normed_t, low_t, d_pre, hidden = [refs[first:last] for first, last in counts]
    out = refs[-1]
    half = pl.num_programs(0) // 2

    @pl.when(pl.program_id(0) < half)
    def _():
        out[...] = weight_tile(normed_t, d_pre)

    @pl.when(pl.program_id(0) >= half)
    def _():
        out[...] = weight_tile(low_t, hidden)


def heads_weight_kernel(counts, bits, *refs):
    normed_t, low_t, rights, gain, *sums = [refs[first:last] for first, last in counts]
    if sums:
        kept, sent, both, lined = refs[-4:]
    else:
        kept, sent, both = refs[-3:]
    inner = rights[0].shape[1]
    for part in range(4):

        @pl.when(pl.program_id(0) == part)
        def _(part=part):
            lefts = low_t if part == 3 else normed_t
            columns = slice(part * inner, (part + 1) * inner)
            store_tile(bits[0], weight_tile(lefts, rights), both, kept, sent, columns)

    if not sums:
        return

    @pl.when(pl.program_id(0) == 0)
    def _():
        lined[...] = jnp.zeros(lined.shape, F32)
        row = 0
        for layer in range(len(sums) // 4):
            s_row, s_gain, s_down, s_up = [
                functools.reduce(lambda a, b: a + b, [one[...] for one in group])
                for group in sums[4 * layer : 4 * layer + 4]
            ]
            s_row = s_row / gain[0][layer : layer + 1, :]
            s_gain = jnp.sum(s_gain.T, axis=0, keepdims=True)
            for values in (s_row, s_gain, s_down, s_up):
                for at in range(0, values.shape[1], 128):
                    lined[row : row + 1, :] = values[:, at : at + 128]
                    row += 1
        none = jnp.zeros((kept.shape[0], 128), BF16)
        kept[:, 4 * inner :] = none
        sent[:, 4 * inner :] = none
        small = lined[...].astype(BF16)

        @pl.when(bits[0] == 0)
        def _():
            kept[: lined.shape[0], 4 * inner :] = small

        @pl.when(bits[0] == 1)
        def _():
            sent[: lined.shape[0], 4 * inner :] = small


def halve_kernel(bits, kept, got, *refs):
    total = (kept[...].astype(F32) + got[...].astype(F32)).astype(BF16)
    if len(refs) == 1:
        refs[0][...] = total
        return
    left, sent, both = refs
    both[...] = total.reshape(both.shape)
    left[...] = both[bits[0]]
    sent[...] = both[1 - bits[0]]


def join_kernel(bits, own, got, out):
    out[bits[0]] = own[...]
    out[1 - bits[0]] = got[...]


def feed_unpack_kernel(bits, own, got, *refs):
    up, down = refs[-2:]
    units = up.shape[2]

    def place(pack):
        up[0] = pack[:, :units].astype(F32)
        down[0] = pack[:, units : 2 * units].astype(F32).T

    pl.when(pl.program_id(0) == 0)(lambda: place(own))
    pl.when(pl.program_id(0) == 1)(lambda: place(got))


def heads_unpack_kernel(bits, own, got, *refs):
    qkv, out = refs[-2:]
    inner = qkv.shape[3]

    def place(pack):
        for at in range(3):
            qkv[0, at] = pack[:, at * inner : (at + 1) * inner].astype(F32)
        out[0] = pack[:, 3 * inner : 4 * inner].astype(F32).T

    pl.when(pl.program_id(0) == 0)(lambda: place(own))
    pl.when(pl.program_id(0) == 1)(lambda: place(got))


def spans(groups):
    ends = []
    for group in groups:
        first = ends[-1][1] if ends else 0
        ends.append((first, first + len(group)))
    return tuple(ends)


def whole_spec(array):
    return pl.BlockSpec(array.shape, lambda i, *_: (0,) * array.ndim)


def layer_spec(array, layer):
    if layer is None:
        return whole_spec(array)
    return pl.BlockSpec((1,) + array.shape[1:], lambda i, *_: (layer,) + (0,) * (array.ndim - 1))


def rows_spec(rows, columns, first=0):
    return pl.BlockSpec((rows, columns), lambda i, *_: (first + i, 0))


def image_spec(images, slots, columns, first=0):
    return pl.BlockSpec((images, slots, columns), lambda i, *_: (first + i, 0, 0))


def slots_spec(images, slots, columns):
    return pl.BlockSpec((images, slots, columns), lambda i, *_: (0, i, 0))


def call(kernel, operands, specs, shapes, out_specs, scratch, grid, flops, moved, prefetch=1, aliases=None):
    return pl.pallas_call(
        kernel,
        grid_spec=pltpu.PrefetchScalarGridSpec(
            num_scalar_prefetch=prefetch,
            grid=(grid,),
            in_specs=specs,
            out_specs=out_specs,
            scratch_shapes=scratch,
        ),
        out_shape=shapes,
        compiler_params=pltpu.CompilerParams(
            dimension_semantics=("arbitrary",), vmem_limit_bytes=VMEM_BYTES
        ),
        cost_estimate=pl.CostEstimate(flops=flops // COST_SCALE, bytes_accessed=moved // COST_SCALE, transcendentals=0),
        input_output_aliases=aliases or {},
    )(*operands)


def bit_steps(axis):
    size = lax.axis_size(axis)
    bits = size.bit_length() - 1
    here = lax.axis_index(axis)
    steps = []
    for step in range(bits):

        def bit_of(place, step=step):
            if bits < 3 or step not in (1, 2):
                return 1 << step
            return 1 << (step if place % 2 == 0 else 3 - step)
        pairs = [(place, place ^ bit_of(place)) for place in range(size)]
        bit = (here >> step) & 1
        if bits >= 3 and step in (1, 2):
            bit = jnp.where(here % 2 == 0, bit, (here >> (3 - step)) & 1)
        steps.append((pairs, bit))
    return steps


def tie(value, *others):
    return lax.optimization_barrier((value,) + others)[0]


def column_tiles(width):
    return 3 if width % 3 == 0 and width >= 3072 else 1


def halve(bit, kept, got, last):
    rows, width = kept.shape
    tiles = column_tiles(width)
    tile = width // tiles
    out_rows = rows if last else rows // 2
    spec = pl.BlockSpec((out_rows, tile), lambda i, *_: (0, i))
    whole = pl.BlockSpec((rows, tile), lambda i, *_: (0, i))
    count = 1 if last else 2
    return call(
        halve_kernel,
        (bit, kept, got),
        [whole] * 2,
        [jax.ShapeDtypeStruct((out_rows, width), BF16)] * count,
        [spec] * count,
        [] if last else [pltpu.VMEM((2, out_rows, tile), BF16)],
        tiles,
        rows * width,
        6 * rows * width,
    )


def join(bit, own, got):
    rows, width = own.shape
    tiles = column_tiles(width)
    tile = width // tiles
    spec = pl.BlockSpec((rows, tile), lambda i, *_: (0, i))
    out = call(
        join_kernel,
        (bit, own, got),
        [spec] * 2,
        jax.ShapeDtypeStruct((2, rows, width), BF16),
        pl.BlockSpec((2, rows, tile), lambda i, *_: (0, 0, i)),
        [],
        tiles,
        rows * width,
        8 * rows * width,
    )
    return out.reshape(2 * rows, width)


class HalvingSum:
    def __init__(self, kept, sent, axis):
        self.axis, self.value = axis, kept
        steps = bit_steps(axis)
        self.bits = [jnp.reshape(bit, (1,)).astype(jnp.int32) for _, bit in steps]
        self.pairs = [pairs for pairs, _ in steps]
        self.todo = [(True, at) for at in range(len(steps))] + [(False, at) for at in reversed(range(len(steps)))]
        self.begin(sent)

    def begin(self, sent):
        self.sent = sent
        self.got = lax.ppermute(sent, self.axis, self.pairs[self.todo[0][1]])

    def step(self, *after):
        if len(self.todo) == 1:
            return
        halving, at = self.todo.pop(0)
        got = tie(self.got, *after) if after else self.got
        if halving:
            last = at + 1 == len(self.bits)
            made = halve(self.bits[0 if last else at + 1], self.value, got, last)
            self.value = made[0]
            self.begin(made[-1])
        else:
            self.value = join(self.bits[at], self.value, got)
            self.begin(self.value)

    def halves(self, *after):
        while len(self.todo) > 1:
            self.step()
        return self.bits[0], self.value, tie(self.got, *after) if after else self.got


def split_body(tokens, merge_map, counts, ln_gain, w_qkv, qk_gain, w_out, w_up, b_up, w_down, b_down, cotangent):
    images, slots, dim = tokens.shape
    layers, inner = w_out.shape[:2]
    units = w_up.shape[2]
    head_dim = qk_gain.shape[-1]
    heads = inner // head_dim
    rows, lanes = padded_to(slots, 16), padded_to(slots, 128)
    n_narrow = lax.axis_size("narrow")
    size = images // 2
    firsts = (0, size)
    pair = 2 if size % 2 == 0 else 1
    chunk_rows = size * rows
    core_bit = jnp.reshape(lax.axis_index("wide") & 1, (1,)).astype(jnp.int32)
    small_rows = layers * (2 * dim + 2 * head_dim + units) // 128

    def others(value):
        if n_narrow == 2:
            return lax.ppermute(value, "narrow", [(0, 1), (1, 0)])
        wide_value = value.astype(F32)
        return (lax.psum(wide_value, "narrow") - wide_value).astype(BF16)

    row_array = jax.ShapeDtypeStruct((chunk_rows, dim), BF16)
    unit_array = jax.ShapeDtypeStruct((chunk_rows, units), BF16)
    head_flops = 2 * chunk_rows * dim * inner * 4 + 4 * chunk_rows * rows * inner
    feed_flops = 2 * chunk_rows * dim * units * 2
    layer_bytes = 2 * (4 * dim * inner + 2 * dim * units)
    lane_rows = pltpu.VMEM((lanes, dim), BF16)
    proj_rows = pltpu.VMEM((3 * inner, lanes), F32)
    low_rows = pltpu.VMEM((3 * inner, lanes), BF16)
    score_rows = pltpu.VMEM((heads, rows, lanes), F32)
    soft_rows = pltpu.VMEM((heads, lanes, lanes), BF16)
    head_rows = pltpu.VMEM((inner, lanes), BF16)
    row_spec = rows_spec(rows, dim)

    def forward(layer, first, qkv, qkv_layer, turn):
        piece_array = jax.ShapeDtypeStruct((pair * rows, dim), BF16)
        weights = [
            (merge_map, None),
            (ln_gain, None),
            (qkv, qkv_layer),
            (qk_gain, None),
            (w_out, layer),
            (w_up, layer),
            (b_up, None),
            (w_down, layer),
        ]
        turned = jax.ShapeDtypeStruct((layers, 3, inner, dim), BF16)
        return call(
            functools.partial(forward_kernel, layer, first, rows, turn),
            (counts, tokens) + tuple(w for w, _ in weights),
            [image_spec(1, slots, dim, first)] + [layer_spec(w, at) for w, at in weights],
            [piece_array] + [turned] * turn,
            [row_spec] + [whole_spec(turned)] * turn,
            [
                pltpu.VMEM((1, rows, dim), F32),
                lane_rows,
                proj_rows,
                low_rows,
                score_rows,
                soft_rows,
                head_rows,
                pltpu.VMEM((2, rows, units // 3), F32),
                pltpu.VMEM((rows, units), BF16),
            ],
            pair,
            2 * (head_flops + feed_flops),
            layer_bytes,
        )

    def feed_back(layer, top, first, pieces):
        weights = [(ln_gain, None), (b_down, None), (w_up, layer), (b_up, None), (w_down, layer)]
        outs = [
            row_array if top else jax.ShapeDtypeStruct((chunk_rows, dim), F32),
            row_array,
            row_array,
            row_array,
            unit_array,
            unit_array,
            jax.ShapeDtypeStruct((1, units), F32),
            jax.ShapeDtypeStruct((1, dim), F32),
        ] + [jax.ShapeDtypeStruct((size // pair, dim, pair * rows), BF16)] * 2
        block = rows_spec(pair * rows, dim)
        out_specs = [block] * 4 + [rows_spec(pair * rows, units)] * 2 + [whole_spec(outs[6]), whole_spec(outs[7])]
        out_specs += [image_spec(1, dim, pair * rows)] * 2
        operands = (tokens, cotangent, *pieces[0], *pieces[1], *pieces[2:])
        image_block = image_spec(pair, slots, dim, first // pair)
        specs = [image_block] * 2 + [whole_spec(one) for one in (*pieces[0], *pieces[1])] + [block] * len(pieces[2:])
        return call(
            functools.partial(feed_kernel, layer, top, first, rows, pair, size),
            (counts,) + operands + tuple(w for w, _ in weights),
            specs + [layer_spec(w, at) for w, at in weights],
            outs,
            out_specs,
            [pltpu.VMEM((2, rows, dim), F32)]
            + [pltpu.VMEM((2, pair * rows, units // 3), F32)] * 2
            + [pltpu.VMEM((pair * rows, dim), BF16)] * 2,
            size // pair,
            3 * feed_flops,
            layer_bytes + 12 * chunk_rows * dim * 2,
        )

    def heads_back(layer, top, first, turned, normed, low, d_feed, fed, begin=0, count=size):
        weights = [(turned, layer), (qk_gain, None), (w_out, layer)]
        streams = (normed, low, d_feed) + ((fed,) if top else ())
        row_array = jax.ShapeDtypeStruct((count * rows, dim), BF16)
        outs = ([row_array] if top else []) + [
            row_array,
            jax.ShapeDtypeStruct((count * rows, 4 * inner), BF16),
            jax.ShapeDtypeStruct((2 * head_dim, lanes), F32),
            jax.ShapeDtypeStruct((1, dim), F32),
        ]
        out_specs = ([row_spec] if top else []) + [
            row_spec,
            rows_spec(rows, 4 * inner),
            whole_spec(outs[-2]),
            whole_spec(outs[-1]),
        ]
        return call(
            functools.partial(heads_kernel, layer, top, first + begin, rows),
            (merge_map,) + streams + tuple(w for w, _ in weights),
            [whole_spec(merge_map)] + [rows_spec(rows, dim, begin)] * len(streams) + [layer_spec(w, at) for w, at in weights],
            outs,
            out_specs,
            [lane_rows] * 2
            + [proj_rows, low_rows, head_rows, score_rows, score_rows, soft_rows, soft_rows, head_rows]
            + [pltpu.VMEM((2 * inner, lanes), F32), low_rows, pltpu.VMEM((padded_to(heads, 8), lanes), F32), pltpu.VMEM((rows, dim), F32)],
            count,
            6 * head_flops,
            layer_bytes,
            prefetch=0,
        )

    def feed_grads(fed, before=()):
        groups = [[one[at] for one in fed] for at in (8, 9, 5, 4)]
        tile = units // 3
        tiles = units // tile
        flat = [array for group in groups for array in group]
        specs = [whole_spec(one) for one in groups[0] + groups[1]]
        specs += [pl.BlockSpec((chunk_rows, tile), lambda i: (0, jnp.minimum(i, tiles - 1)))] * len(fed)
        specs += [pl.BlockSpec((chunk_rows, tile), lambda i: (0, jnp.maximum(i - tiles, 0)))] * len(fed)
        return call(
            functools.partial(feed_weight_kernel, spans(groups)),
            (*flat, *before),
            specs + [pl.BlockSpec(memory_space=pl.ANY)] * len(before),
            jax.ShapeDtypeStruct((dim, before[0].shape[1] if before else 2 * units), BF16),
            pl.BlockSpec((dim, tile), lambda i: (0, i)),
            [],
            2 * tiles,
            2 * images * rows * dim * units * 2,
            2 * images * rows * (dim + units) * 2,
            prefetch=0,
            aliases={len(flat): 0} if before else None,
        )

    def heads_grads(fed, made, sums=()):
        columns = 4 * inner + (128 if sums else 0)
        groups = [[one[at] for one in fed] for at in (8, 9)] + [[one[1] for one in made], [ln_gain]] + list(sums)
        flat = [array for group in groups for array in group]
        specs = [whole_spec(one) for one in groups[0] + groups[1]]
        specs += [pl.BlockSpec((one.shape[0], inner), lambda i, *_: (0, i)) for one in groups[2]]
        specs += [whole_spec(one) for group in groups[3:] for one in group]
        return call(
            functools.partial(heads_weight_kernel, spans(groups)),
            (core_bit, *flat),
            specs,
            [jax.ShapeDtypeStruct((dim // 2, columns), BF16)] * 2,
            [pl.BlockSpec((dim // 2, columns), lambda i, *_: (0, 0))] * 2,
            [pltpu.VMEM((2, dim // 2, inner), BF16)]
            + ([pltpu.VMEM((padded_to(small_rows, 16), 128), F32)] if sums else []),
            4,
            2 * images * rows * dim * inner * 4,
            2 * images * rows * (dim + inner) * 4,
        )

    def unpack(kernel, halves, width, place, shapes, blocks, places, before):
        return call(
            kernel,
            (*halves, *before),
            [pl.BlockSpec((dim // 2, width), lambda i, *_: (0, place))]
            + [pl.BlockSpec((dim // 2, width), lambda i, *_: (halves[2].shape[0] // (dim // 2) - 1, place))]
            + [pl.BlockSpec(memory_space=pl.ANY)] * len(before),
            [jax.ShapeDtypeStruct(shape, F32) for shape in shapes],
            [pl.BlockSpec(block, place_of) for block, place_of in zip(blocks, places)],
            [],
            2,
            dim * width,
            6 * dim * width,
            aliases={at + 3: at for at in range(len(before))},
        )

    def row_half(i, bits):
        return lax.rem(i + bits[0], 2)

    def feed_unpack(halves, layer, before=()):
        return unpack(
            feed_unpack_kernel,
            halves,
            2 * units,
            0,
            ((layers, dim, units), (layers, units, dim)),
            ((1, dim // 2, units), (1, units, dim // 2)),
            (lambda i, bits: (layer, row_half(i, bits), 0), lambda i, bits: (layer, 0, row_half(i, bits))),
            before,
        )

    def heads_unpack(halves, layer, place=0, before=()):
        return unpack(
            heads_unpack_kernel,
            halves,
            halves[1].shape[1] - place * 4 * inner,
            place,
            ((layers, 3, dim, inner), (layers, inner, dim)),
            ((1, 3, dim // 2, inner), (1, inner, dim // 2)),
            (lambda i, bits: (layer, 0, row_half(i, bits), 0), lambda i, bits: (layer, 0, row_half(i, bits))),
            before,
        )

    tokens_slots = jnp.swapaxes(tokens, 0, 1)
    step_slots = 16
    slot_spec = pl.BlockSpec((step_slots, images, dim), lambda i, *_: (i, 0, 0))
    slot_array = jax.ShapeDtypeStruct((slots, images, dim), F32)
    chunk_spec = slots_spec(size, step_slots, dim)
    turned_rows = pltpu.VMEM((step_slots, images, dim), F32)

    def by_image(value):
        return value.reshape(value.shape[0] // rows, rows, dim)

    def paired(ours, theirs):
        return [by_image(one) for two in zip(ours, theirs) for one in two]

    def layer_output(before, ours, theirs, layer):
        pieces = paired(ours, theirs)
        return call(
            functools.partial(output_kernel, layer, len(ours)),
            (counts, before, *pieces, b_down),
            [slot_spec] + [slots_spec(one.shape[0], step_slots, dim) for one in pieces] + [whole_spec(b_down)],
            slot_array,
            slot_spec,
            [turned_rows],
            -(-slots // step_slots),
            10 * images * rows * dim,
            12 * images * rows * dim,
        )

    own, far = [], []
    qkv = w_qkv
    for first in range(0, images, pair):
        made = forward(0, first, tie(qkv, *own[-1:]) if own else qkv, 0 if own else None, not own)
        if not own:
            qkv = turned = made[1]
        own.append(made[0])
        far.append(others(made[0]))
    own_a, own_b = own[: len(own) // 2], own[len(own) // 2 :]
    far_a, far_b = far[: len(far) // 2], far[len(far) // 2 :]
    cotangent = tie(cotangent, own[-1])
    fed1_a = feed_back(1, True, 0, (own_a, far_a[:-1] + [tie(far_a[-1], own[-1])]))
    fed1_b = feed_back(1, True, size, (own_b, far_b[:-1] + [tie(far_b[-1], fed1_a[0])]))
    fed1 = (fed1_a, fed1_b)
    pack_feed1 = feed_grads(fed1)
    part_feed1 = lax.psum_scatter(pack_feed1, "wide", scatter_dimension=0, tiled=True)
    made1_a = heads_back(1, True, 0, turned, tie(fed1_a[1], pack_feed1), *fed1_a[2:4], fed1_a[0])
    far_grad_a = others(made1_a[1])
    made1_b = heads_back(1, True, size, turned, tie(fed1_b[1], made1_a[0]), *fed1_b[2:4], fed1_b[0])
    far_grad_b = others(made1_b[1])
    made1 = (made1_a[1:], made1_b[1:])
    heads1 = HalvingSum(*heads_grads(fed1, made1), "wide")
    fed0_a = feed_back(0, False, 0, (own_a, far_a, made1_a[1], tie(far_grad_a, heads1.sent)))
    heads1.step(fed0_a[0])
    first_out = layer_output(tie(tokens_slots, fed0_a[0], heads1.sent), own, far, 0)
    heads1.step(first_out)
    pack_feed1 = lax.all_gather(tie(part_feed1, heads1.sent, far_grad_b), "wide", axis=0, tiled=True)
    fed0_b = feed_back(0, False, size, (own_b, far_b, made1_b[1], tie(far_grad_b, heads1.sent)))
    fed0 = (fed0_a, fed0_b)
    far_next_a = others(tie(made1_a[0], first_out))
    far_next_b = others(tie(made1_b[0], first_out))
    heads1.step(fed0_b[0])
    pack_rest = feed_grads([tuple(one[:-1]) + (tie(one[-1], heads1.sent),) for one in fed0])
    heads1.step(pack_rest)
    made0, far_last = [], []
    for at in range(2):
        source = fed0[at]
        ready = (heads1.sent,) + tuple(one[0] for one in made0)
        made0.append(heads_back(0, False, at * size, turned, tie(source[1], *ready), *source[2:4], None))
        far_last.append(others(made0[-1][0]))
        if at == 0:
            pack_rest = tie(pack_rest, made0[0][0], far_next_a, far_next_b, pack_feed1, heads1.got)
    part_rest = lax.psum_scatter(pack_rest, "wide", scatter_dimension=0, tiled=True)
    heads1.step(made0[1][0])
    sums = []
    for fed, made in ((fed0, made0), (fed1, made1)):
        sums += [[one[3] for one in made], [one[2] for one in made], [one[7] for one in fed], [one[6] for one in fed]]
    sums[0][0] = tie(sums[0][0], heads1.sent)
    heads0 = HalvingSum(*heads_grads(fed0, made0, sums), "wide")
    heads0.step(far_last[0])
    second_out = layer_output(
        tie(first_out, heads0.sent), (made1_a[0], made1_b[0]), (far_next_a, far_next_b), 1
    )
    heads1.step(second_out)
    heads0.step(second_out, far_last[1])
    none = jnp.zeros((1,), jnp.int32)
    feed_outs = feed_unpack((none,) + (tie(pack_feed1, heads0.sent, heads1.sent),) * 2, 1)
    heads0.step(feed_outs[0])
    heads1.step(feed_outs[0])
    heads_outs = heads_unpack(heads1.halves(heads0.sent), 1)
    heads0.step(heads_outs[0])
    pack_rest = lax.all_gather(tie(part_rest, heads0.sent), "wide", axis=0, tiled=True)
    grad_tokens = call(
        functools.partial(tokens_kernel, len(made0)),
        (
            counts,
            tie(tokens_slots, heads0.sent),
            *paired([one[0] for one in made0], far_last),
            by_image(fed0_a[0]),
            by_image(fed0_b[0]),
            ln_gain,
        ),
        [slot_spec] + [chunk_spec] * (3 * len(made0)) + [whole_spec(ln_gain)],
        slot_array,
        slot_spec,
        [turned_rows] * 2,
        -(-slots // step_slots),
        10 * images * rows * dim,
        12 * images * rows * dim,
    )
    heads0.step(grad_tokens)
    while len(heads0.todo) > 1:
        heads0.step()
    rest = (none,) + (tie(pack_rest, heads0.sent),) * 2
    up, down = feed_unpack(rest, 0, feed_outs)
    halves0 = heads0.halves(up)
    small = jnp.where(halves0[0][0] == 0, *[half[:small_rows, 4 * inner :] for half in halves0[1:]])
    small = small.astype(F32).reshape(layers, -1)
    narrow_part = small[:, : dim + 2 * head_dim]
    if n_narrow == 2:
        narrow_part = narrow_part + lax.ppermute(narrow_part, "narrow", [(0, 1), (1, 0)])
    else:
        narrow_part = lax.psum(narrow_part, "narrow")
    g_b_down = small[:, dim + 2 * head_dim : 2 * dim + 2 * head_dim]
    g_b_up = small[:, 2 * dim + 2 * head_dim :]
    qkv, out = heads_unpack((halves0[0], tie(halves0[1], g_b_up), halves0[2]), 0, 0, heads_outs)
    return (
        jnp.swapaxes(first_out, 0, 1),
        jnp.swapaxes(second_out, 0, 1),
        jnp.swapaxes(grad_tokens, 0, 1),
        narrow_part[:, :dim],
        qkv,
        narrow_part[:, dim:].reshape(qk_gain.shape),
        out,
        up,
        g_b_up,
        down,
        g_b_down,
    )


def pick_body(*arrays):
    images, dim, inner, units = arrays[0].shape[0], arrays[0].shape[2], arrays[4].shape[-1], arrays[7].shape[-1]
    whole_heads = inner % arrays[5].shape[-1] == 0
    if whole_heads and images % 4 == 0 and units % inner == 0 and dim % 256 == 0 and inner % 128 == 0:
        return split_body(*arrays)
    return body(*arrays)


def solution(mesh):
    placed = (
        P("wide", None, None),
        P("wide", None),
        P("wide"),
        P(),
        P(None, None, None, "narrow"),
        P(),
        P(None, "narrow", None),
        P(None, None, "narrow"),
        P(None, "narrow"),
        P(None, "narrow", None),
        P(),
        P("wide", None, None),
    )
    return jax.shard_map(
        pick_body,
        mesh=mesh,
        in_specs=placed,
        out_specs=(
            P("wide", None, None),
            P("wide", None, None),
            P("wide", None, None),
            P(),
            P(None, None, None, "narrow"),
            P(),
            P(None, "narrow", None),
            P(None, None, "narrow"),
            P(None, "narrow"),
            P(None, "narrow", None),
            P(),
        ),
        check_vma=False,
    )
```

```python
import functools

import jax
import jax.numpy as jnp
from jax import lax
from jax.experimental import pallas as pl
from jax.experimental.pallas import tpu as pltpu
from jax.sharding import PartitionSpec as P


def shifted_2(value, axis, by):
    length = lax.axis_size(axis)
    pairs = [(i, i + by) for i in range(length) if 0 <= i + by < length]
    return lax.ppermute(value, axis, pairs)


def norm_rows(inputs, gain_row):
    centre = jnp.mean(inputs, axis=-1, keepdims=True)
    centered = inputs - centre
    inverse = lax.rsqrt(jnp.mean(centered * centered, axis=-1, keepdims=True) + 1e-06)
    normal = centered * inverse
    return (normal, inverse, normal * gain_row)


def norm_back(upstream, normal, inverse, gain_row):
    scaled = upstream * gain_row
    return inverse * (
        scaled
        - jnp.mean(scaled, axis=-1, keepdims=True)
        - normal * jnp.mean(scaled * normal, axis=-1, keepdims=True)
    )


def attend(normed_low, key_bias, qkv_full, out_full, qk_gains):
    head_dim = qk_gains.shape[-1]
    head_count = qkv_full.shape[-1] // head_dim
    qkv_heads = qkv_full.reshape(3, qkv_full.shape[1], head_count, head_dim)
    projected = jnp.einsum(
        "bsd,kdhe->kbhse", normed_low, qkv_heads, preferred_element_type=jnp.float32
    )
    q_normal, q_inverse, queries = norm_rows(projected[0], qk_gains[0])
    k_normal, k_inverse, keys_normed = norm_rows(projected[1], qk_gains[1])
    queries_low = queries.astype(jnp.bfloat16)
    keys_low = keys_normed.astype(jnp.bfloat16)
    values_low = projected[2].astype(jnp.bfloat16)
    score_scale = head_dim ** (-0.5)
    scores = jnp.einsum(
        "bhse,bhte->bhst", queries_low, keys_low, preferred_element_type=jnp.float32
    )
    logits = scores * score_scale + key_bias[:, None, None, :]
    shifted = jnp.exp(logits - jnp.max(logits, axis=-1, keepdims=True))
    softened = shifted / jnp.sum(shifted, axis=-1, keepdims=True)
    soft_low = softened.astype(jnp.bfloat16)
    mixed_low = jnp.einsum(
        "bhst,bhte->bhse", soft_low, values_low, preferred_element_type=jnp.float32
    ).astype(jnp.bfloat16)
    out_heads = out_full.reshape(head_count, head_dim, out_full.shape[-1])
    branch = jnp.einsum("bhse,hed->bsd", mixed_low, out_heads, preferred_element_type=jnp.float32)
    kept_parts = (
        q_normal,
        q_inverse,
        k_normal,
        k_inverse,
        queries_low,
        keys_low,
        values_low,
        softened,
        soft_low,
        mixed_low,
        qkv_heads,
        out_heads,
        score_scale,
    )
    return (branch, kept_parts)


def attend_back(normed_low, key_bias, qkv_full, out_full, qk_gains, grad_low):
    branch, kept_parts = attend(normed_low, key_bias, qkv_full, out_full, qk_gains)
    (
        q_normal,
        q_inverse,
        k_normal,
        k_inverse,
        queries_low,
        keys_low,
        values_low,
        softened,
        soft_low,
        mixed_low,
        qkv_heads,
        out_heads,
        score_scale,
    ) = kept_parts
    d_mixed = jnp.einsum(
        "bsd,hed->bhse", grad_low, out_heads, preferred_element_type=jnp.float32
    ).astype(jnp.bfloat16)
    g_out = jnp.einsum(
        "bhse,bsd->hed", mixed_low, grad_low, preferred_element_type=jnp.float32
    ).reshape(out_full.shape)
    d_soft = jnp.einsum("bhse,bhte->bhst", d_mixed, values_low, preferred_element_type=jnp.float32)
    row_dot = jnp.sum(softened * d_soft, axis=-1, keepdims=True)
    d_scores = (softened * (d_soft - row_dot) * score_scale).astype(jnp.bfloat16)
    d_queries = jnp.einsum(
        "bhst,bhte->bhse", d_scores, keys_low, preferred_element_type=jnp.float32
    )
    d_keys = jnp.einsum(
        "bhst,bhse->bhte", d_scores, queries_low, preferred_element_type=jnp.float32
    )
    d_values = jnp.einsum("bhst,bhse->bhte", soft_low, d_mixed, preferred_element_type=jnp.float32)
    g_gains = jnp.stack(
        [jnp.sum(d_queries * q_normal, axis=(0, 1, 2)), jnp.sum(d_keys * k_normal, axis=(0, 1, 2))]
    )
    d_projected = jnp.stack(
        [
            norm_back(d_queries, q_normal, q_inverse, qk_gains[0]),
            norm_back(d_keys, k_normal, k_inverse, qk_gains[1]),
            d_values,
        ]
    ).astype(jnp.bfloat16)
    g_qkv = jnp.einsum(
        "bsd,kbhse->kdhe", normed_low, d_projected, preferred_element_type=jnp.float32
    ).reshape(qkv_full.shape)
    d_normed = jnp.einsum(
        "kbhse,kdhe->bsd", d_projected, qkv_heads, preferred_element_type=jnp.float32
    )
    return (d_normed, g_qkv, g_out, g_gains)


def expand(normed_low, up_full, bias_full, down_full):
    pre_act = jnp.einsum(
        "bsd,df->bsf", normed_low, up_full, preferred_element_type=jnp.float32
    ) + bias_full.astype(jnp.float32)
    hidden, gelu_back = jax.vjp(jax.nn.gelu, pre_act)
    hidden_low = hidden.astype(jnp.bfloat16)
    branch = jnp.einsum("bsf,fd->bsd", hidden_low, down_full, preferred_element_type=jnp.float32)
    return (branch, hidden_low, gelu_back)


def expand_back(normed_low, up_full, bias_full, down_full, grad_low):
    branch, hidden_low, gelu_back = expand(normed_low, up_full, bias_full, down_full)
    d_hidden = jnp.einsum("bsd,fd->bsf", grad_low, down_full, preferred_element_type=jnp.float32)
    d_pre = gelu_back(d_hidden)[0].astype(jnp.bfloat16)
    g_bias = jnp.sum(d_pre, axis=(0, 1), dtype=jnp.float32)
    g_up = jnp.einsum("bsd,bsf->df", normed_low, d_pre, preferred_element_type=jnp.float32)
    g_down = jnp.einsum("bsf,bsd->fd", hidden_low, grad_low, preferred_element_type=jnp.float32)
    d_normed = jnp.einsum("bsf,df->bsd", d_pre, up_full, preferred_element_type=jnp.float32)
    return (d_normed, g_up, g_bias, g_down)


def body(
    tokens, merge_map, counts, ln_gain, w_qkv, qk_gain, w_out, w_up, b_up, w_down, b_down, cotangent
):
    pair_gap = lax.axis_size("narrow") // 2
    on_attention = lax.axis_index("narrow") < pair_gap
    layers = ln_gain.shape[0]
    col_half = w_qkv.shape[-1]
    unit_half = w_up.shape[-1]
    model_dim = tokens.shape[-1]
    slot_ids = jnp.arange(tokens.shape[1], dtype=jnp.int32)
    live_rows = slot_ids[None, :] < counts[:, None]
    row_weight = jnp.where(live_rows, 1.0, 0.0).astype(jnp.float32)[:, :, None]
    merged_sizes = jnp.sum(
        jnp.where(merge_map[:, :, None] == slot_ids[None, None, :], 1.0, 0.0), axis=1
    ).astype(jnp.float32)
    key_bias = jnp.where(live_rows, jnp.log(jnp.where(live_rows, merged_sizes, 1.0)), -1e30)
    attn_far = shifted_2((w_qkv, w_out), "narrow", -pair_gap)
    mlp_far = shifted_2((w_up, b_up, w_down), "narrow", pair_gap)

    def attention_weights(layer_at):
        qkv_full = jnp.concatenate([w_qkv[layer_at], attn_far[0][layer_at]], axis=-1)
        out_full = jnp.concatenate([w_out[layer_at], attn_far[1][layer_at]], axis=0)
        return (qkv_full, out_full)

    def feed_weights(layer_at):
        up_full = jnp.concatenate([mlp_far[0][layer_at], w_up[layer_at]], axis=-1)
        bias_full = jnp.concatenate([mlp_far[1][layer_at], b_up[layer_at]], axis=-1)
        down_full = jnp.concatenate([mlp_far[2][layer_at], w_down[layer_at]], axis=0)
        return (up_full, bias_full, down_full)

    current = tokens.astype(jnp.float32)
    layer_inputs = []
    outputs = []
    for layer_at in range(layers):
        normal, inverse, normed = norm_rows(current, ln_gain[layer_at])
        normed_low = normed.astype(jnp.bfloat16)

        def attention_forward():
            qkv_full, out_full = attention_weights(layer_at)
            return attend(normed_low, key_bias, qkv_full, out_full, qk_gain[layer_at])[0]

        def feed_forward():
            up_full, bias_full, down_full = feed_weights(layer_at)
            return expand(normed_low, up_full, bias_full, down_full)[0]

        partial_value = lax.cond(on_attention, attention_forward, feed_forward)
        layer_inputs.append(current)
        branch_total = lax.psum(partial_value, "narrow")
        current = row_weight * (current + branch_total + b_down[layer_at])
        outputs.append(current)
    grad_rows = cotangent.astype(jnp.float32)
    collected = []
    for layer_at in reversed(range(layers)):
        normal, inverse, normed = norm_rows(layer_inputs[layer_at], ln_gain[layer_at])
        normed_low = normed.astype(jnp.bfloat16)
        masked_grad = row_weight * grad_rows
        grad_low = masked_grad.astype(jnp.bfloat16)

        def attention_side():
            qkv_full, out_full = attention_weights(layer_at)
            d_normed, g_qkv, g_out, g_gains = attend_back(
                normed_low, key_bias, qkv_full, out_full, qk_gain[layer_at], grad_low
            )
            return (
                d_normed,
                g_gains,
                g_qkv,
                g_out,
                jnp.zeros((model_dim, 2 * unit_half), jnp.float32),
                jnp.zeros((2 * unit_half,), jnp.float32),
                jnp.zeros((2 * unit_half, model_dim), jnp.float32),
            )

        def feed_side():
            up_full, bias_full, down_full = feed_weights(layer_at)
            d_normed, g_up, g_bias, g_down = expand_back(
                normed_low, up_full, bias_full, down_full, grad_low
            )
            return (
                d_normed,
                jnp.zeros(qk_gain[layer_at].shape, jnp.float32),
                jnp.zeros((3, model_dim, 2 * col_half), jnp.float32),
                jnp.zeros((2 * col_half, model_dim), jnp.float32),
                g_up,
                g_bias,
                g_down,
            )

        returned = lax.cond(on_attention, attention_side, feed_side)
        d_normed, g_gains = (
            lax.psum(returned[0].astype(jnp.bfloat16), "narrow").astype(jnp.float32),
            lax.psum(returned[1].astype(jnp.bfloat16), "narrow").astype(jnp.float32),
        )
        g_ln = jnp.sum(d_normed * normal, axis=(0, 1))
        grad_rows = masked_grad + norm_back(d_normed, normal, inverse, ln_gain[layer_at])
        qkv_far, out_far = (
            shifted_2(returned[2][..., col_half:].astype(jnp.bfloat16), "narrow", pair_gap).astype(
                jnp.float32
            ),
            shifted_2(returned[3][col_half:].astype(jnp.bfloat16), "narrow", pair_gap).astype(
                jnp.float32
            ),
        )
        up_far, bias_far, down_far = (
            shifted_2(returned[4][:, :unit_half].astype(jnp.bfloat16), "narrow", -pair_gap).astype(
                jnp.float32
            ),
            shifted_2(returned[5][:unit_half].astype(jnp.bfloat16), "narrow", -pair_gap).astype(
                jnp.float32
            ),
            shifted_2(returned[6][:unit_half].astype(jnp.bfloat16), "narrow", -pair_gap).astype(
                jnp.float32
            ),
        )
        own_qkv = jnp.where(on_attention, returned[2][..., :col_half], qkv_far)
        own_out = jnp.where(on_attention, returned[3][:col_half], out_far)
        own_up = jnp.where(on_attention, up_far, returned[4][:, unit_half:])
        own_bias = jnp.where(on_attention, bias_far, returned[5][unit_half:])
        own_down = jnp.where(on_attention, down_far, returned[6][unit_half:])
        g_bdown = jnp.sum(masked_grad, axis=(0, 1))
        shards = (own_qkv, own_out, own_up, own_bias, own_down, g_ln, g_gains, g_bdown)
        collected.append(shards)
    collected = collected[::-1]
    stacked = tuple(
        (jnp.stack([element[position] for element in collected]) for position in range(8))
    )
    stacked = (
        lax.psum(stacked[0].astype(jnp.bfloat16), "wide").astype(jnp.float32),
        lax.psum(stacked[1].astype(jnp.bfloat16), "wide").astype(jnp.float32),
        lax.psum(stacked[2].astype(jnp.bfloat16), "wide").astype(jnp.float32),
        lax.psum(stacked[3].astype(jnp.bfloat16), "wide").astype(jnp.float32),
        lax.psum(stacked[4].astype(jnp.bfloat16), "wide").astype(jnp.float32),
        lax.psum(stacked[5].astype(jnp.bfloat16), "wide").astype(jnp.float32),
        lax.psum(stacked[6].astype(jnp.bfloat16), "wide").astype(jnp.float32),
        lax.psum(stacked[7].astype(jnp.bfloat16), "wide").astype(jnp.float32),
    )
    return (
        outputs[0],
        outputs[-1],
        grad_rows,
        stacked[5],
        stacked[0],
        stacked[6],
        stacked[1],
        stacked[2],
        stacked[3],
        stacked[4],
        stacked[7],
    )


EPS = 1e-06
F32 = jnp.float32
BF16 = jnp.bfloat16
COST_SCALE = 2
AG_AFTER = 1
VMEM_BYTES = 60 * 1024 * 1024
GELU_IN = 0.7978845608028654
GELU_CUBE = 0.044715


def padded_to(length, step):
    return -(-length // step) * step


def dot(a, b):
    return jnp.dot(a, b, preferred_element_type=F32)


def dot_nt(a, b):
    return lax.dot_general(a, b, (((1,), (1,)), ((), ())), preferred_element_type=F32)


def normal_rows(x):
    centered = x - jnp.mean(x, axis=-1, keepdims=True)
    inverse = lax.rsqrt(jnp.mean(centered * centered, axis=-1, keepdims=True) + EPS)
    return centered * inverse, inverse


def back_rows(upstream, normal, inverse, gain):
    scaled = upstream * gain
    return inverse * (
        scaled
        - jnp.mean(scaled, axis=-1, keepdims=True)
        - normal * jnp.mean(scaled * normal, axis=-1, keepdims=True)
    )


def live_of(count, rows):
    return lax.broadcasted_iota(jnp.int32, (rows, 1), 0) < count


def fill_rows(source, wide_rows):
    slots = source.shape[0]
    edge = slots // 8 * 8
    wide_rows[edge:, :] = jnp.zeros((wide_rows.shape[0] - edge, wide_rows.shape[1]), F32)
    wide_rows[:slots, :] = source[...].astype(F32)


def head_norm(x):
    centered = x - jnp.mean(x, axis=1, keepdims=True)
    inverse = lax.rsqrt(jnp.mean(centered * centered, axis=1, keepdims=True) + EPS)
    return centered * inverse, inverse


def head_back(upstream, normal, inverse, gain):
    scaled = upstream * gain
    return inverse * (
        scaled
        - jnp.mean(scaled, axis=1, keepdims=True)
        - normal * jnp.mean(scaled * normal, axis=1, keepdims=True)
    )


def key_sizes(patch_ref, image, rows):
    slots = patch_ref.shape[1]
    slot = lax.broadcasted_iota(jnp.int32, (rows, slots), 0)
    named = jnp.where(patch_ref[pl.ds(image, 1), :] == slot, 1.0, 0.0)
    return jnp.sum(named, axis=-1, keepdims=True)


def head_gains(qk_gain, layer):
    both = qk_gain[layer]
    return [jnp.broadcast_to(both[at : at + 1, :], (8, both.shape[1])).T[:, :1] for at in range(2)]


def project(turned, normed, gains, proj, lows):
    inner, head_dim = proj.shape[0] // 3, gains[0].shape[0]
    heads, lanes = inner // head_dim, proj.shape[1]
    proj[...] = dot_nt(turned, normed)
    inverses = []
    for part in range(2):
        here = slice(part * inner, (part + 1) * inner)
        normal, inverse = head_norm(proj[here, :].reshape(heads, head_dim, lanes))
        inverses.append(inverse)
        proj[here, :] = normal.reshape(inner, lanes)
        low = (normal * gains[part][None]).astype(BF16)
        if part == 0:
            low = (low.astype(F32) * head_dim ** (-0.5)).astype(BF16)
        lows[here, :] = low.reshape(inner, lanes)
    lows[2 * inner :, :] = proj[2 * inner :, :].astype(BF16)
    return inverses


def soften(lows, sizes, scores, soft):
    heads, rows, strip = scores.shape[0], scores.shape[1], 16
    inner = lows.shape[0] // 3
    head_dim = inner // heads
    for head in range(heads):
        at = head * head_dim
        keys = lows[inner + at : inner + at + head_dim, :]
        scores[head] = dot(keys.T[:rows], lows[at : at + head_dim, :])
    over = []
    for head in range(heads):
        total = jnp.zeros((8, scores.shape[2]), F32)
        for at in range(0, rows, strip):
            raised = jnp.exp(scores[head, at : at + strip, :]) * sizes[at : at + strip, :]
            scores[head, at : at + strip, :] = raised
            soft[head, at : at + strip, :] = raised.astype(BF16)
            total = total + (raised[:8] + raised[8:])
        over.append(1.0 / jnp.sum(total, axis=0, keepdims=True))
    return over


def forward_kernel(layer, first, rows, turn, counts, *refs):
    tok, patch, gain, w_qkv, qk_gain, w_out, w_up, b_up, w_down, out = refs[:10]
    if turn:
        turned = refs[10]
        refs = refs[11:]
    else:
        turned = w_qkv
        refs = refs[10:]
    wide_rows, normed, proj, lows, scores, soft, mixed, pre_rows, hidden = refs
    step = pl.program_id(0)
    inner = w_out.shape[1]

    @pl.when(step == 0)
    def _():
        normed[...] = jnp.zeros(normed.shape, BF16)
        soft[...] = jnp.zeros(soft.shape, BF16)
        if turn:
            for at in range(w_qkv.shape[0]):
                for part in range(3):
                    turned[at, part] = w_qkv[at, part].T

    fill_rows(tok.at[0], wide_rows.at[0])
    strip = 16
    for at in range(0, rows, strip):
        x = jnp.where(live_of(counts[first + step] - at, strip), wide_rows[0, at : at + strip, :], 0.0)
        normed[at : at + strip, :] = (normal_rows(x)[0] * gain[layer : layer + 1, :]).astype(BF16)
    gains = head_gains(qk_gain, layer)
    head_dim = gains[0].shape[0]
    project(turned[0].reshape(3 * inner, turned.shape[3]), normed[...], gains, proj, lows)
    over = soften(lows, key_sizes(patch, first + step, rows), scores, soft)
    for head in range(inner // head_dim):
        at = head * head_dim
        values = lows[2 * inner + at : 2 * inner + at + head_dim, :]
        mixed[at : at + head_dim, :] = (dot(values, soft[head]) * over[head]).astype(BF16)
    bias = b_up[...].astype(F32)[layer : layer + 1, :]
    units = w_up.shape[2]
    tile = units // 3
    for slot, at in enumerate(range(0, units, tile)):
        pre_rows[slot % 2] = dot(normed[:rows, :], w_up[0, :, at : at + tile])
        for row in range(0, rows, strip):
            pre = pre_rows[slot % 2, row : row + strip, :] + bias[:, at : at + tile]
            bent = jnp.tanh(pre * (GELU_IN + (GELU_IN * GELU_CUBE) * (pre * pre)))
            hidden[row : row + strip, at : at + tile] = (pre * (0.5 + 0.5 * bent)).astype(BF16)
    out[...] = (dot(mixed[...].T[:rows], w_out[0]) + dot(hidden[...], w_down[0])).astype(BF16)


def feed_kernel(layer, top, first, rows, per_step, tok_images, counts, *refs):
    refs = list(refs)
    tok, cot = refs[:2]
    steps = (tok_images + per_step - 1) // per_step
    own_pieces, far_pieces = refs[2 : 2 + steps], refs[2 + steps : 2 + 2 * steps]
    refs = refs[2 + 2 * steps :]
    if not top:
        own_grad, far_grad = refs[:2]
        refs = refs[2:]
    gain, b_prev, w_up, b_up, w_down = refs[:5]
    refs = refs[5:]
    extra = refs[0]
    refs = refs[1:]
    normed, low, d_feed, hidden_out, d_pre_out, sum_up, sum_down, normed_t, low_t, wide_rows, pre_rows, d_rows, own, far = refs
    step = pl.program_id(0)
    for at in range(steps):

        @pl.when(step == at)
        def _(at=at):
            own[...] = own_pieces[at][...]
            far[...] = far_pieces[at][...]


    @pl.when(step == 0)
    def _():
        sum_up[...] = jnp.zeros(sum_up.shape, F32)
        sum_down[...] = jnp.zeros(sum_down.shape, F32)

    strip = 16
    for j in range(per_step):
        count = counts[first + step * per_step + j]
        fill_rows(tok.at[j], wide_rows.at[0])
        fill_rows(cot.at[j], wide_rows.at[1])
        total = jnp.zeros((8, tok.shape[2]), F32)
        for at in range(0, rows, strip):
            block = slice(j * rows + at, j * rows + at + strip)
            live = live_of(count - at, strip)
            x0 = jnp.where(live, wide_rows[0, at : at + strip, :], 0.0)
            branch = own[block, :].astype(F32) + far[block, :].astype(F32)
            x1 = jnp.where(live, x0 + branch + b_prev[:1, :], 0.0)
            grad = jnp.where(live, wide_rows[1, at : at + strip, :], 0.0)
            if top:
                x = x1
            else:
                x = x0
                normal, inverse = normal_rows(x1)
                d_normed = own_grad[block, :].astype(F32) + far_grad[block, :].astype(F32)
                grad = grad + back_rows(d_normed, normal, inverse, gain[layer + 1 : layer + 2, :])
                extra[block, :] = grad
            normed[block, :] = (normal_rows(x)[0] * gain[layer : layer + 1, :]).astype(BF16)
            low[block, :] = grad.astype(BF16)
            total = total + (grad[:8] + grad[8:])
        sum_down[...] += jnp.sum(total, axis=0, keepdims=True)
    normed_t[0] = normed[...].T
    low_t[0] = low[...].T
    bias = b_up[...].astype(F32)[layer : layer + 1, :]
    units = w_up.shape[2]
    tile = units // 3
    for slot, at in enumerate(range(0, units, tile)):
        part = slice(at, at + tile)
        pre_rows[slot % 2] = dot(normed[...], w_up[0, :, part])
        d_rows[slot % 2] = dot_nt(low[...], w_down[0, part, :])
        total = jnp.zeros((8, tile), F32)
        for row in range(0, per_step * rows, strip):
            block = slice(row, row + strip)
            pre = pre_rows[slot % 2, block, :] + bias[:, part]
            square = pre * pre
            bent = jnp.tanh(pre * (GELU_IN + (GELU_IN * GELU_CUBE) * square))
            half = 0.5 + 0.5 * bent
            hidden_out[block, part] = (pre * half).astype(BF16)
            steep = GELU_IN + (3 * GELU_IN * GELU_CUBE) * square
            slope = half + (0.5 * pre) * ((1.0 - bent * bent) * steep)
            d_pre = (d_rows[slot % 2, block, :] * slope).astype(BF16)
            d_pre_out[block, part] = d_pre
            d_pre = d_pre.astype(F32)
            total = total + (d_pre[:8] + d_pre[8:])
        sum_up[:, part] += jnp.sum(total, axis=0, keepdims=True)
    d_feed[...] = dot_nt(d_pre_out[...], w_up[0]).astype(BF16)
    if top:
        extra[...] = dot(hidden_out[...], w_down[0]).astype(BF16)


def heads_kernel(layer, top, first, rows, patch, normed_in, low_in, d_feed, *refs):
    refs = list(refs)
    if top:
        fed = refs[0]
        refs = refs[1:]
    w_qkv, qk_gain, w_out = refs[:3]
    refs = refs[3:]
    if top:
        out = refs[0]
        refs = refs[1:]
    d_normed, rights, sum_gain, sum_row = refs[:4]
    normed, low, proj, lows, d_mixed, scores, slopes, soft, d_soft, mixed, d_heads, d_proj, row_dots, total = refs[4:]
    step = pl.program_id(0)
    inner = w_out.shape[1]
    gains = head_gains(qk_gain, layer)
    head_dim = gains[0].shape[0]

    @pl.when(step == 0)
    def _():
        normed[...] = jnp.zeros(normed.shape, BF16)
        low[...] = jnp.zeros(low.shape, BF16)
        soft[...] = jnp.zeros(soft.shape, BF16)
        d_soft[...] = jnp.zeros(d_soft.shape, BF16)
        sum_gain[...] = jnp.zeros(sum_gain.shape, F32)
        sum_row[...] = jnp.zeros(sum_row.shape, F32)

    normed[:rows, :] = normed_in[...]
    low[:rows, :] = low_in[...]
    turned = w_qkv[0].reshape(3 * inner, w_qkv.shape[3])
    heads, lanes = inner // head_dim, proj.shape[1]
    inverses = project(turned, normed[...], gains, proj, lows)
    d_mixed[...] = dot_nt(w_out[0], low[...]).astype(BF16)
    over = soften(lows, key_sizes(patch, first + step, rows), scores, soft)
    for head in range(heads):
        here = slice(head * head_dim, (head + 1) * head_dim)
        mixed_here = dot(lows[2 * inner + here.start : 2 * inner + here.stop, :], soft[head]) * over[head]
        mixed[here, :] = mixed_here.astype(BF16)
        d_mixed_here = d_mixed[here, :].astype(F32)
        row_dots[head : head + 1, :] = jnp.sum(d_mixed_here * mixed_here, axis=0, keepdims=True) * over[head]
        d_mixed[here, :] = (d_mixed_here * over[head]).astype(BF16)
    for head in range(heads):
        here = slice(head * head_dim, (head + 1) * head_dim)
        values = lows[2 * inner + here.start : 2 * inner + here.stop, :]
        slopes[head] = dot(values.T[:rows], d_mixed[here, :])
    for head in range(heads):
        for row in range(0, rows, 16):
            block = slice(row, row + 16)
            slope = slopes[head, block, :] - row_dots[head : head + 1, :]
            d_soft[head, block, :] = (scores[head, block, :] * slope).astype(BF16)
    for head in range(heads):
        here = slice(head * head_dim, (head + 1) * head_dim)
        keys = slice(inner + here.start, inner + here.stop)
        values = slice(2 * inner + here.start, 2 * inner + here.stop)
        d_heads[here, :] = dot(lows[keys, :], d_soft[head]) * head_dim ** (-0.5)
        d_heads[keys, :] = dot_nt(lows[here, :], d_soft[head])
        d_proj[values, :] = dot_nt(d_mixed[here, :], soft[head]).astype(BF16)
    for part in range(2):
        here = slice(part * inner, (part + 1) * inner)
        normal = proj[here, :].reshape(heads, head_dim, lanes)
        upstream = d_heads[here, :].reshape(heads, head_dim, lanes)
        sum_gain[part * head_dim : (part + 1) * head_dim, :] += jnp.sum(upstream * normal, axis=0)
        back = head_back(upstream, normal, inverses[part], gains[part][None])
        d_proj[here, :] = back.reshape(inner, lanes).astype(BF16)
    mixed_rows = mixed[...].T[:rows]
    rights[:, 3 * inner :] = mixed_rows
    if top:
        out[...] = (fed[...].astype(F32) + dot(mixed_rows, w_out[0])).astype(BF16)
    for part in range(3):
        rights[:, part * inner : (part + 1) * inner] = d_proj[part * inner : (part + 1) * inner, :].T[:rows]
    total[...] = dot(rights[:, : 3 * inner], turned)
    row_sum = jnp.zeros((8, total.shape[1]), F32)
    for row in range(0, rows, 16):
        block = slice(row, row + 16)
        d_here = total[block, :] + d_feed[block, :].astype(F32)
        d_normed[block, :] = d_here.astype(BF16)
        d_here = d_here * normed_in[block, :].astype(F32)
        row_sum = row_sum + (d_here[:8] + d_here[8:])
    sum_row[...] += jnp.sum(row_sum, axis=0, keepdims=True)


def live_slots(counts, shape):
    slot = lax.broadcasted_iota(jnp.int32, shape, 0) + pl.program_id(0) * shape[0]
    image = lax.broadcasted_iota(jnp.int32, shape, 1)
    count = jnp.zeros(shape, jnp.int32)
    for at in range(shape[1]):
        count = jnp.where(image == at, counts[at], count)
    return slot < count


def chunk_sums(refs, sums):
    image = 0
    for own, far in refs:
        for at in range(own.shape[0]):
            sums[:, image, :] = own[at].astype(F32) + far[at].astype(F32)
            image += 1


def output_kernel(layer, chunks, counts, before, *refs):
    pairs = [(refs[2 * at], refs[2 * at + 1]) for at in range(chunks)]
    bias, out, sums = refs[2 * chunks :]
    live = live_slots(counts, out.shape[:2] + (1,))
    chunk_sums(pairs, sums)
    for at in range(0, out.shape[0], 2):
        part = slice(at, at + 2)
        total = before[part].astype(F32) + sums[part] + bias[layer : layer + 1, :]
        out[part] = jnp.where(live[part], total, 0.0)


def tokens_kernel(chunks, counts, tok, *refs):
    pairs = [(refs[2 * at], refs[2 * at + 1]) for at in range(chunks)]
    grads = refs[2 * chunks : -4]
    gain, out, sums, turned = refs[-4:]
    live = live_slots(counts, out.shape[:2] + (1,))
    chunk_sums(pairs, sums)
    image = 0
    for grad in grads:
        for at in range(grad.shape[0]):
            turned[:, image, :] = grad[at]
            image += 1
    for at in range(0, out.shape[0], 2):
        part = slice(at, at + 2)
        normal, inverse = normal_rows(jnp.where(live[part], tok[part].astype(F32), 0.0))
        total = turned[part] + back_rows(sums[part], normal, inverse, gain[:1, :])
        out[part] = jnp.where(live[part], total, 0.0)


def weight_tile(lefts, rights):
    total, first, at = None, 0, 0
    for left in lefts:
        for block in range(left.shape[0]):
            rows = left.shape[2]
            if first == rights[at].shape[0]:
                first, at = 0, at + 1
            term = dot(left[block], rights[at][first : first + rows, :])
            total = term if total is None else total + term
            first += rows
    return total.astype(BF16)


def store_tile(bit, tile, both, kept, sent, columns=slice(None)):
    if sent is None:
        kept[:, columns] = tile
        return
    both[:, :, : tile.shape[1]] = tile.reshape(2, -1, tile.shape[1])
    kept[:, columns] = both[bit, :, : tile.shape[1]]
    sent[:, columns] = both[1 - bit, :, : tile.shape[1]]


def feed_weight_kernel(counts, *refs):
    normed_t, low_t, d_pre, hidden = [refs[first:last] for first, last in counts]
    out = refs[-1]
    half = pl.num_programs(0) // 2

    @pl.when(pl.program_id(0) < half)
    def _():
        out[...] = weight_tile(normed_t, d_pre)

    @pl.when(pl.program_id(0) >= half)
    def _():
        out[...] = weight_tile(low_t, hidden)


def heads_weight_kernel(counts, bits, *refs):
    normed_t, low_t, rights, gain, *sums = [refs[first:last] for first, last in counts]
    if sums:
        kept, sent, both, lined = refs[-4:]
    else:
        kept, sent, both = refs[-3:]
    inner = rights[0].shape[1]
    for part in range(4):

        @pl.when(pl.program_id(0) == part)
        def _(part=part):
            lefts = low_t if part == 3 else normed_t
            columns = slice(part * inner, (part + 1) * inner)
            store_tile(bits[0], weight_tile(lefts, rights), both, kept, sent, columns)

    if not sums:
        return

    @pl.when(pl.program_id(0) == 0)
    def _():
        lined[...] = jnp.zeros(lined.shape, F32)
        row = 0
        for layer in range(len(sums) // 4):
            s_row, s_gain, s_down, s_up = [
                functools.reduce(lambda a, b: a + b, [one[...] for one in group])
                for group in sums[4 * layer : 4 * layer + 4]
            ]
            s_row = s_row / gain[0][layer : layer + 1, :]
            s_gain = jnp.sum(s_gain.T, axis=0, keepdims=True)
            for values in (s_row, s_gain, s_down, s_up):
                for at in range(0, values.shape[1], 128):
                    lined[row : row + 1, :] = values[:, at : at + 128]
                    row += 1
        none = jnp.zeros((kept.shape[0], 128), BF16)
        kept[:, 4 * inner :] = none
        sent[:, 4 * inner :] = none
        small = lined[...].astype(BF16)

        @pl.when(bits[0] == 0)
        def _():
            kept[: lined.shape[0], 4 * inner :] = small

        @pl.when(bits[0] == 1)
        def _():
            sent[: lined.shape[0], 4 * inner :] = small


def halve_kernel(bits, kept, got, *refs):
    total = (kept[...].astype(F32) + got[...].astype(F32)).astype(BF16)
    if len(refs) == 1:
        refs[0][...] = total
        return
    left, sent, both = refs
    both[...] = total.reshape(both.shape)
    left[...] = both[bits[0]]
    sent[...] = both[1 - bits[0]]


def join_kernel(bits, own, got, out):
    out[bits[0]] = own[...]
    out[1 - bits[0]] = got[...]


def feed_unpack_kernel(bits, own, got, *refs):
    up, down = refs[-2:]
    units = up.shape[2]

    def place(pack):
        up[0] = pack[:, :units].astype(F32)
        down[0] = pack[:, units : 2 * units].astype(F32).T

    pl.when(pl.program_id(0) == 0)(lambda: place(own))
    pl.when(pl.program_id(0) == 1)(lambda: place(got))


def heads_unpack_kernel(bits, own, got, *refs):
    qkv, out = refs[-2:]
    inner = qkv.shape[3]

    def place(pack):
        for at in range(3):
            qkv[0, at] = pack[:, at * inner : (at + 1) * inner].astype(F32)
        out[0] = pack[:, 3 * inner : 4 * inner].astype(F32).T

    pl.when(pl.program_id(0) == 0)(lambda: place(own))
    pl.when(pl.program_id(0) == 1)(lambda: place(got))


def spans(groups):
    ends = []
    for group in groups:
        first = ends[-1][1] if ends else 0
        ends.append((first, first + len(group)))
    return tuple(ends)


def whole_spec(array):
    return pl.BlockSpec(array.shape, lambda i, *_: (0,) * array.ndim)


def layer_spec(array, layer):
    if layer is None:
        return whole_spec(array)
    return pl.BlockSpec((1,) + array.shape[1:], lambda i, *_: (layer,) + (0,) * (array.ndim - 1))


def rows_spec(rows, columns, first=0):
    return pl.BlockSpec((rows, columns), lambda i, *_: (first + i, 0))


def image_spec(images, slots, columns, first=0):
    return pl.BlockSpec((images, slots, columns), lambda i, *_: (first + i, 0, 0))


def slots_spec(images, slots, columns):
    return pl.BlockSpec((images, slots, columns), lambda i, *_: (0, i, 0))


def call(kernel, operands, specs, shapes, out_specs, scratch, grid, flops, moved, prefetch=1, aliases=None):
    return pl.pallas_call(
        kernel,
        grid_spec=pltpu.PrefetchScalarGridSpec(
            num_scalar_prefetch=prefetch,
            grid=(grid,),
            in_specs=specs,
            out_specs=out_specs,
            scratch_shapes=scratch,
        ),
        out_shape=shapes,
        compiler_params=pltpu.CompilerParams(
            dimension_semantics=("arbitrary",), vmem_limit_bytes=VMEM_BYTES
        ),
        cost_estimate=pl.CostEstimate(flops=flops // COST_SCALE, bytes_accessed=moved // COST_SCALE, transcendentals=0),
        input_output_aliases=aliases or {},
    )(*operands)


def bit_steps(axis):
    size = lax.axis_size(axis)
    bits = size.bit_length() - 1
    here = lax.axis_index(axis)
    steps = []
    for step in range(bits):

        def bit_of(place, step=step):
            if bits < 3 or step not in (1, 2):
                return 1 << step
            return 1 << (step if place % 2 == 0 else 3 - step)
        pairs = [(place, place ^ bit_of(place)) for place in range(size)]
        bit = (here >> step) & 1
        if bits >= 3 and step in (1, 2):
            bit = jnp.where(here % 2 == 0, bit, (here >> (3 - step)) & 1)
        steps.append((pairs, bit))
    return steps


def tie(value, *others):
    return lax.optimization_barrier((value,) + others)[0]


def column_tiles(width):
    return 3 if width % 3 == 0 and width >= 3072 else 1


def halve(bit, kept, got, last):
    rows, width = kept.shape
    tiles = column_tiles(width)
    tile = width // tiles
    out_rows = rows if last else rows // 2
    spec = pl.BlockSpec((out_rows, tile), lambda i, *_: (0, i))
    whole = pl.BlockSpec((rows, tile), lambda i, *_: (0, i))
    count = 1 if last else 2
    return call(
        halve_kernel,
        (bit, kept, got),
        [whole] * 2,
        [jax.ShapeDtypeStruct((out_rows, width), BF16)] * count,
        [spec] * count,
        [] if last else [pltpu.VMEM((2, out_rows, tile), BF16)],
        tiles,
        rows * width,
        6 * rows * width,
    )


def join(bit, own, got):
    rows, width = own.shape
    tiles = column_tiles(width)
    tile = width // tiles
    spec = pl.BlockSpec((rows, tile), lambda i, *_: (0, i))
    out = call(
        join_kernel,
        (bit, own, got),
        [spec] * 2,
        jax.ShapeDtypeStruct((2, rows, width), BF16),
        pl.BlockSpec((2, rows, tile), lambda i, *_: (0, 0, i)),
        [],
        tiles,
        rows * width,
        8 * rows * width,
    )
    return out.reshape(2 * rows, width)


class HalvingSum:
    def __init__(self, kept, sent, axis):
        self.axis, self.value = axis, kept
        steps = bit_steps(axis)
        self.bits = [jnp.reshape(bit, (1,)).astype(jnp.int32) for _, bit in steps]
        self.pairs = [pairs for pairs, _ in steps]
        self.todo = [(True, at) for at in range(len(steps))] + [(False, at) for at in reversed(range(len(steps)))]
        self.begin(sent)

    def begin(self, sent):
        self.sent = sent
        self.got = lax.ppermute(sent, self.axis, self.pairs[self.todo[0][1]])

    def step(self, *after):
        if len(self.todo) == 1:
            return
        halving, at = self.todo.pop(0)
        got = tie(self.got, *after) if after else self.got
        if halving:
            last = at + 1 == len(self.bits)
            made = halve(self.bits[0 if last else at + 1], self.value, got, last)
            self.value = made[0]
            self.begin(made[-1])
        else:
            self.value = join(self.bits[at], self.value, got)
            self.begin(self.value)

    def halves(self, *after):
        while len(self.todo) > 1:
            self.step()
        return self.bits[0], self.value, tie(self.got, *after) if after else self.got


def split_body(tokens, merge_map, counts, ln_gain, w_qkv, qk_gain, w_out, w_up, b_up, w_down, b_down, cotangent):
    images, slots, dim = tokens.shape
    layers, inner = w_out.shape[:2]
    units = w_up.shape[2]
    head_dim = qk_gain.shape[-1]
    heads = inner // head_dim
    rows, lanes = padded_to(slots, 16), padded_to(slots, 128)
    n_narrow = lax.axis_size("narrow")
    size = images // 2
    firsts = (0, size)
    pair = 2 if size % 2 == 0 else 1
    chunk_rows = size * rows
    core_bit = jnp.reshape(lax.axis_index("wide") & 1, (1,)).astype(jnp.int32)
    small_rows = layers * (2 * dim + 2 * head_dim + units) // 128

    def others(value):
        if n_narrow == 2:
            return lax.ppermute(value, "narrow", [(0, 1), (1, 0)])
        wide_value = value.astype(F32)
        return (lax.psum(wide_value, "narrow") - wide_value).astype(BF16)

    row_array = jax.ShapeDtypeStruct((chunk_rows, dim), BF16)
    unit_array = jax.ShapeDtypeStruct((chunk_rows, units), BF16)
    head_flops = 2 * chunk_rows * dim * inner * 4 + 4 * chunk_rows * rows * inner
    feed_flops = 2 * chunk_rows * dim * units * 2
    layer_bytes = 2 * (4 * dim * inner + 2 * dim * units)
    lane_rows = pltpu.VMEM((lanes, dim), BF16)
    proj_rows = pltpu.VMEM((3 * inner, lanes), F32)
    low_rows = pltpu.VMEM((3 * inner, lanes), BF16)
    score_rows = pltpu.VMEM((heads, rows, lanes), F32)
    soft_rows = pltpu.VMEM((heads, lanes, lanes), BF16)
    head_rows = pltpu.VMEM((inner, lanes), BF16)
    row_spec = rows_spec(rows, dim)

    def forward(layer, first, qkv, qkv_layer, turn):
        piece_array = jax.ShapeDtypeStruct((pair * rows, dim), BF16)
        weights = [
            (merge_map, None),
            (ln_gain, None),
            (qkv, qkv_layer),
            (qk_gain, None),
            (w_out, layer),
            (w_up, layer),
            (b_up, None),
            (w_down, layer),
        ]
        turned = jax.ShapeDtypeStruct((layers, 3, inner, dim), BF16)
        return call(
            functools.partial(forward_kernel, layer, first, rows, turn),
            (counts, tokens) + tuple(w for w, _ in weights),
            [image_spec(1, slots, dim, first)] + [layer_spec(w, at) for w, at in weights],
            [piece_array] + [turned] * turn,
            [row_spec] + [whole_spec(turned)] * turn,
            [
                pltpu.VMEM((1, rows, dim), F32),
                lane_rows,
                proj_rows,
                low_rows,
                score_rows,
                soft_rows,
                head_rows,
                pltpu.VMEM((2, rows, units // 3), F32),
                pltpu.VMEM((rows, units), BF16),
            ],
            pair,
            2 * (head_flops + feed_flops),
            layer_bytes,
        )

    def feed_back(layer, top, first, pieces):
        weights = [(ln_gain, None), (b_down, None), (w_up, layer), (b_up, None), (w_down, layer)]
        outs = [
            row_array if top else jax.ShapeDtypeStruct((chunk_rows, dim), F32),
            row_array,
            row_array,
            row_array,
            unit_array,
            unit_array,
            jax.ShapeDtypeStruct((1, units), F32),
            jax.ShapeDtypeStruct((1, dim), F32),
        ] + [jax.ShapeDtypeStruct((size // pair, dim, pair * rows), BF16)] * 2
        block = rows_spec(pair * rows, dim)
        out_specs = [block] * 4 + [rows_spec(pair * rows, units)] * 2 + [whole_spec(outs[6]), whole_spec(outs[7])]
        out_specs += [image_spec(1, dim, pair * rows)] * 2
        operands = (tokens, cotangent, *pieces[0], *pieces[1], *pieces[2:])
        image_block = image_spec(pair, slots, dim, first // pair)
        specs = [image_block] * 2 + [whole_spec(one) for one in (*pieces[0], *pieces[1])] + [block] * len(pieces[2:])
        return call(
            functools.partial(feed_kernel, layer, top, first, rows, pair, size),
            (counts,) + operands + tuple(w for w, _ in weights),
            specs + [layer_spec(w, at) for w, at in weights],
            outs,
            out_specs,
            [pltpu.VMEM((2, rows, dim), F32)]
            + [pltpu.VMEM((2, pair * rows, units // 3), F32)] * 2
            + [pltpu.VMEM((pair * rows, dim), BF16)] * 2,
            size // pair,
            3 * feed_flops,
            layer_bytes + 12 * chunk_rows * dim * 2,
        )

    def heads_back(layer, top, first, turned, normed, low, d_feed, fed, begin=0, count=size):
        weights = [(turned, layer), (qk_gain, None), (w_out, layer)]
        streams = (normed, low, d_feed) + ((fed,) if top else ())
        row_array = jax.ShapeDtypeStruct((count * rows, dim), BF16)
        outs = ([row_array] if top else []) + [
            row_array,
            jax.ShapeDtypeStruct((count * rows, 4 * inner), BF16),
            jax.ShapeDtypeStruct((2 * head_dim, lanes), F32),
            jax.ShapeDtypeStruct((1, dim), F32),
        ]
        out_specs = ([row_spec] if top else []) + [
            row_spec,
            rows_spec(rows, 4 * inner),
            whole_spec(outs[-2]),
            whole_spec(outs[-1]),
        ]
        return call(
            functools.partial(heads_kernel, layer, top, first + begin, rows),
            (merge_map,) + streams + tuple(w for w, _ in weights),
            [whole_spec(merge_map)] + [rows_spec(rows, dim, begin)] * len(streams) + [layer_spec(w, at) for w, at in weights],
            outs,
            out_specs,
            [lane_rows] * 2
            + [proj_rows, low_rows, head_rows, score_rows, score_rows, soft_rows, soft_rows, head_rows]
            + [pltpu.VMEM((2 * inner, lanes), F32), low_rows, pltpu.VMEM((padded_to(heads, 8), lanes), F32), pltpu.VMEM((rows, dim), F32)],
            count,
            6 * head_flops,
            layer_bytes,
            prefetch=0,
        )

    def feed_grads(fed, before=()):
        groups = [[one[at] for one in fed] for at in (8, 9, 5, 4)]
        tile = units // 3
        tiles = units // tile
        flat = [array for group in groups for array in group]
        specs = [whole_spec(one) for one in groups[0] + groups[1]]
        specs += [pl.BlockSpec((chunk_rows, tile), lambda i: (0, jnp.minimum(i, tiles - 1)))] * len(fed)
        specs += [pl.BlockSpec((chunk_rows, tile), lambda i: (0, jnp.maximum(i - tiles, 0)))] * len(fed)
        return call(
            functools.partial(feed_weight_kernel, spans(groups)),
            (*flat, *before),
            specs + [pl.BlockSpec(memory_space=pl.ANY)] * len(before),
            jax.ShapeDtypeStruct((dim, before[0].shape[1] if before else 2 * units), BF16),
            pl.BlockSpec((dim, tile), lambda i: (0, i)),
            [],
            2 * tiles,
            2 * images * rows * dim * units * 2,
            2 * images * rows * (dim + units) * 2,
            prefetch=0,
            aliases={len(flat): 0} if before else None,
        )

    def heads_grads(fed, made, sums=()):
        columns = 4 * inner + (128 if sums else 0)
        groups = [[one[at] for one in fed] for at in (8, 9)] + [[one[1] for one in made], [ln_gain]] + list(sums)
        flat = [array for group in groups for array in group]
        specs = [whole_spec(one) for one in groups[0] + groups[1]]
        specs += [pl.BlockSpec((one.shape[0], inner), lambda i, *_: (0, i)) for one in groups[2]]
        specs += [whole_spec(one) for group in groups[3:] for one in group]
        return call(
            functools.partial(heads_weight_kernel, spans(groups)),
            (core_bit, *flat),
            specs,
            [jax.ShapeDtypeStruct((dim // 2, columns), BF16)] * 2,
            [pl.BlockSpec((dim // 2, columns), lambda i, *_: (0, 0))] * 2,
            [pltpu.VMEM((2, dim // 2, inner), BF16)]
            + ([pltpu.VMEM((padded_to(small_rows, 16), 128), F32)] if sums else []),
            4,
            2 * images * rows * dim * inner * 4,
            2 * images * rows * (dim + inner) * 4,
        )

    def unpack(kernel, halves, width, place, shapes, blocks, places, before):
        return call(
            kernel,
            (*halves, *before),
            [pl.BlockSpec((dim // 2, width), lambda i, *_: (0, place))]
            + [pl.BlockSpec((dim // 2, width), lambda i, *_: (halves[2].shape[0] // (dim // 2) - 1, place))]
            + [pl.BlockSpec(memory_space=pl.ANY)] * len(before),
            [jax.ShapeDtypeStruct(shape, F32) for shape in shapes],
            [pl.BlockSpec(block, place_of) for block, place_of in zip(blocks, places)],
            [],
            2,
            dim * width,
            6 * dim * width,
            aliases={at + 3: at for at in range(len(before))},
        )

    def row_half(i, bits):
        return lax.rem(i + bits[0], 2)

    def feed_unpack(halves, layer, before=()):
        return unpack(
            feed_unpack_kernel,
            halves,
            2 * units,
            0,
            ((layers, dim, units), (layers, units, dim)),
            ((1, dim // 2, units), (1, units, dim // 2)),
            (lambda i, bits: (layer, row_half(i, bits), 0), lambda i, bits: (layer, 0, row_half(i, bits))),
            before,
        )

    def heads_unpack(halves, layer, place=0, before=()):
        return unpack(
            heads_unpack_kernel,
            halves,
            halves[1].shape[1] - place * 4 * inner,
            place,
            ((layers, 3, dim, inner), (layers, inner, dim)),
            ((1, 3, dim // 2, inner), (1, inner, dim // 2)),
            (lambda i, bits: (layer, 0, row_half(i, bits), 0), lambda i, bits: (layer, 0, row_half(i, bits))),
            before,
        )

    tokens_slots = jnp.swapaxes(tokens, 0, 1)
    step_slots = 16
    slot_spec = pl.BlockSpec((step_slots, images, dim), lambda i, *_: (i, 0, 0))
    slot_array = jax.ShapeDtypeStruct((slots, images, dim), F32)
    chunk_spec = slots_spec(size, step_slots, dim)
    turned_rows = pltpu.VMEM((step_slots, images, dim), F32)

    def by_image(value):
        return value.reshape(value.shape[0] // rows, rows, dim)

    def paired(ours, theirs):
        return [by_image(one) for two in zip(ours, theirs) for one in two]

    def layer_output(before, ours, theirs, layer):
        pieces = paired(ours, theirs)
        return call(
            functools.partial(output_kernel, layer, len(ours)),
            (counts, before, *pieces, b_down),
            [slot_spec] + [slots_spec(one.shape[0], step_slots, dim) for one in pieces] + [whole_spec(b_down)],
            slot_array,
            slot_spec,
            [turned_rows],
            -(-slots // step_slots),
            10 * images * rows * dim,
            12 * images * rows * dim,
        )

    own, far = [], []
    qkv = w_qkv
    for first in range(0, images, pair):
        made = forward(0, first, tie(qkv, *own[-1:]) if own else qkv, 0 if own else None, not own)
        if not own:
            qkv = turned = made[1]
        own.append(made[0])
        far.append(others(made[0]))
    own_a, own_b = own[: len(own) // 2], own[len(own) // 2 :]
    far_a, far_b = far[: len(far) // 2], far[len(far) // 2 :]
    cotangent = tie(cotangent, own[-1])
    fed1_a = feed_back(1, True, 0, (own_a, far_a[:-1] + [tie(far_a[-1], own[-1])]))
    fed1_b = feed_back(1, True, size, (own_b, far_b[:-1] + [tie(far_b[-1], fed1_a[0])]))
    fed1 = (fed1_a, fed1_b)
    pack_feed1 = feed_grads(fed1)
    part_feed1 = lax.psum_scatter(pack_feed1, "wide", scatter_dimension=0, tiled=True)
    made1_a = heads_back(1, True, 0, turned, tie(fed1_a[1], pack_feed1), *fed1_a[2:4], fed1_a[0])
    far_grad_a = others(made1_a[1])
    made1_b = heads_back(1, True, size, turned, tie(fed1_b[1], made1_a[0]), *fed1_b[2:4], fed1_b[0])
    far_grad_b = others(made1_b[1])
    made1 = (made1_a[1:], made1_b[1:])
    heads1 = HalvingSum(*heads_grads(fed1, made1), "wide")
    fed0_a = feed_back(0, False, 0, (own_a, far_a, made1_a[1], tie(far_grad_a, heads1.sent)))
    heads1.step(fed0_a[0])
    first_out = layer_output(tie(tokens_slots, fed0_a[0], heads1.sent), own, far, 0)
    heads1.step(first_out)
    pack_feed1 = lax.all_gather(tie(part_feed1, heads1.sent, far_grad_b), "wide", axis=0, tiled=True)
    fed0_b = feed_back(0, False, size, (own_b, far_b, made1_b[1], tie(far_grad_b, heads1.sent)))
    fed0 = (fed0_a, fed0_b)
    far_next_a = others(tie(made1_a[0], first_out))
    far_next_b = others(tie(made1_b[0], first_out))
    heads1.step(fed0_b[0])
    pack_rest = feed_grads([tuple(one[:-1]) + (tie(one[-1], heads1.sent),) for one in fed0])
    heads1.step(pack_rest)
    made0, far_last = [], []
    for at in range(2):
        source = fed0[at]
        ready = (heads1.sent,) + tuple(one[0] for one in made0)
        made0.append(heads_back(0, False, at * size, turned, tie(source[1], *ready), *source[2:4], None))
        far_last.append(others(made0[-1][0]))
        if at == 0:
            pack_rest = tie(pack_rest, made0[0][0], far_next_a, far_next_b, pack_feed1, heads1.got)
    part_rest = lax.psum_scatter(pack_rest, "wide", scatter_dimension=0, tiled=True)
    heads1.step(made0[1][0])
    sums = []
    for fed, made in ((fed0, made0), (fed1, made1)):
        sums += [[one[3] for one in made], [one[2] for one in made], [one[7] for one in fed], [one[6] for one in fed]]
    sums[0][0] = tie(sums[0][0], heads1.sent)
    heads0 = HalvingSum(*heads_grads(fed0, made0, sums), "wide")
    heads0.step(far_last[0])
    second_out = layer_output(
        tie(first_out, heads0.sent), (made1_a[0], made1_b[0]), (far_next_a, far_next_b), 1
    )
    heads1.step(second_out)
    heads0.step(second_out, far_last[1])
    none = jnp.zeros((1,), jnp.int32)
    feed_outs = feed_unpack((none,) + (tie(pack_feed1, heads0.sent, heads1.sent),) * 2, 1)
    heads0.step(feed_outs[0])
    heads1.step(feed_outs[0])
    heads_outs = heads_unpack(heads1.halves(heads0.sent), 1)
    heads0.step(heads_outs[0])
    pack_rest = lax.all_gather(tie(part_rest, heads0.sent), "wide", axis=0, tiled=True)
    grad_tokens = call(
        functools.partial(tokens_kernel, len(made0)),
        (
            counts,
            tie(tokens_slots, heads0.sent),
            *paired([one[0] for one in made0], far_last),
            by_image(fed0_a[0]),
            by_image(fed0_b[0]),
            ln_gain,
        ),
        [slot_spec] + [chunk_spec] * (3 * len(made0)) + [whole_spec(ln_gain)],
        slot_array,
        slot_spec,
        [turned_rows] * 2,
        -(-slots // step_slots),
        10 * images * rows * dim,
        12 * images * rows * dim,
    )
    heads0.step(grad_tokens)
    while len(heads0.todo) > 1:
        heads0.step()
    rest = (none,) + (tie(pack_rest, heads0.sent),) * 2
    up, down = feed_unpack(rest, 0, feed_outs)
    halves0 = heads0.halves(up)
    small = jnp.where(halves0[0][0] == 0, *[half[:small_rows, 4 * inner :] for half in halves0[1:]])
    small = small.astype(F32).reshape(layers, -1)
    narrow_part = small[:, : dim + 2 * head_dim]
    if n_narrow == 2:
        narrow_part = narrow_part + lax.ppermute(narrow_part, "narrow", [(0, 1), (1, 0)])
    else:
        narrow_part = lax.psum(narrow_part, "narrow")
    g_b_down = small[:, dim + 2 * head_dim : 2 * dim + 2 * head_dim]
    g_b_up = small[:, 2 * dim + 2 * head_dim :]
    qkv, out = heads_unpack((halves0[0], tie(halves0[1], g_b_up), halves0[2]), 0, 0, heads_outs)
    return (
        jnp.swapaxes(first_out, 0, 1),
        jnp.swapaxes(second_out, 0, 1),
        jnp.swapaxes(grad_tokens, 0, 1),
        narrow_part[:, :dim],
        qkv,
        narrow_part[:, dim:].reshape(qk_gain.shape),
        out,
        up,
        g_b_up,
        down,
        g_b_down,
    )


def pick_body(*arrays):
    images, dim, inner, units = arrays[0].shape[0], arrays[0].shape[2], arrays[4].shape[-1], arrays[7].shape[-1]
    whole_heads = inner % arrays[5].shape[-1] == 0
    if whole_heads and images % 4 == 0 and units % inner == 0 and dim % 256 == 0 and inner % 128 == 0:
        return split_body(*arrays)
    return body(*arrays)


def solution(mesh):
    placed = (
        P("wide", None, None),
        P("wide", None),
        P("wide"),
        P(),
        P(None, None, None, "narrow"),
        P(),
        P(None, "narrow", None),
        P(None, None, "narrow"),
        P(None, "narrow"),
        P(None, "narrow", None),
        P(),
        P("wide", None, None),
    )
    return jax.shard_map(
        pick_body,
        mesh=mesh,
        in_specs=placed,
        out_specs=(
            P("wide", None, None),
            P("wide", None, None),
            P("wide", None, None),
            P(),
            P(None, None, None, "narrow"),
            P(),
            P(None, "narrow", None),
            P(None, None, "narrow"),
            P(None, "narrow"),
            P(None, "narrow", None),
            P(),
        ),
        check_vma=False,
    )
```

```python
import functools

import jax
import jax.numpy as jnp
from jax import lax
from jax.experimental import pallas as pl
from jax.experimental.pallas import tpu as pltpu
from jax.sharding import PartitionSpec as P


def shifted_2(value, axis, by):
    length = lax.axis_size(axis)
    pairs = [(i, i + by) for i in range(length) if 0 <= i + by < length]
    return lax.ppermute(value, axis, pairs)


def norm_rows(inputs, gain_row):
    centre = jnp.mean(inputs, axis=-1, keepdims=True)
    centered = inputs - centre
    inverse = lax.rsqrt(jnp.mean(centered * centered, axis=-1, keepdims=True) + 1e-06)
    normal = centered * inverse
    return (normal, inverse, normal * gain_row)


def norm_back(upstream, normal, inverse, gain_row):
    scaled = upstream * gain_row
    return inverse * (
        scaled
        - jnp.mean(scaled, axis=-1, keepdims=True)
        - normal * jnp.mean(scaled * normal, axis=-1, keepdims=True)
    )


def attend(normed_low, key_bias, qkv_full, out_full, qk_gains):
    head_dim = qk_gains.shape[-1]
    head_count = qkv_full.shape[-1] // head_dim
    qkv_heads = qkv_full.reshape(3, qkv_full.shape[1], head_count, head_dim)
    projected = jnp.einsum(
        "bsd,kdhe->kbhse", normed_low, qkv_heads, preferred_element_type=jnp.float32
    )
    q_normal, q_inverse, queries = norm_rows(projected[0], qk_gains[0])
    k_normal, k_inverse, keys_normed = norm_rows(projected[1], qk_gains[1])
    queries_low = queries.astype(jnp.bfloat16)
    keys_low = keys_normed.astype(jnp.bfloat16)
    values_low = projected[2].astype(jnp.bfloat16)
    score_scale = head_dim ** (-0.5)
    scores = jnp.einsum(
        "bhse,bhte->bhst", queries_low, keys_low, preferred_element_type=jnp.float32
    )
    logits = scores * score_scale + key_bias[:, None, None, :]
    shifted = jnp.exp(logits - jnp.max(logits, axis=-1, keepdims=True))
    softened = shifted / jnp.sum(shifted, axis=-1, keepdims=True)
    soft_low = softened.astype(jnp.bfloat16)
    mixed_low = jnp.einsum(
        "bhst,bhte->bhse", soft_low, values_low, preferred_element_type=jnp.float32
    ).astype(jnp.bfloat16)
    out_heads = out_full.reshape(head_count, head_dim, out_full.shape[-1])
    branch = jnp.einsum("bhse,hed->bsd", mixed_low, out_heads, preferred_element_type=jnp.float32)
    kept_parts = (
        q_normal,
        q_inverse,
        k_normal,
        k_inverse,
        queries_low,
        keys_low,
        values_low,
        softened,
        soft_low,
        mixed_low,
        qkv_heads,
        out_heads,
        score_scale,
    )
    return (branch, kept_parts)


def attend_back(normed_low, key_bias, qkv_full, out_full, qk_gains, grad_low):
    branch, kept_parts = attend(normed_low, key_bias, qkv_full, out_full, qk_gains)
    (
        q_normal,
        q_inverse,
        k_normal,
        k_inverse,
        queries_low,
        keys_low,
        values_low,
        softened,
        soft_low,
        mixed_low,
        qkv_heads,
        out_heads,
        score_scale,
    ) = kept_parts
    d_mixed = jnp.einsum(
        "bsd,hed->bhse", grad_low, out_heads, preferred_element_type=jnp.float32
    ).astype(jnp.bfloat16)
    g_out = jnp.einsum(
        "bhse,bsd->hed", mixed_low, grad_low, preferred_element_type=jnp.float32
    ).reshape(out_full.shape)
    d_soft = jnp.einsum("bhse,bhte->bhst", d_mixed, values_low, preferred_element_type=jnp.float32)
    row_dot = jnp.sum(softened * d_soft, axis=-1, keepdims=True)
    d_scores = (softened * (d_soft - row_dot) * score_scale).astype(jnp.bfloat16)
    d_queries = jnp.einsum(
        "bhst,bhte->bhse", d_scores, keys_low, preferred_element_type=jnp.float32
    )
    d_keys = jnp.einsum(
        "bhst,bhse->bhte", d_scores, queries_low, preferred_element_type=jnp.float32
    )
    d_values = jnp.einsum("bhst,bhse->bhte", soft_low, d_mixed, preferred_element_type=jnp.float32)
    g_gains = jnp.stack(
        [jnp.sum(d_queries * q_normal, axis=(0, 1, 2)), jnp.sum(d_keys * k_normal, axis=(0, 1, 2))]
    )
    d_projected = jnp.stack(
        [
            norm_back(d_queries, q_normal, q_inverse, qk_gains[0]),
            norm_back(d_keys, k_normal, k_inverse, qk_gains[1]),
            d_values,
        ]
    ).astype(jnp.bfloat16)
    g_qkv = jnp.einsum(
        "bsd,kbhse->kdhe", normed_low, d_projected, preferred_element_type=jnp.float32
    ).reshape(qkv_full.shape)
    d_normed = jnp.einsum(
        "kbhse,kdhe->bsd", d_projected, qkv_heads, preferred_element_type=jnp.float32
    )
    return (d_normed, g_qkv, g_out, g_gains)


def expand(normed_low, up_full, bias_full, down_full):
    pre_act = jnp.einsum(
        "bsd,df->bsf", normed_low, up_full, preferred_element_type=jnp.float32
    ) + bias_full.astype(jnp.float32)
    hidden, gelu_back = jax.vjp(jax.nn.gelu, pre_act)
    hidden_low = hidden.astype(jnp.bfloat16)
    branch = jnp.einsum("bsf,fd->bsd", hidden_low, down_full, preferred_element_type=jnp.float32)
    return (branch, hidden_low, gelu_back)


def expand_back(normed_low, up_full, bias_full, down_full, grad_low):
    branch, hidden_low, gelu_back = expand(normed_low, up_full, bias_full, down_full)
    d_hidden = jnp.einsum("bsd,fd->bsf", grad_low, down_full, preferred_element_type=jnp.float32)
    d_pre = gelu_back(d_hidden)[0].astype(jnp.bfloat16)
    g_bias = jnp.sum(d_pre, axis=(0, 1), dtype=jnp.float32)
    g_up = jnp.einsum("bsd,bsf->df", normed_low, d_pre, preferred_element_type=jnp.float32)
    g_down = jnp.einsum("bsf,bsd->fd", hidden_low, grad_low, preferred_element_type=jnp.float32)
    d_normed = jnp.einsum("bsf,df->bsd", d_pre, up_full, preferred_element_type=jnp.float32)
    return (d_normed, g_up, g_bias, g_down)


def body(
    tokens, merge_map, counts, ln_gain, w_qkv, qk_gain, w_out, w_up, b_up, w_down, b_down, cotangent
):
    pair_gap = lax.axis_size("narrow") // 2
    on_attention = lax.axis_index("narrow") < pair_gap
    layers = ln_gain.shape[0]
    col_half = w_qkv.shape[-1]
    unit_half = w_up.shape[-1]
    model_dim = tokens.shape[-1]
    slot_ids = jnp.arange(tokens.shape[1], dtype=jnp.int32)
    live_rows = slot_ids[None, :] < counts[:, None]
    row_weight = jnp.where(live_rows, 1.0, 0.0).astype(jnp.float32)[:, :, None]
    merged_sizes = jnp.sum(
        jnp.where(merge_map[:, :, None] == slot_ids[None, None, :], 1.0, 0.0), axis=1
    ).astype(jnp.float32)
    key_bias = jnp.where(live_rows, jnp.log(jnp.where(live_rows, merged_sizes, 1.0)), -1e30)
    attn_far = shifted_2((w_qkv, w_out), "narrow", -pair_gap)
    mlp_far = shifted_2((w_up, b_up, w_down), "narrow", pair_gap)

    def attention_weights(layer_at):
        qkv_full = jnp.concatenate([w_qkv[layer_at], attn_far[0][layer_at]], axis=-1)
        out_full = jnp.concatenate([w_out[layer_at], attn_far[1][layer_at]], axis=0)
        return (qkv_full, out_full)

    def feed_weights(layer_at):
        up_full = jnp.concatenate([mlp_far[0][layer_at], w_up[layer_at]], axis=-1)
        bias_full = jnp.concatenate([mlp_far[1][layer_at], b_up[layer_at]], axis=-1)
        down_full = jnp.concatenate([mlp_far[2][layer_at], w_down[layer_at]], axis=0)
        return (up_full, bias_full, down_full)

    current = tokens.astype(jnp.float32)
    layer_inputs = []
    outputs = []
    for layer_at in range(layers):
        normal, inverse, normed = norm_rows(current, ln_gain[layer_at])
        normed_low = normed.astype(jnp.bfloat16)

        def attention_forward():
            qkv_full, out_full = attention_weights(layer_at)
            return attend(normed_low, key_bias, qkv_full, out_full, qk_gain[layer_at])[0]

        def feed_forward():
            up_full, bias_full, down_full = feed_weights(layer_at)
            return expand(normed_low, up_full, bias_full, down_full)[0]

        partial_value = lax.cond(on_attention, attention_forward, feed_forward)
        layer_inputs.append(current)
        branch_total = lax.psum(partial_value, "narrow")
        current = row_weight * (current + branch_total + b_down[layer_at])
        outputs.append(current)
    grad_rows = cotangent.astype(jnp.float32)
    collected = []
    for layer_at in reversed(range(layers)):
        normal, inverse, normed = norm_rows(layer_inputs[layer_at], ln_gain[layer_at])
        normed_low = normed.astype(jnp.bfloat16)
        masked_grad = row_weight * grad_rows
        grad_low = masked_grad.astype(jnp.bfloat16)

        def attention_side():
            qkv_full, out_full = attention_weights(layer_at)
            d_normed, g_qkv, g_out, g_gains = attend_back(
                normed_low, key_bias, qkv_full, out_full, qk_gain[layer_at], grad_low
            )
            return (
                d_normed,
                g_gains,
                g_qkv,
                g_out,
                jnp.zeros((model_dim, 2 * unit_half), jnp.float32),
                jnp.zeros((2 * unit_half,), jnp.float32),
                jnp.zeros((2 * unit_half, model_dim), jnp.float32),
            )

        def feed_side():
            up_full, bias_full, down_full = feed_weights(layer_at)
            d_normed, g_up, g_bias, g_down = expand_back(
                normed_low, up_full, bias_full, down_full, grad_low
            )
            return (
                d_normed,
                jnp.zeros(qk_gain[layer_at].shape, jnp.float32),
                jnp.zeros((3, model_dim, 2 * col_half), jnp.float32),
                jnp.zeros((2 * col_half, model_dim), jnp.float32),
                g_up,
                g_bias,
                g_down,
            )

        returned = lax.cond(on_attention, attention_side, feed_side)
        d_normed, g_gains = (
            lax.psum(returned[0].astype(jnp.bfloat16), "narrow").astype(jnp.float32),
            lax.psum(returned[1].astype(jnp.bfloat16), "narrow").astype(jnp.float32),
        )
        g_ln = jnp.sum(d_normed * normal, axis=(0, 1))
        grad_rows = masked_grad + norm_back(d_normed, normal, inverse, ln_gain[layer_at])
        qkv_far, out_far = (
            shifted_2(returned[2][..., col_half:].astype(jnp.bfloat16), "narrow", pair_gap).astype(
                jnp.float32
            ),
            shifted_2(returned[3][col_half:].astype(jnp.bfloat16), "narrow", pair_gap).astype(
                jnp.float32
            ),
        )
        up_far, bias_far, down_far = (
            shifted_2(returned[4][:, :unit_half].astype(jnp.bfloat16), "narrow", -pair_gap).astype(
                jnp.float32
            ),
            shifted_2(returned[5][:unit_half].astype(jnp.bfloat16), "narrow", -pair_gap).astype(
                jnp.float32
            ),
            shifted_2(returned[6][:unit_half].astype(jnp.bfloat16), "narrow", -pair_gap).astype(
                jnp.float32
            ),
        )
        own_qkv = jnp.where(on_attention, returned[2][..., :col_half], qkv_far)
        own_out = jnp.where(on_attention, returned[3][:col_half], out_far)
        own_up = jnp.where(on_attention, up_far, returned[4][:, unit_half:])
        own_bias = jnp.where(on_attention, bias_far, returned[5][unit_half:])
        own_down = jnp.where(on_attention, down_far, returned[6][unit_half:])
        g_bdown = jnp.sum(masked_grad, axis=(0, 1))
        shards = (own_qkv, own_out, own_up, own_bias, own_down, g_ln, g_gains, g_bdown)
        collected.append(shards)
    collected = collected[::-1]
    stacked = tuple(
        (jnp.stack([element[position] for element in collected]) for position in range(8))
    )
    stacked = (
        lax.psum(stacked[0].astype(jnp.bfloat16), "wide").astype(jnp.float32),
        lax.psum(stacked[1].astype(jnp.bfloat16), "wide").astype(jnp.float32),
        lax.psum(stacked[2].astype(jnp.bfloat16), "wide").astype(jnp.float32),
        lax.psum(stacked[3].astype(jnp.bfloat16), "wide").astype(jnp.float32),
        lax.psum(stacked[4].astype(jnp.bfloat16), "wide").astype(jnp.float32),
        lax.psum(stacked[5].astype(jnp.bfloat16), "wide").astype(jnp.float32),
        lax.psum(stacked[6].astype(jnp.bfloat16), "wide").astype(jnp.float32),
        lax.psum(stacked[7].astype(jnp.bfloat16), "wide").astype(jnp.float32),
    )
    return (
        outputs[0],
        outputs[-1],
        grad_rows,
        stacked[5],
        stacked[0],
        stacked[6],
        stacked[1],
        stacked[2],
        stacked[3],
        stacked[4],
        stacked[7],
    )


EPS = 1e-06
F32 = jnp.float32
BF16 = jnp.bfloat16
COST_SCALE = 3
AG_AFTER = 1
VMEM_BYTES = 60 * 1024 * 1024
GELU_IN = 0.7978845608028654
GELU_CUBE = 0.044715


def padded_to(length, step):
    return -(-length // step) * step


def dot(a, b):
    return jnp.dot(a, b, preferred_element_type=F32)


def dot_nt(a, b):
    return lax.dot_general(a, b, (((1,), (1,)), ((), ())), preferred_element_type=F32)


def normal_rows(x):
    centered = x - jnp.mean(x, axis=-1, keepdims=True)
    inverse = lax.rsqrt(jnp.mean(centered * centered, axis=-1, keepdims=True) + EPS)
    return centered * inverse, inverse


def back_rows(upstream, normal, inverse, gain):
    scaled = upstream * gain
    return inverse * (
        scaled
        - jnp.mean(scaled, axis=-1, keepdims=True)
        - normal * jnp.mean(scaled * normal, axis=-1, keepdims=True)
    )


def live_of(count, rows):
    return lax.broadcasted_iota(jnp.int32, (rows, 1), 0) < count


def fill_rows(source, wide_rows):
    slots = source.shape[0]
    edge = slots // 8 * 8
    wide_rows[edge:, :] = jnp.zeros((wide_rows.shape[0] - edge, wide_rows.shape[1]), F32)
    wide_rows[:slots, :] = source[...].astype(F32)


def head_norm(x):
    centered = x - jnp.mean(x, axis=1, keepdims=True)
    inverse = lax.rsqrt(jnp.mean(centered * centered, axis=1, keepdims=True) + EPS)
    return centered * inverse, inverse


def head_back(upstream, normal, inverse, gain):
    scaled = upstream * gain
    return inverse * (
        scaled
        - jnp.mean(scaled, axis=1, keepdims=True)
        - normal * jnp.mean(scaled * normal, axis=1, keepdims=True)
    )


def key_sizes(patch_ref, image, rows):
    slots = patch_ref.shape[1]
    slot = lax.broadcasted_iota(jnp.int32, (rows, slots), 0)
    named = jnp.where(patch_ref[pl.ds(image, 1), :] == slot, 1.0, 0.0)
    return jnp.sum(named, axis=-1, keepdims=True)


def head_gains(qk_gain, layer):
    both = qk_gain[layer]
    return [jnp.broadcast_to(both[at : at + 1, :], (8, both.shape[1])).T[:, :1] for at in range(2)]


def project(turned, normed, gains, proj, lows):
    inner, head_dim = proj.shape[0] // 3, gains[0].shape[0]
    heads, lanes = inner // head_dim, proj.shape[1]
    proj[...] = dot_nt(turned, normed)
    inverses = []
    for part in range(2):
        here = slice(part * inner, (part + 1) * inner)
        normal, inverse = head_norm(proj[here, :].reshape(heads, head_dim, lanes))
        inverses.append(inverse)
        proj[here, :] = normal.reshape(inner, lanes)
        low = (normal * gains[part][None]).astype(BF16)
        if part == 0:
            low = (low.astype(F32) * head_dim ** (-0.5)).astype(BF16)
        lows[here, :] = low.reshape(inner, lanes)
    lows[2 * inner :, :] = proj[2 * inner :, :].astype(BF16)
    return inverses


def soften(lows, sizes, scores, soft):
    heads, rows, strip = scores.shape[0], scores.shape[1], 16
    inner = lows.shape[0] // 3
    head_dim = inner // heads
    for head in range(heads):
        at = head * head_dim
        keys = lows[inner + at : inner + at + head_dim, :]
        scores[head] = dot(keys.T[:rows], lows[at : at + head_dim, :])
    over = []
    for head in range(heads):
        total = jnp.zeros((8, scores.shape[2]), F32)
        for at in range(0, rows, strip):
            raised = jnp.exp(scores[head, at : at + strip, :]) * sizes[at : at + strip, :]
            scores[head, at : at + strip, :] = raised
            soft[head, at : at + strip, :] = raised.astype(BF16)
            total = total + (raised[:8] + raised[8:])
        over.append(1.0 / jnp.sum(total, axis=0, keepdims=True))
    return over


def forward_kernel(layer, first, rows, turn, counts, *refs):
    tok, patch, gain, w_qkv, qk_gain, w_out, w_up, b_up, w_down, out = refs[:10]
    if turn:
        turned = refs[10]
        refs = refs[11:]
    else:
        turned = w_qkv
        refs = refs[10:]
    wide_rows, normed, proj, lows, scores, soft, mixed, pre_rows, hidden = refs
    step = pl.program_id(0)
    inner = w_out.shape[1]

    @pl.when(step == 0)
    def _():
        normed[...] = jnp.zeros(normed.shape, BF16)
        soft[...] = jnp.zeros(soft.shape, BF16)
        if turn:
            for at in range(w_qkv.shape[0]):
                for part in range(3):
                    turned[at, part] = w_qkv[at, part].T

    fill_rows(tok.at[0], wide_rows.at[0])
    strip = 16
    for at in range(0, rows, strip):
        x = jnp.where(live_of(counts[first + step] - at, strip), wide_rows[0, at : at + strip, :], 0.0)
        normed[at : at + strip, :] = (normal_rows(x)[0] * gain[layer : layer + 1, :]).astype(BF16)
    gains = head_gains(qk_gain, layer)
    head_dim = gains[0].shape[0]
    project(turned[0].reshape(3 * inner, turned.shape[3]), normed[...], gains, proj, lows)
    over = soften(lows, key_sizes(patch, first + step, rows), scores, soft)
    for head in range(inner // head_dim):
        at = head * head_dim
        values = lows[2 * inner + at : 2 * inner + at + head_dim, :]
        mixed[at : at + head_dim, :] = (dot(values, soft[head]) * over[head]).astype(BF16)
    bias = b_up[...].astype(F32)[layer : layer + 1, :]
    units = w_up.shape[2]
    tile = units // 3
    for slot, at in enumerate(range(0, units, tile)):
        pre_rows[slot % 2] = dot(normed[:rows, :], w_up[0, :, at : at + tile])
        for row in range(0, rows, strip):
            pre = pre_rows[slot % 2, row : row + strip, :] + bias[:, at : at + tile]
            bent = jnp.tanh(pre * (GELU_IN + (GELU_IN * GELU_CUBE) * (pre * pre)))
            hidden[row : row + strip, at : at + tile] = (pre * (0.5 + 0.5 * bent)).astype(BF16)
    out[...] = (dot(mixed[...].T[:rows], w_out[0]) + dot(hidden[...], w_down[0])).astype(BF16)


def feed_kernel(layer, top, first, rows, per_step, tok_images, counts, *refs):
    refs = list(refs)
    tok, cot = refs[:2]
    steps = (tok_images + per_step - 1) // per_step
    own_pieces, far_pieces = refs[2 : 2 + steps], refs[2 + steps : 2 + 2 * steps]
    refs = refs[2 + 2 * steps :]
    if not top:
        own_grad, far_grad = refs[:2]
        refs = refs[2:]
    gain, b_prev, w_up, b_up, w_down = refs[:5]
    refs = refs[5:]
    extra = refs[0]
    refs = refs[1:]
    normed, low, d_feed, hidden_out, d_pre_out, sum_up, sum_down, normed_t, low_t, wide_rows, pre_rows, d_rows, own, far = refs
    step = pl.program_id(0)
    for at in range(steps):

        @pl.when(step == at)
        def _(at=at):
            own[...] = own_pieces[at][...]
            far[...] = far_pieces[at][...]


    @pl.when(step == 0)
    def _():
        sum_up[...] = jnp.zeros(sum_up.shape, F32)
        sum_down[...] = jnp.zeros(sum_down.shape, F32)

    strip = 16
    for j in range(per_step):
        count = counts[first + step * per_step + j]
        fill_rows(tok.at[j], wide_rows.at[0])
        fill_rows(cot.at[j], wide_rows.at[1])
        total = jnp.zeros((8, tok.shape[2]), F32)
        for at in range(0, rows, strip):
            block = slice(j * rows + at, j * rows + at + strip)
            live = live_of(count - at, strip)
            x0 = jnp.where(live, wide_rows[0, at : at + strip, :], 0.0)
            branch = own[block, :].astype(F32) + far[block, :].astype(F32)
            x1 = jnp.where(live, x0 + branch + b_prev[:1, :], 0.0)
            grad = jnp.where(live, wide_rows[1, at : at + strip, :], 0.0)
            if top:
                x = x1
            else:
                x = x0
                normal, inverse = normal_rows(x1)
                d_normed = own_grad[block, :].astype(F32) + far_grad[block, :].astype(F32)
                grad = grad + back_rows(d_normed, normal, inverse, gain[layer + 1 : layer + 2, :])
                extra[block, :] = grad
            normed[block, :] = (normal_rows(x)[0] * gain[layer : layer + 1, :]).astype(BF16)
            low[block, :] = grad.astype(BF16)
            total = total + (grad[:8] + grad[8:])
        sum_down[...] += jnp.sum(total, axis=0, keepdims=True)
    normed_t[0] = normed[...].T
    low_t[0] = low[...].T
    bias = b_up[...].astype(F32)[layer : layer + 1, :]
    units = w_up.shape[2]
    tile = units // 3
    for slot, at in enumerate(range(0, units, tile)):
        part = slice(at, at + tile)
        pre_rows[slot % 2] = dot(normed[...], w_up[0, :, part])
        d_rows[slot % 2] = dot_nt(low[...], w_down[0, part, :])
        total = jnp.zeros((8, tile), F32)
        for row in range(0, per_step * rows, strip):
            block = slice(row, row + strip)
            pre = pre_rows[slot % 2, block, :] + bias[:, part]
            square = pre * pre
            bent = jnp.tanh(pre * (GELU_IN + (GELU_IN * GELU_CUBE) * square))
            half = 0.5 + 0.5 * bent
            hidden_out[block, part] = (pre * half).astype(BF16)
            steep = GELU_IN + (3 * GELU_IN * GELU_CUBE) * square
            slope = half + (0.5 * pre) * ((1.0 - bent * bent) * steep)
            d_pre = (d_rows[slot % 2, block, :] * slope).astype(BF16)
            d_pre_out[block, part] = d_pre
            d_pre = d_pre.astype(F32)
            total = total + (d_pre[:8] + d_pre[8:])
        sum_up[:, part] += jnp.sum(total, axis=0, keepdims=True)
    d_feed[...] = dot_nt(d_pre_out[...], w_up[0]).astype(BF16)
    if top:
        extra[...] = dot(hidden_out[...], w_down[0]).astype(BF16)


def heads_kernel(layer, top, first, rows, patch, normed_in, low_in, d_feed, *refs):
    refs = list(refs)
    if top:
        fed = refs[0]
        refs = refs[1:]
    w_qkv, qk_gain, w_out = refs[:3]
    refs = refs[3:]
    if top:
        out = refs[0]
        refs = refs[1:]
    d_normed, rights, sum_gain, sum_row = refs[:4]
    normed, low, proj, lows, d_mixed, scores, slopes, soft, d_soft, mixed, d_heads, d_proj, row_dots, total = refs[4:]
    step = pl.program_id(0)
    inner = w_out.shape[1]
    gains = head_gains(qk_gain, layer)
    head_dim = gains[0].shape[0]

    @pl.when(step == 0)
    def _():
        normed[...] = jnp.zeros(normed.shape, BF16)
        low[...] = jnp.zeros(low.shape, BF16)
        soft[...] = jnp.zeros(soft.shape, BF16)
        d_soft[...] = jnp.zeros(d_soft.shape, BF16)
        sum_gain[...] = jnp.zeros(sum_gain.shape, F32)
        sum_row[...] = jnp.zeros(sum_row.shape, F32)

    normed[:rows, :] = normed_in[...]
    low[:rows, :] = low_in[...]
    turned = w_qkv[0].reshape(3 * inner, w_qkv.shape[3])
    heads, lanes = inner // head_dim, proj.shape[1]
    inverses = project(turned, normed[...], gains, proj, lows)
    d_mixed[...] = dot_nt(w_out[0], low[...]).astype(BF16)
    over = soften(lows, key_sizes(patch, first + step, rows), scores, soft)
    for head in range(heads):
        here = slice(head * head_dim, (head + 1) * head_dim)
        mixed_here = dot(lows[2 * inner + here.start : 2 * inner + here.stop, :], soft[head]) * over[head]
        mixed[here, :] = mixed_here.astype(BF16)
        d_mixed_here = d_mixed[here, :].astype(F32)
        row_dots[head : head + 1, :] = jnp.sum(d_mixed_here * mixed_here, axis=0, keepdims=True) * over[head]
        d_mixed[here, :] = (d_mixed_here * over[head]).astype(BF16)
    for head in range(heads):
        here = slice(head * head_dim, (head + 1) * head_dim)
        values = lows[2 * inner + here.start : 2 * inner + here.stop, :]
        slopes[head] = dot(values.T[:rows], d_mixed[here, :])
    for head in range(heads):
        for row in range(0, rows, 16):
            block = slice(row, row + 16)
            slope = slopes[head, block, :] - row_dots[head : head + 1, :]
            d_soft[head, block, :] = (scores[head, block, :] * slope).astype(BF16)
    for head in range(heads):
        here = slice(head * head_dim, (head + 1) * head_dim)
        keys = slice(inner + here.start, inner + here.stop)
        values = slice(2 * inner + here.start, 2 * inner + here.stop)
        d_heads[here, :] = dot(lows[keys, :], d_soft[head]) * head_dim ** (-0.5)
        d_heads[keys, :] = dot_nt(lows[here, :], d_soft[head])
        d_proj[values, :] = dot_nt(d_mixed[here, :], soft[head]).astype(BF16)
    for part in range(2):
        here = slice(part * inner, (part + 1) * inner)
        normal = proj[here, :].reshape(heads, head_dim, lanes)
        upstream = d_heads[here, :].reshape(heads, head_dim, lanes)
        sum_gain[part * head_dim : (part + 1) * head_dim, :] += jnp.sum(upstream * normal, axis=0)
        back = head_back(upstream, normal, inverses[part], gains[part][None])
        d_proj[here, :] = back.reshape(inner, lanes).astype(BF16)
    mixed_rows = mixed[...].T[:rows]
    rights[:, 3 * inner :] = mixed_rows
    if top:
        out[...] = (fed[...].astype(F32) + dot(mixed_rows, w_out[0])).astype(BF16)
    for part in range(3):
        rights[:, part * inner : (part + 1) * inner] = d_proj[part * inner : (part + 1) * inner, :].T[:rows]
    total[...] = dot(rights[:, : 3 * inner], turned)
    row_sum = jnp.zeros((8, total.shape[1]), F32)
    for row in range(0, rows, 16):
        block = slice(row, row + 16)
        d_here = total[block, :] + d_feed[block, :].astype(F32)
        d_normed[block, :] = d_here.astype(BF16)
        d_here = d_here * normed_in[block, :].astype(F32)
        row_sum = row_sum + (d_here[:8] + d_here[8:])
    sum_row[...] += jnp.sum(row_sum, axis=0, keepdims=True)


def live_slots(counts, shape):
    slot = lax.broadcasted_iota(jnp.int32, shape, 0) + pl.program_id(0) * shape[0]
    image = lax.broadcasted_iota(jnp.int32, shape, 1)
    count = jnp.zeros(shape, jnp.int32)
    for at in range(shape[1]):
        count = jnp.where(image == at, counts[at], count)
    return slot < count


def chunk_sums(refs, sums):
    image = 0
    for own, far in refs:
        for at in range(own.shape[0]):
            sums[:, image, :] = own[at].astype(F32) + far[at].astype(F32)
            image += 1


def output_kernel(layer, chunks, counts, before, *refs):
    pairs = [(refs[2 * at], refs[2 * at + 1]) for at in range(chunks)]
    bias, out, sums = refs[2 * chunks :]
    live = live_slots(counts, out.shape[:2] + (1,))
    chunk_sums(pairs, sums)
    for at in range(0, out.shape[0], 2):
        part = slice(at, at + 2)
        total = before[part].astype(F32) + sums[part] + bias[layer : layer + 1, :]
        out[part] = jnp.where(live[part], total, 0.0)


def tokens_kernel(chunks, counts, tok, *refs):
    pairs = [(refs[2 * at], refs[2 * at + 1]) for at in range(chunks)]
    grads = refs[2 * chunks : -4]
    gain, out, sums, turned = refs[-4:]
    live = live_slots(counts, out.shape[:2] + (1,))
    chunk_sums(pairs, sums)
    image = 0
    for grad in grads:
        for at in range(grad.shape[0]):
            turned[:, image, :] = grad[at]
            image += 1
    for at in range(0, out.shape[0], 2):
        part = slice(at, at + 2)
        normal, inverse = normal_rows(jnp.where(live[part], tok[part].astype(F32), 0.0))
        total = turned[part] + back_rows(sums[part], normal, inverse, gain[:1, :])
        out[part] = jnp.where(live[part], total, 0.0)


def weight_tile(lefts, rights):
    total, first, at = None, 0, 0
    for left in lefts:
        for block in range(left.shape[0]):
            rows = left.shape[2]
            if first == rights[at].shape[0]:
                first, at = 0, at + 1
            term = dot(left[block], rights[at][first : first + rows, :])
            total = term if total is None else total + term
            first += rows
    return total.astype(BF16)


def store_tile(bit, tile, both, kept, sent, columns=slice(None)):
    if sent is None:
        kept[:, columns] = tile
        return
    both[:, :, : tile.shape[1]] = tile.reshape(2, -1, tile.shape[1])
    kept[:, columns] = both[bit, :, : tile.shape[1]]
    sent[:, columns] = both[1 - bit, :, : tile.shape[1]]


def feed_weight_kernel(counts, *refs):
    normed_t, low_t, d_pre, hidden = [refs[first:last] for first, last in counts]
    out = refs[-1]
    half = pl.num_programs(0) // 2

    @pl.when(pl.program_id(0) < half)
    def _():
        out[...] = weight_tile(normed_t, d_pre)

    @pl.when(pl.program_id(0) >= half)
    def _():
        out[...] = weight_tile(low_t, hidden)


def heads_weight_kernel(counts, bits, *refs):
    normed_t, low_t, rights, gain, *sums = [refs[first:last] for first, last in counts]
    if sums:
        kept, sent, both, lined = refs[-4:]
    else:
        kept, sent, both = refs[-3:]
    inner = rights[0].shape[1]
    for part in range(4):

        @pl.when(pl.program_id(0) == part)
        def _(part=part):
            lefts = low_t if part == 3 else normed_t
            columns = slice(part * inner, (part + 1) * inner)
            store_tile(bits[0], weight_tile(lefts, rights), both, kept, sent, columns)

    if not sums:
        return

    @pl.when(pl.program_id(0) == 0)
    def _():
        lined[...] = jnp.zeros(lined.shape, F32)
        row = 0
        for layer in range(len(sums) // 4):
            s_row, s_gain, s_down, s_up = [
                functools.reduce(lambda a, b: a + b, [one[...] for one in group])
                for group in sums[4 * layer : 4 * layer + 4]
            ]
            s_row = s_row / gain[0][layer : layer + 1, :]
            s_gain = jnp.sum(s_gain.T, axis=0, keepdims=True)
            for values in (s_row, s_gain, s_down, s_up):
                for at in range(0, values.shape[1], 128):
                    lined[row : row + 1, :] = values[:, at : at + 128]
                    row += 1
        none = jnp.zeros((kept.shape[0], 128), BF16)
        kept[:, 4 * inner :] = none
        sent[:, 4 * inner :] = none
        small = lined[...].astype(BF16)

        @pl.when(bits[0] == 0)
        def _():
            kept[: lined.shape[0], 4 * inner :] = small

        @pl.when(bits[0] == 1)
        def _():
            sent[: lined.shape[0], 4 * inner :] = small


def halve_kernel(bits, kept, got, *refs):
    total = (kept[...].astype(F32) + got[...].astype(F32)).astype(BF16)
    if len(refs) == 1:
        refs[0][...] = total
        return
    left, sent, both = refs
    both[...] = total.reshape(both.shape)
    left[...] = both[bits[0]]
    sent[...] = both[1 - bits[0]]


def join_kernel(bits, own, got, out):
    out[bits[0]] = own[...]
    out[1 - bits[0]] = got[...]


def feed_unpack_kernel(bits, own, got, *refs):
    up, down = refs[-2:]
    units = up.shape[2]

    def place(pack):
        up[0] = pack[:, :units].astype(F32)
        down[0] = pack[:, units : 2 * units].astype(F32).T

    pl.when(pl.program_id(0) == 0)(lambda: place(own))
    pl.when(pl.program_id(0) == 1)(lambda: place(got))


def heads_unpack_kernel(bits, own, got, *refs):
    qkv, out = refs[-2:]
    inner = qkv.shape[3]

    def place(pack):
        for at in range(3):
            qkv[0, at] = pack[:, at * inner : (at + 1) * inner].astype(F32)
        out[0] = pack[:, 3 * inner : 4 * inner].astype(F32).T

    pl.when(pl.program_id(0) == 0)(lambda: place(own))
    pl.when(pl.program_id(0) == 1)(lambda: place(got))


def spans(groups):
    ends = []
    for group in groups:
        first = ends[-1][1] if ends else 0
        ends.append((first, first + len(group)))
    return tuple(ends)


def whole_spec(array):
    return pl.BlockSpec(array.shape, lambda i, *_: (0,) * array.ndim)


def layer_spec(array, layer):
    if layer is None:
        return whole_spec(array)
    return pl.BlockSpec((1,) + array.shape[1:], lambda i, *_: (layer,) + (0,) * (array.ndim - 1))


def rows_spec(rows, columns, first=0):
    return pl.BlockSpec((rows, columns), lambda i, *_: (first + i, 0))


def image_spec(images, slots, columns, first=0):
    return pl.BlockSpec((images, slots, columns), lambda i, *_: (first + i, 0, 0))


def slots_spec(images, slots, columns):
    return pl.BlockSpec((images, slots, columns), lambda i, *_: (0, i, 0))


def call(kernel, operands, specs, shapes, out_specs, scratch, grid, flops, moved, prefetch=1, aliases=None):
    return pl.pallas_call(
        kernel,
        grid_spec=pltpu.PrefetchScalarGridSpec(
            num_scalar_prefetch=prefetch,
            grid=(grid,),
            in_specs=specs,
            out_specs=out_specs,
            scratch_shapes=scratch,
        ),
        out_shape=shapes,
        compiler_params=pltpu.CompilerParams(
            dimension_semantics=("arbitrary",), vmem_limit_bytes=VMEM_BYTES
        ),
        cost_estimate=pl.CostEstimate(flops=flops // COST_SCALE, bytes_accessed=moved // COST_SCALE, transcendentals=0),
        input_output_aliases=aliases or {},
    )(*operands)


def bit_steps(axis):
    size = lax.axis_size(axis)
    bits = size.bit_length() - 1
    here = lax.axis_index(axis)
    steps = []
    for step in range(bits):

        def bit_of(place, step=step):
            if bits < 3 or step not in (1, 2):
                return 1 << step
            return 1 << (step if place % 2 == 0 else 3 - step)
        pairs = [(place, place ^ bit_of(place)) for place in range(size)]
        bit = (here >> step) & 1
        if bits >= 3 and step in (1, 2):
            bit = jnp.where(here % 2 == 0, bit, (here >> (3 - step)) & 1)
        steps.append((pairs, bit))
    return steps


def tie(value, *others):
    return lax.optimization_barrier((value,) + others)[0]


def column_tiles(width):
    return 3 if width % 3 == 0 and width >= 3072 else 1


def halve(bit, kept, got, last):
    rows, width = kept.shape
    tiles = column_tiles(width)
    tile = width // tiles
    out_rows = rows if last else rows // 2
    spec = pl.BlockSpec((out_rows, tile), lambda i, *_: (0, i))
    whole = pl.BlockSpec((rows, tile), lambda i, *_: (0, i))
    count = 1 if last else 2
    return call(
        halve_kernel,
        (bit, kept, got),
        [whole] * 2,
        [jax.ShapeDtypeStruct((out_rows, width), BF16)] * count,
        [spec] * count,
        [] if last else [pltpu.VMEM((2, out_rows, tile), BF16)],
        tiles,
        rows * width,
        6 * rows * width,
    )


def join(bit, own, got):
    rows, width = own.shape
    tiles = column_tiles(width)
    tile = width // tiles
    spec = pl.BlockSpec((rows, tile), lambda i, *_: (0, i))
    out = call(
        join_kernel,
        (bit, own, got),
        [spec] * 2,
        jax.ShapeDtypeStruct((2, rows, width), BF16),
        pl.BlockSpec((2, rows, tile), lambda i, *_: (0, 0, i)),
        [],
        tiles,
        rows * width,
        8 * rows * width,
    )
    return out.reshape(2 * rows, width)


class HalvingSum:
    def __init__(self, kept, sent, axis):
        self.axis, self.value = axis, kept
        steps = bit_steps(axis)
        self.bits = [jnp.reshape(bit, (1,)).astype(jnp.int32) for _, bit in steps]
        self.pairs = [pairs for pairs, _ in steps]
        self.todo = [(True, at) for at in range(len(steps))] + [(False, at) for at in reversed(range(len(steps)))]
        self.begin(sent)

    def begin(self, sent):
        self.sent = sent
        self.got = lax.ppermute(sent, self.axis, self.pairs[self.todo[0][1]])

    def step(self, *after):
        if len(self.todo) == 1:
            return
        halving, at = self.todo.pop(0)
        got = tie(self.got, *after) if after else self.got
        if halving:
            last = at + 1 == len(self.bits)
            made = halve(self.bits[0 if last else at + 1], self.value, got, last)
            self.value = made[0]
            self.begin(made[-1])
        else:
            self.value = join(self.bits[at], self.value, got)
            self.begin(self.value)

    def halves(self, *after):
        while len(self.todo) > 1:
            self.step()
        return self.bits[0], self.value, tie(self.got, *after) if after else self.got


def split_body(tokens, merge_map, counts, ln_gain, w_qkv, qk_gain, w_out, w_up, b_up, w_down, b_down, cotangent):
    images, slots, dim = tokens.shape
    layers, inner = w_out.shape[:2]
    units = w_up.shape[2]
    head_dim = qk_gain.shape[-1]
    heads = inner // head_dim
    rows, lanes = padded_to(slots, 16), padded_to(slots, 128)
    n_narrow = lax.axis_size("narrow")
    size = images // 2
    firsts = (0, size)
    pair = 2 if size % 2 == 0 else 1
    chunk_rows = size * rows
    core_bit = jnp.reshape(lax.axis_index("wide") & 1, (1,)).astype(jnp.int32)
    small_rows = layers * (2 * dim + 2 * head_dim + units) // 128

    def others(value):
        if n_narrow == 2:
            return lax.ppermute(value, "narrow", [(0, 1), (1, 0)])
        wide_value = value.astype(F32)
        return (lax.psum(wide_value, "narrow") - wide_value).astype(BF16)

    row_array = jax.ShapeDtypeStruct((chunk_rows, dim), BF16)
    unit_array = jax.ShapeDtypeStruct((chunk_rows, units), BF16)
    head_flops = 2 * chunk_rows * dim * inner * 4 + 4 * chunk_rows * rows * inner
    feed_flops = 2 * chunk_rows * dim * units * 2
    layer_bytes = 2 * (4 * dim * inner + 2 * dim * units)
    lane_rows = pltpu.VMEM((lanes, dim), BF16)
    proj_rows = pltpu.VMEM((3 * inner, lanes), F32)
    low_rows = pltpu.VMEM((3 * inner, lanes), BF16)
    score_rows = pltpu.VMEM((heads, rows, lanes), F32)
    soft_rows = pltpu.VMEM((heads, lanes, lanes), BF16)
    head_rows = pltpu.VMEM((inner, lanes), BF16)
    row_spec = rows_spec(rows, dim)

    def forward(layer, first, qkv, qkv_layer, turn):
        piece_array = jax.ShapeDtypeStruct((pair * rows, dim), BF16)
        weights = [
            (merge_map, None),
            (ln_gain, None),
            (qkv, qkv_layer),
            (qk_gain, None),
            (w_out, layer),
            (w_up, layer),
            (b_up, None),
            (w_down, layer),
        ]
        turned = jax.ShapeDtypeStruct((layers, 3, inner, dim), BF16)
        return call(
            functools.partial(forward_kernel, layer, first, rows, turn),
            (counts, tokens) + tuple(w for w, _ in weights),
            [image_spec(1, slots, dim, first)] + [layer_spec(w, at) for w, at in weights],
            [piece_array] + [turned] * turn,
            [row_spec] + [whole_spec(turned)] * turn,
            [
                pltpu.VMEM((1, rows, dim), F32),
                lane_rows,
                proj_rows,
                low_rows,
                score_rows,
                soft_rows,
                head_rows,
                pltpu.VMEM((2, rows, units // 3), F32),
                pltpu.VMEM((rows, units), BF16),
            ],
            pair,
            2 * (head_flops + feed_flops),
            layer_bytes,
        )

    def feed_back(layer, top, first, pieces):
        weights = [(ln_gain, None), (b_down, None), (w_up, layer), (b_up, None), (w_down, layer)]
        outs = [
            row_array if top else jax.ShapeDtypeStruct((chunk_rows, dim), F32),
            row_array,
            row_array,
            row_array,
            unit_array,
            unit_array,
            jax.ShapeDtypeStruct((1, units), F32),
            jax.ShapeDtypeStruct((1, dim), F32),
        ] + [jax.ShapeDtypeStruct((size // pair, dim, pair * rows), BF16)] * 2
        block = rows_spec(pair * rows, dim)
        out_specs = [block] * 4 + [rows_spec(pair * rows, units)] * 2 + [whole_spec(outs[6]), whole_spec(outs[7])]
        out_specs += [image_spec(1, dim, pair * rows)] * 2
        operands = (tokens, cotangent, *pieces[0], *pieces[1], *pieces[2:])
        image_block = image_spec(pair, slots, dim, first // pair)
        specs = [image_block] * 2 + [whole_spec(one) for one in (*pieces[0], *pieces[1])] + [block] * len(pieces[2:])
        return call(
            functools.partial(feed_kernel, layer, top, first, rows, pair, size),
            (counts,) + operands + tuple(w for w, _ in weights),
            specs + [layer_spec(w, at) for w, at in weights],
            outs,
            out_specs,
            [pltpu.VMEM((2, rows, dim), F32)]
            + [pltpu.VMEM((2, pair * rows, units // 3), F32)] * 2
            + [pltpu.VMEM((pair * rows, dim), BF16)] * 2,
            size // pair,
            3 * feed_flops,
            layer_bytes + 12 * chunk_rows * dim * 2,
        )

    def heads_back(layer, top, first, turned, normed, low, d_feed, fed, begin=0, count=size):
        weights = [(turned, layer), (qk_gain, None), (w_out, layer)]
        streams = (normed, low, d_feed) + ((fed,) if top else ())
        row_array = jax.ShapeDtypeStruct((count * rows, dim), BF16)
        outs = ([row_array] if top else []) + [
            row_array,
            jax.ShapeDtypeStruct((count * rows, 4 * inner), BF16),
            jax.ShapeDtypeStruct((2 * head_dim, lanes), F32),
            jax.ShapeDtypeStruct((1, dim), F32),
        ]
        out_specs = ([row_spec] if top else []) + [
            row_spec,
            rows_spec(rows, 4 * inner),
            whole_spec(outs[-2]),
            whole_spec(outs[-1]),
        ]
        return call(
            functools.partial(heads_kernel, layer, top, first + begin, rows),
            (merge_map,) + streams + tuple(w for w, _ in weights),
            [whole_spec(merge_map)] + [rows_spec(rows, dim, begin)] * len(streams) + [layer_spec(w, at) for w, at in weights],
            outs,
            out_specs,
            [lane_rows] * 2
            + [proj_rows, low_rows, head_rows, score_rows, score_rows, soft_rows, soft_rows, head_rows]
            + [pltpu.VMEM((2 * inner, lanes), F32), low_rows, pltpu.VMEM((padded_to(heads, 8), lanes), F32), pltpu.VMEM((rows, dim), F32)],
            count,
            6 * head_flops,
            layer_bytes,
            prefetch=0,
        )

    def feed_grads(fed, before=()):
        groups = [[one[at] for one in fed] for at in (8, 9, 5, 4)]
        tile = units // 3
        tiles = units // tile
        flat = [array for group in groups for array in group]
        specs = [whole_spec(one) for one in groups[0] + groups[1]]
        specs += [pl.BlockSpec((chunk_rows, tile), lambda i: (0, jnp.minimum(i, tiles - 1)))] * len(fed)
        specs += [pl.BlockSpec((chunk_rows, tile), lambda i: (0, jnp.maximum(i - tiles, 0)))] * len(fed)
        return call(
            functools.partial(feed_weight_kernel, spans(groups)),
            (*flat, *before),
            specs + [pl.BlockSpec(memory_space=pl.ANY)] * len(before),
            jax.ShapeDtypeStruct((dim, before[0].shape[1] if before else 2 * units), BF16),
            pl.BlockSpec((dim, tile), lambda i: (0, i)),
            [],
            2 * tiles,
            2 * images * rows * dim * units * 2,
            2 * images * rows * (dim + units) * 2,
            prefetch=0,
            aliases={len(flat): 0} if before else None,
        )

    def heads_grads(fed, made, sums=()):
        columns = 4 * inner + (128 if sums else 0)
        groups = [[one[at] for one in fed] for at in (8, 9)] + [[one[1] for one in made], [ln_gain]] + list(sums)
        flat = [array for group in groups for array in group]
        specs = [whole_spec(one) for one in groups[0] + groups[1]]
        specs += [pl.BlockSpec((one.shape[0], inner), lambda i, *_: (0, i)) for one in groups[2]]
        specs += [whole_spec(one) for group in groups[3:] for one in group]
        return call(
            functools.partial(heads_weight_kernel, spans(groups)),
            (core_bit, *flat),
            specs,
            [jax.ShapeDtypeStruct((dim // 2, columns), BF16)] * 2,
            [pl.BlockSpec((dim // 2, columns), lambda i, *_: (0, 0))] * 2,
            [pltpu.VMEM((2, dim // 2, inner), BF16)]
            + ([pltpu.VMEM((padded_to(small_rows, 16), 128), F32)] if sums else []),
            4,
            2 * images * rows * dim * inner * 4,
            2 * images * rows * (dim + inner) * 4,
        )

    def unpack(kernel, halves, width, place, shapes, blocks, places, before):
        return call(
            kernel,
            (*halves, *before),
            [pl.BlockSpec((dim // 2, width), lambda i, *_: (0, place))]
            + [pl.BlockSpec((dim // 2, width), lambda i, *_: (halves[2].shape[0] // (dim // 2) - 1, place))]
            + [pl.BlockSpec(memory_space=pl.ANY)] * len(before),
            [jax.ShapeDtypeStruct(shape, F32) for shape in shapes],
            [pl.BlockSpec(block, place_of) for block, place_of in zip(blocks, places)],
            [],
            2,
            dim * width,
            6 * dim * width,
            aliases={at + 3: at for at in range(len(before))},
        )

    def row_half(i, bits):
        return lax.rem(i + bits[0], 2)

    def feed_unpack(halves, layer, before=()):
        return unpack(
            feed_unpack_kernel,
            halves,
            2 * units,
            0,
            ((layers, dim, units), (layers, units, dim)),
            ((1, dim // 2, units), (1, units, dim // 2)),
            (lambda i, bits: (layer, row_half(i, bits), 0), lambda i, bits: (layer, 0, row_half(i, bits))),
            before,
        )

    def heads_unpack(halves, layer, place=0, before=()):
        return unpack(
            heads_unpack_kernel,
            halves,
            halves[1].shape[1] - place * 4 * inner,
            place,
            ((layers, 3, dim, inner), (layers, inner, dim)),
            ((1, 3, dim // 2, inner), (1, inner, dim // 2)),
            (lambda i, bits: (layer, 0, row_half(i, bits), 0), lambda i, bits: (layer, 0, row_half(i, bits))),
            before,
        )

    tokens_slots = jnp.swapaxes(tokens, 0, 1)
    step_slots = 16
    slot_spec = pl.BlockSpec((step_slots, images, dim), lambda i, *_: (i, 0, 0))
    slot_array = jax.ShapeDtypeStruct((slots, images, dim), F32)
    chunk_spec = slots_spec(size, step_slots, dim)
    turned_rows = pltpu.VMEM((step_slots, images, dim), F32)

    def by_image(value):
        return value.reshape(value.shape[0] // rows, rows, dim)

    def paired(ours, theirs):
        return [by_image(one) for two in zip(ours, theirs) for one in two]

    def layer_output(before, ours, theirs, layer):
        pieces = paired(ours, theirs)
        return call(
            functools.partial(output_kernel, layer, len(ours)),
            (counts, before, *pieces, b_down),
            [slot_spec] + [slots_spec(one.shape[0], step_slots, dim) for one in pieces] + [whole_spec(b_down)],
            slot_array,
            slot_spec,
            [turned_rows],
            -(-slots // step_slots),
            10 * images * rows * dim,
            12 * images * rows * dim,
        )

    own, far = [], []
    qkv = w_qkv
    for first in range(0, images, pair):
        made = forward(0, first, tie(qkv, *own[-1:]) if own else qkv, 0 if own else None, not own)
        if not own:
            qkv = turned = made[1]
        own.append(made[0])
        far.append(others(made[0]))
    own_a, own_b = own[: len(own) // 2], own[len(own) // 2 :]
    far_a, far_b = far[: len(far) // 2], far[len(far) // 2 :]
    cotangent = tie(cotangent, own[-1])
    fed1_a = feed_back(1, True, 0, (own_a, far_a[:-1] + [tie(far_a[-1], own[-1], *far_b[:-1])]))
    fed1_b = feed_back(1, True, size, (own_b, far_b[:-1] + [tie(far_b[-1], fed1_a[0])]))
    fed1 = (fed1_a, fed1_b)
    pack_feed1 = feed_grads(fed1)
    part_feed1 = lax.psum_scatter(pack_feed1, "wide", scatter_dimension=0, tiled=True)
    made1_a = heads_back(1, True, 0, turned, tie(fed1_a[1], pack_feed1), *fed1_a[2:4], fed1_a[0])
    far_grad_a = others(made1_a[1])
    made1_b = heads_back(1, True, size, turned, tie(fed1_b[1], made1_a[0]), *fed1_b[2:4], fed1_b[0])
    far_grad_b = others(made1_b[1])
    made1 = (made1_a[1:], made1_b[1:])
    heads1 = HalvingSum(*heads_grads(fed1, made1), "wide")
    fed0_a = feed_back(0, False, 0, (own_a, far_a, made1_a[1], tie(far_grad_a, heads1.sent)))
    heads1.step(fed0_a[0])
    first_out = layer_output(tie(tokens_slots, fed0_a[0], heads1.sent), own, far, 0)
    pack_feed1 = lax.all_gather(tie(part_feed1, first_out, heads1.got, far_grad_b), "wide", axis=0, tiled=True)
    heads1.step(first_out)
    fed0_b = feed_back(0, False, size, (own_b, far_b, made1_b[1], tie(far_grad_b, heads1.sent)))
    fed0 = (fed0_a, fed0_b)
    far_next_a = others(tie(made1_a[0], first_out))
    far_next_b = others(tie(made1_b[0], first_out))
    heads1.step(fed0_b[0])
    pack_rest = feed_grads([tuple(one[:-1]) + (tie(one[-1], heads1.sent),) for one in fed0])
    heads1.step(pack_rest)
    made0, far_last = [], []
    for at in range(2):
        source = fed0[at]
        ready = (heads1.sent,) + tuple(one[0] for one in made0)
        made0.append(heads_back(0, False, at * size, turned, tie(source[1], *ready), *source[2:4], None))
        far_last.append(others(made0[-1][0]))
        if at == 0:
            pack_rest = tie(pack_rest, made0[0][0], far_next_a, far_next_b, pack_feed1, heads1.got)
    part_rest = lax.psum_scatter(pack_rest, "wide", scatter_dimension=0, tiled=True)
    heads1.step(made0[1][0])
    sums = []
    for fed, made in ((fed0, made0), (fed1, made1)):
        sums += [[one[3] for one in made], [one[2] for one in made], [one[7] for one in fed], [one[6] for one in fed]]
    sums[0][0] = tie(sums[0][0], heads1.sent)
    heads0 = HalvingSum(*heads_grads(fed0, made0, sums), "wide")
    heads0.step(far_last[0])
    second_out = layer_output(
        tie(first_out, heads0.sent), (made1_a[0], made1_b[0]), (far_next_a, far_next_b), 1
    )
    heads1.step(second_out)
    heads0.step(second_out, far_last[1])
    none = jnp.zeros((1,), jnp.int32)
    feed_outs = feed_unpack((none,) + (tie(pack_feed1, heads0.sent, heads1.sent),) * 2, 1)
    heads0.step(feed_outs[0])
    heads1.step(feed_outs[0])
    heads_outs = heads_unpack(heads1.halves(heads0.sent), 1)
    heads0.step(heads_outs[0])
    pack_rest = lax.all_gather(tie(part_rest, heads0.sent), "wide", axis=0, tiled=True)
    grad_tokens = call(
        functools.partial(tokens_kernel, len(made0)),
        (
            counts,
            tie(tokens_slots, heads0.sent),
            *paired([one[0] for one in made0], far_last),
            by_image(fed0_a[0]),
            by_image(fed0_b[0]),
            ln_gain,
        ),
        [slot_spec] + [chunk_spec] * (3 * len(made0)) + [whole_spec(ln_gain)],
        slot_array,
        slot_spec,
        [turned_rows] * 2,
        -(-slots // step_slots),
        10 * images * rows * dim,
        12 * images * rows * dim,
    )
    heads0.step(grad_tokens)
    while len(heads0.todo) > 1:
        heads0.step()
    rest = (none,) + (tie(pack_rest, heads0.sent),) * 2
    up, down = feed_unpack(rest, 0, feed_outs)
    halves0 = heads0.halves(up)
    small = jnp.where(halves0[0][0] == 0, *[half[:small_rows, 4 * inner :] for half in halves0[1:]])
    small = small.astype(F32).reshape(layers, -1)
    narrow_part = small[:, : dim + 2 * head_dim]
    if n_narrow == 2:
        narrow_part = narrow_part + lax.ppermute(narrow_part, "narrow", [(0, 1), (1, 0)])
    else:
        narrow_part = lax.psum(narrow_part, "narrow")
    g_b_down = small[:, dim + 2 * head_dim : 2 * dim + 2 * head_dim]
    g_b_up = small[:, 2 * dim + 2 * head_dim :]
    qkv, out = heads_unpack((halves0[0], tie(halves0[1], g_b_up), halves0[2]), 0, 0, heads_outs)
    return (
        jnp.swapaxes(first_out, 0, 1),
        jnp.swapaxes(second_out, 0, 1),
        jnp.swapaxes(grad_tokens, 0, 1),
        narrow_part[:, :dim],
        qkv,
        narrow_part[:, dim:].reshape(qk_gain.shape),
        out,
        up,
        g_b_up,
        down,
        g_b_down,
    )


def pick_body(*arrays):
    images, dim, inner, units = arrays[0].shape[0], arrays[0].shape[2], arrays[4].shape[-1], arrays[7].shape[-1]
    whole_heads = inner % arrays[5].shape[-1] == 0
    if whole_heads and images % 4 == 0 and units % inner == 0 and dim % 256 == 0 and inner % 128 == 0:
        return split_body(*arrays)
    return body(*arrays)


def solution(mesh):
    placed = (
        P("wide", None, None),
        P("wide", None),
        P("wide"),
        P(),
        P(None, None, None, "narrow"),
        P(),
        P(None, "narrow", None),
        P(None, None, "narrow"),
        P(None, "narrow"),
        P(None, "narrow", None),
        P(),
        P("wide", None, None),
    )
    return jax.shard_map(
        pick_body,
        mesh=mesh,
        in_specs=placed,
        out_specs=(
            P("wide", None, None),
            P("wide", None, None),
            P("wide", None, None),
            P(),
            P(None, None, None, "narrow"),
            P(),
            P(None, "narrow", None),
            P(None, None, "narrow"),
            P(None, "narrow"),
            P(None, "narrow", None),
            P(),
        ),
        check_vma=False,
    )
```
